32 devices in a mesh: seq: 32 (over z, y, x, core).
Axes of the slice: x: 2, y: 2, z: 4, core: 2. Of those that a mesh axis runs over, the one named last changes fastest.
Arguments:
- tokens: bfloat16 [8192, 1024], P('seq'), may hold values from -6 to 6
- w_in: bfloat16 [1024, 4096], replicated, may hold values from -0.1875 to 0.1875
- w_out: bfloat16 [1024, 1024], replicated, may hold values from -0.1875 to 0.1875
- block_counts: int32 [16], replicated, may hold values from 1 to 16, 64 in all
- tails: int32 [16], replicated, may hold values from 1 to 128
- grad_out: bfloat16 [8192, 1024], P('seq'), may hold values from -6 to 6
Outputs:
- layer_out: bfloat16 [8192, 1024], P('seq')
- grad_tokens: bfloat16 [8192, 1024], P('seq')
- grad_w_in: float32 [4096, 1024], P('seq')
The draws below stay inside these ranges and needn't reach their ends.
Inputs may be any that keep to these rules, and one draw needn't show every extreme that they name: `block_counts`: the block counts sum to 64; one user has exactly 16 blocks.
All inputs are finite; a program needn't handle non-finite values.
Results may differ from the reference program's by a relative error of at most 0.013.
Values may be sent and summed in bfloat16 or wider, within the bound.
No kernel may reach another device: no remote copies, remote signals or barrier semaphores. Data moves between devices by JAX's collectives and lax.ppermute only.
A program may use at most 192 MiB of HBM per device.

```python
import math
import jax
import jax.numpy as jnp
import numpy as np
from jax import lax

D = 1024
HEADS = 8
HD = 128
BLK = 128
MAXB = 16
TOK_DEV = 256
TOKENS = 8192
NBLOCKS = 64
USERS = 16
MAXLEN = 2048
HOPS = 8


def with_ends(drawn, stream_key, least, high):
    index_at = [jax.random.randint(jax.random.fold_in(stream_key, axis), (), 0, length) for axis, length in enumerate(drawn.shape)]
    longest = drawn.shape.index(max(drawn.shape))
    next_to = index_at[:longest] + [(index_at[longest] + 1) % drawn.shape[longest]] + index_at[longest + 1:]
    return drawn.at[tuple(index_at)].set(least).at[tuple(next_to)].set(high)


def block_scale(rng, shape, split, least, top_value):
    factor_of, own = 1.0, jax.random.fold_in(rng, 6)
    for axis_at, parts in split:
        draws = jnp.exp(jax.random.uniform(jax.random.fold_in(own, axis_at), (parts,), jnp.float32, least / len(split), top_value / len(split)))
        factor_of = factor_of * jnp.repeat(draws, shape[axis_at] // parts).reshape([-1 if axis == axis_at else 1 for axis in range(len(shape))])
    return factor_of


def profile(amount, total, bound, slope):
    portions = [(1 << 20) // math.isqrt(grade ** slope) + 1 for grade in range(2, amount + 1)]
    surplus, holding = total - bound - (amount - 1), [1] * (amount - 1)
    while surplus > 0:
        candidates = [i for i in range(amount - 1) if holding[i] < bound]
        pool, left = sum([portions[i] for i in candidates]), surplus
        for i in candidates:
            more = min(bound - holding[i], max(1, left * portions[i] // pool), surplus)
            holding[i] = holding[i] + more
            surplus = surplus - more
    return np.array([bound] + holding)


def uneven(stream_key, number_of, total, bound, slope):
    if number_of == 2:
        one = jax.random.randint(stream_key, (), max(1, total - bound), min(bound, total - 1) + 1)
        return jnp.stack([one, total - one])
    sizes = jnp.asarray(profile(number_of, total, bound, slope), jnp.int32)
    couples = (number_of - 1) // 2
    source_of, taker = sizes[1:1 + 2 * couples:2], sizes[2:2 + 2 * couples:2]
    margin = jnp.minimum(source_of - 1, bound - taker)
    moved = jax.random.randint(jax.random.fold_in(stream_key, 1), (couples,), 0, 1 << 20) % (margin + 1)
    sizes = sizes.at[1:1 + 2 * couples:2].set(source_of - moved).at[2:2 + 2 * couples:2].set(taker + moved)
    return sizes[jax.random.permutation(jax.random.fold_in(stream_key, 2), number_of)]


def normal_values(rng, dims, width, reach, shards=(), held_as=jnp.bfloat16):
    loudness = block_scale(rng, dims, shards, -0.22, 0.18) if shards else 1.0
    entries = jax.random.normal(rng, dims, jnp.float32) * width * loudness
    return jnp.minimum(jnp.maximum(entries, -reach), reach).astype(held_as)


def setup_inputs(seed: int = 0) -> dict:
    seeds = jax.random.split(jax.random.key(seed), 7)
    tokens = normal_values(seeds[0], (TOKENS, D), 1.0, 6.0, ((0, 32),))
    w_in = normal_values(seeds[1], (D, 4 * D), D ** -0.5, 0.1875)
    w_out = normal_values(seeds[2], (D, D), D ** -0.5, 0.1875)
    block_counts = uneven(seeds[3], USERS, NBLOCKS, MAXB, 2).astype(jnp.int32)
    tails = with_ends(jax.random.randint(seeds[4], (USERS,), 1, BLK + 1), jax.random.fold_in(seeds[4], 1), 1, BLK).astype(jnp.int32)
    grad_out = normal_values(seeds[5], (TOKENS, D), 1.0, 6.0, ((0, 32),))
    return dict(tokens=tokens, w_in=w_in, w_out=w_out, block_counts=block_counts, tails=tails, grad_out=grad_out)


eps = 1e-05

def row_info(rows, counts, tails):
    ends = jnp.cumsum(counts).astype(jnp.int32) * BLK
    starts = ends - counts * BLK
    lengths = (counts - 1) * BLK + tails
    user = lax.optimization_barrier(jnp.sum((rows[:, None] >= ends[None, :]).astype(jnp.int32), axis=1))
    pick = user[:, None] == jnp.arange(counts.shape[0], dtype=jnp.int32)[None, :]
    start = lax.optimization_barrier(jnp.sum(jnp.where(pick, starts[None, :], 0), axis=1))
    length = lax.optimization_barrier(jnp.sum(jnp.where(pick, lengths[None, :], 0), axis=1))
    valid = (rows >= 0) & (rows - start < length)
    return (user, rows, valid)

def attend(query, keys, values, qinfo, kinfo):
    q_user, q_rows, q_ok = qinfo
    k_user, k_rows, k_ok = kinfo
    qh = query.reshape(query.shape[0], HEADS, HD)
    kh = keys.reshape(keys.shape[0], HEADS, HD)
    vh = values.reshape(values.shape[0], HEADS, HD)
    scores = jnp.einsum('qhd,khd->hqk', qh, kh, preferred_element_type=jnp.float32)
    weights = jax.nn.silu(scores * HD ** (-0.5)) / MAXLEN
    visible = (q_user[:, None] == k_user[None, :]) & (k_rows[None, :] <= q_rows[:, None])
    visible = visible & q_ok[:, None] & k_ok[None, :]
    weights = jnp.where(visible[None], weights, 0.0).astype(jnp.bfloat16)
    out = jnp.einsum('hqk,khd->qhd', weights, vh, preferred_element_type=jnp.float32)
    return out.reshape(query.shape[0], HEADS * HD)

def stem_norm(xf):
    return xf * lax.rsqrt(lax.optimization_barrier(jnp.mean(xf * xf, axis=-1, keepdims=True)) + eps)

def split_parts(pre):
    hidden = jax.nn.silu(pre)
    return tuple((hidden[:, i * D:(i + 1) * D].astype(jnp.bfloat16) for i in range(4)))

def make_tail(w_out):

    def tail_fn(attn, u, xf):
        normed = attn * lax.rsqrt(lax.optimization_barrier(jnp.mean(attn * attn, axis=-1, keepdims=True)) + eps)
        gated = (normed * u).astype(jnp.bfloat16)
        return xf + jnp.dot(gated, w_out, preferred_element_type=jnp.float32)
    return tail_fn

def reference(tokens, w_in, w_out, block_counts, tails, grad_out):
    rows = jnp.arange(TOKENS, dtype=jnp.int32)
    user, rows, valid = row_info(rows, block_counts, tails)
    pad = HOPS * TOK_DEV
    span = (HOPS + 1) * TOK_DEV
    user_pad = jnp.concatenate([jnp.full((pad,), -1, jnp.int32), user])
    rows_pad = jnp.concatenate([jnp.full((pad,), -1, jnp.int32), rows])
    ok_pad = jnp.concatenate([jnp.zeros((pad,), bool), valid])

    def attention(q, k, v):
        k_pad = jnp.concatenate([jnp.zeros((pad, D), jnp.bfloat16), k])
        v_pad = jnp.concatenate([jnp.zeros((pad, D), jnp.bfloat16), v])

        def one(b):
            at = b * TOK_DEV
            qs = lax.dynamic_slice_in_dim(q, at, TOK_DEV, 0)
            qinfo = tuple((lax.dynamic_slice_in_dim(a, at, TOK_DEV, 0) for a in (user, rows, valid)))
            ks = lax.dynamic_slice_in_dim(k_pad, at, span, 0)
            vs = lax.dynamic_slice_in_dim(v_pad, at, span, 0)
            kinfo = tuple((lax.dynamic_slice_in_dim(a, at, span, 0) for a in (user_pad, rows_pad, ok_pad)))
            return attend(qs, ks, vs, qinfo, kinfo)
        out = lax.map(jax.checkpoint(one), jnp.arange(TOKENS // TOK_DEV, dtype=jnp.int32))
        return out.reshape(TOKENS, D)
    xf = tokens.astype(jnp.float32)
    normed_f, norm_back = jax.vjp(stem_norm, xf)
    normed = normed_f.astype(jnp.bfloat16)
    pre = jnp.dot(normed, w_in, preferred_element_type=jnp.float32)
    tail_fn = make_tail(w_out)

    def middle(pre, xf):
        u, v, q, k = split_parts(pre)
        return tail_fn(attention(q, k, v), u, xf)
    out_f, back = jax.vjp(middle, pre, xf)
    layer_out = out_f.astype(jnp.bfloat16)
    d_pre, d_xf = back(grad_out.astype(jnp.float32))
    d_pre_b = d_pre.astype(jnp.bfloat16)
    grad_w_in = lax.dot_general(d_pre_b, normed, (((0,), (0,)), ((), ())), preferred_element_type=jnp.float32)
    d_normed = lax.dot_general(d_pre_b, w_in, (((1,), (1,)), ((), ())), preferred_element_type=jnp.float32)
    grad_tokens = (d_xf + norm_back(d_normed)[0]).astype(jnp.bfloat16)
    return (layer_out, grad_tokens, grad_w_in)
```

```python
import functools

import jax
import jax.numpy as jnp
from jax import lax
from jax.experimental import pallas as pl
from jax.experimental.pallas import tpu as pltpu
from jax.sharding import Mesh, PartitionSpec as P

HEADS = 8
HD = 128
BLK = 128
MAXB = 16
SPAN = MAXB * BLK
TILE = 256
TILES = SPAN // TILE
HALF = 0.5 * HD ** (-0.5)

eps = 1e-05

NT = (((1,), (1,)), ((), ()))
F32, BF16 = jnp.float32, jnp.bfloat16

U, V, Q, K = (slice(i * HD, (i + 1) * HD) for i in range(4))


def block_info(counts, tails, base, blocks):
    ends = jnp.cumsum(counts)
    starts = ends - counts
    at = base + jnp.arange(blocks, dtype=jnp.int32)
    user = jnp.sum((at[:, None] >= ends[None, :]).astype(jnp.int32), axis=1)
    pick = user[:, None] == jnp.arange(counts.shape[0], dtype=jnp.int32)[None, :]
    start = jnp.sum(jnp.where(pick, starts[None, :], 0), axis=1)
    last = jnp.sum(jnp.where(pick, ends[None, :] - 1, 0), axis=1)
    tail = jnp.sum(jnp.where(pick, tails[None, :], 0), axis=1)
    return (start - base) * BLK, jnp.where(at == last, tail, BLK)


def by_half(t, ref, shape, dim):
    side = lax.broadcasted_iota(jnp.int32, shape, dim)
    return jnp.where(side < BLK, ref[2 * t], ref[2 * t + 1])


def valid_rows(t, nv_ref):
    row = lax.broadcasted_iota(jnp.int32, (TILE, 1), 0)
    return (row & (BLK - 1)) < by_half(t, nv_ref, (TILE, 1), 0)


def rows_at(t):
    return pl.ds(pl.multiple_of(t * TILE, TILE), TILE)


def weigh(q, k, v, mask):
    half = lax.dot_general(q, k, NT, preferred_element_type=jnp.float32) * HALF
    w = half + half * jnp.tanh(half)
    w = jnp.where(mask, w, 0.0).astype(jnp.bfloat16)
    return jnp.dot(w, v, preferred_element_type=jnp.float32)


def proj_kernel(masks, first, head_ref, *refs):
    count = len(masks)
    chunks, w_ref = refs[:count], refs[count]
    if first:
        normed_ref, act_ref, slope_ref, kv_ref, wh_ref = refs[-5:]
        for i in range(4):
            at = pl.multiple_of(i * w_ref.shape[0] + head_ref[0] * HD, HD)
            wh_ref[:, i * HD : (i + 1) * HD] = w_ref[:, pl.ds(at, HD)]
    else:
        normed_ref, act_ref, slope_ref, kv_ref = refs[-4:]
        wh_ref = w_ref
    for i, (mask, x_ref) in enumerate(zip(masks, chunks)):
        rows = rows_at(head_ref[0] ^ mask)
        x = x_ref[...].astype(F32)
        xn = (x * lax.rsqrt(jnp.mean(x * x, axis=-1, keepdims=True) + eps)).astype(BF16)
        normed_ref[rows, :] = xn
        pre = jnp.dot(xn, wh_ref[...], preferred_element_type=F32)
        s = 0.5 + 0.5 * jnp.tanh(0.5 * pre)
        act = (pre * s).astype(BF16)
        act_ref[rows, :] = act
        slope_ref[rows, :] = (s * (1.0 + pre * (1.0 - s))).astype(BF16)
        kv_ref[i * TILE : (i + 1) * TILE, :HD] = act[:, V]
        kv_ref[i * TILE : (i + 1) * TILE, HD:] = act[:, K]


def project(head, masks, chunks, w, kept):
    width = chunks[0].shape[1]
    first = not kept
    outs = [((SPAN, width), BF16), ((SPAN, 4 * HD), BF16), ((SPAN, 4 * HD), BF16), ((len(masks) * TILE, 2 * HD), BF16)]
    if first:
        outs.append(((width, 4 * HD), BF16))
    start = 2 + len(chunks)
    return call(
        functools.partial(proj_kernel, masks, first),
        (head,),
        (*chunks, w, *kept),
        outs,
        flops=0,
        specs=[None] * (len(chunks) + 1) + [pl.BlockSpec(memory_space=pl.ANY)] * len(kept),
        aliases={start + i: i for i in range(len(kept))},
    )


def join_kernel(a_ref, b_ref, after_ref, out_ref):
    out_ref[:BLK, :] = a_ref[...]
    out_ref[BLK:, :] = b_ref[...]


def own_rows_kernel(tokens_ref, g_ref, w_in_ref, w_out_ref, dg_ref, u_ref, slope_ref):
    width = tokens_ref.shape[1]
    d = lax.dot_general(g_ref[...], w_out_ref[...], NT, preferred_element_type=F32).astype(BF16)
    for h in range(HEADS):
        dg_ref[h] = d[:, h * HD : (h + 1) * HD]
    x = tokens_ref[...].astype(F32)
    xn = (x * lax.rsqrt(jnp.mean(x * x, axis=-1, keepdims=True) + eps)).astype(BF16)
    pre = jnp.dot(xn, w_in_ref[:, :width], preferred_element_type=F32)
    s = 0.5 + 0.5 * jnp.tanh(0.5 * pre)
    u_ref[...] = (pre * s).astype(BF16)
    slope_ref[...] = (s * (1.0 + pre * (1.0 - s))).astype(BF16)


def fwd_own_kernel(lo_ref, nv_ref, act_ref, out_ref, kt_ref):
    row = lax.broadcasted_iota(jnp.int32, (TILE, TILE), 0)
    col = lax.broadcasted_iota(jnp.int32, (TILE, TILE), 1)

    def q_tile(t, carry):
        lo = by_half(t, lo_ref, (TILE, 1), 0) - t * TILE
        q = act_ref[rows_at(t), Q]
        acc = weigh(q, act_ref[rows_at(t), K], act_ref[rows_at(t), V], (col <= row) & (col >= lo))

        def k_tile(s, acc):
            return acc + weigh(q, act_ref[rows_at(s), K], act_ref[rows_at(s), V], col >= lo + (t - s) * TILE)

        first = jnp.maximum(lo_ref[2 * t], 0) // TILE
        acc = lax.fori_loop(first, t, k_tile, acc)
        out_ref[rows_at(t), :] = jnp.where(valid_rows(t, nv_ref), acc, 0.0)
        return carry

    lax.fori_loop(0, TILES, q_tile, 0)
    for t in range(TILES):
        rows = slice(t * TILE, (t + 1) * TILE)
        kt_ref[:, rows] = act_ref[rows, K].T


def place(head_ref, pieces, out_ref):
    slot = 0
    for piece in pieces:
        for at in range(0, piece.shape[0], TILE):
            out_ref[rows_at(slot ^ head_ref[0]), :] = piece[at : at + TILE, :]
            slot += 1


def fwd_far_kernel(head_ref, lo_ref, nv_ref, act_ref, kva_ref, kvb_ref, kvc_ref, near_ref, dg_ref, out_ref, sum_ref, kv_ref):
    place(head_ref, (kva_ref, kvb_ref, kvc_ref), kv_ref)
    col = lax.broadcasted_iota(jnp.int32, (TILE, TILE), 1)

    def q_tile(t, carry):
        lo = by_half(t, lo_ref, (TILE, 1), 0) + SPAN
        q = act_ref[rows_at(t), Q]

        def k_tile(s, acc):
            return acc + weigh(q, kv_ref[rows_at(s), HD:], kv_ref[rows_at(s), :HD], col >= lo - s * TILE)

        first = jnp.minimum(lo_ref[2 * t] + SPAN, SPAN) // TILE
        acc = lax.fori_loop(first, TILES, k_tile, jnp.zeros((TILE, HD), F32))
        acc = jnp.where(valid_rows(t, nv_ref), acc, 0.0) + near_ref[rows_at(t), :]
        attn = acc * (1.0 / SPAN)
        out_ref[rows_at(t), :] = attn.astype(BF16)
        d_n = dg_ref[rows_at(t), :].astype(F32) * act_ref[rows_at(t), U].astype(F32)
        square = jnp.sum((attn * attn).T, axis=0, keepdims=True)
        cross = jnp.sum((attn * d_n).T, axis=0, keepdims=True)
        for h in range(HEADS):
            sum_ref[h, pl.ds(t, 1), :] = square
            sum_ref[h, pl.ds(TILES + t, 1), :] = cross
        return carry

    lax.fori_loop(0, TILES, q_tile, 0)


def row_scales(sum_ref):
    width = HEADS * HD
    total = jnp.sum(sum_ref[...], axis=0)
    r = lax.rsqrt(total[:TILES] * (1.0 / width) + eps)
    c = total[TILES:] * (1.0 / width) * r
    return jnp.concatenate([r, c], axis=0).T


def back(q, k, kt, v, g, mask):
    half = lax.dot_general(k, q, NT, preferred_element_type=F32) * HALF
    th = jnp.tanh(half)
    up = 1.0 + th
    w = jnp.where(mask, half * up, 0.0).astype(BF16)
    dw = lax.dot_general(v, g, NT, preferred_element_type=F32)
    ds = jnp.where(mask, dw * (up * (1.0 + half * (1.0 - th))), 0.0).astype(BF16)
    dv = jnp.dot(w, g, preferred_element_type=F32)
    dk = jnp.dot(ds, q, preferred_element_type=F32)
    dqt = jnp.dot(kt, ds, preferred_element_type=F32)
    return dv, dk, dqt


def cotangent(t, scales, nv_ref, act_ref, attn_ref, dg_ref):
    rows = slice(t * TILE, (t + 1) * TILE)
    r, c = scales[:, t : t + 1], scales[:, TILES + t : TILES + t + 1]
    d_gated = dg_ref[rows, :].astype(F32)
    n = attn_ref[rows, :].astype(F32) * r
    g = r * (d_gated * act_ref[rows, U].astype(F32) - n * c)
    return n, d_gated, jnp.where(valid_rows(t, nv_ref), g, 0.0).astype(BF16)


def bwd_far_kernel(
    head_ref, lo_ref, nv_ref, sum_ref, act_ref, attn_ref, dg_ref, kva_ref, kvb_ref, kvc_ref,
    dq_ref, dkv_ref, kv_ref, kt_ref, acc_ref,
):
    place(head_ref, (kva_ref, kvb_ref, kvc_ref), kv_ref)
    scales = row_scales(sum_ref)
    first = jnp.minimum(lo_ref[0] + SPAN, SPAN) // TILE
    for s in range(TILES):
        rows = slice(s * TILE, (s + 1) * TILE)

        @pl.when(s >= first)
        def _():
            acc_ref[rows, :] = jnp.zeros((TILE, 2 * HD), F32)
            kt_ref[:, rows] = kv_ref[rows, HD:].T

    for t in range(TILES):

        @pl.when(lo_ref[2 * t] < 0)
        def _():
            lo = by_half(t, lo_ref, (1, TILE), 1) + SPAN
            rows = slice(t * TILE, (t + 1) * TILE)
            q = act_ref[rows, Q]
            g = cotangent(t, scales, nv_ref, act_ref, attn_ref, dg_ref)[2]
            key = lax.broadcasted_iota(jnp.int32, (TILE, TILE), 0)

            def k_tile(s, dqt):
                k, v = kv_ref[rows_at(s), HD:], kv_ref[rows_at(s), :HD]
                dv, dk, dqt_part = back(q, k, kt_ref[:, rows_at(s)], v, g, key >= lo - s * TILE)
                acc_ref[rows_at(s), :HD] += dv
                acc_ref[rows_at(s), HD:] += dk
                return dqt + dqt_part

            start = (lo_ref[2 * t] + SPAN) // TILE
            dqt = lax.fori_loop(start, TILES, k_tile, jnp.zeros((HD, TILE), F32))
            dq_ref[rows, :] = dqt.T

    for s in range(TILES):
        rows = slice(s * TILE, (s + 1) * TILE)

        @pl.when(s >= first)
        def _():
            dkv_ref[rows, :HD] = (acc_ref[rows, :HD] * (1.0 / SPAN)).astype(BF16)
            dkv_ref[rows, HD:] = (acc_ref[rows, HD:] * (HALF / SPAN)).astype(BF16)

        @pl.when(s < first)
        def _():
            dkv_ref[rows, :] = jnp.zeros((TILE, 2 * HD), BF16)


def bwd_own_kernel(
    lo_ref, nv_ref, sum_ref, act_ref, slope_ref, attn_ref, dg_ref, kt_ref, far_ref,
    rows_ref, cols_ref, dkv_ref, g_ref,
):
    scales = row_scales(sum_ref)
    for t in range(TILES):
        rows = slice(t * TILE, (t + 1) * TILE)
        n, d_gated, g = cotangent(t, scales, nv_ref, act_ref, attn_ref, dg_ref)
        g_ref[rows, :] = g
        du = (d_gated * n).astype(BF16).astype(F32)
        cols_ref[:HD, rows] = (du * slope_ref[rows, U].astype(F32)).astype(BF16).T

    def q_tile(t, carry):
        lo = by_half(t, lo_ref, (1, TILE), 1) - t * TILE
        q = act_ref[rows_at(t), Q]
        g = g_ref[rows_at(t), :]
        key = lax.broadcasted_iota(jnp.int32, (TILE, TILE), 0)
        query = lax.broadcasted_iota(jnp.int32, (TILE, TILE), 1)
        mask = (key <= query) & (key >= lo)
        dv, dk, dqt = back(q, act_ref[rows_at(t), K], kt_ref[:, rows_at(t)], act_ref[rows_at(t), V], g, mask)
        dkv_ref[rows_at(t), :HD] = dv
        dkv_ref[rows_at(t), HD:] = dk

        def k_tile(s, dqt):
            mask = key >= lo + (t - s) * TILE
            dv, dk, dqt_part = back(q, act_ref[rows_at(s), K], kt_ref[:, rows_at(s)], act_ref[rows_at(s), V], g, mask)
            dkv_ref[rows_at(s), :HD] += dv
            dkv_ref[rows_at(s), HD:] += dk
            return dqt + dqt_part

        first = jnp.maximum(lo_ref[2 * t], 0) // TILE
        dqt = lax.fori_loop(first, t, k_tile, dqt)
        dq = dqt.T + jnp.where(lo_ref[2 * t] < 0, far_ref[rows_at(t), :], 0.0)
        dq = (dq * (HALF / SPAN)).astype(BF16).astype(F32)
        dq = (dq * slope_ref[rows_at(t), Q].astype(F32)).astype(BF16)
        rows_ref[rows_at(t), :] = dq
        cols_ref[HD:, rows_at(t)] = dq.T
        return carry

    lax.fori_loop(0, TILES, q_tile, 0)


def key_kernel(own_ref, far_ref, slope_ref, rows_ref, cols_ref):
    for t in range(TILES):
        rows = slice(t * TILE, (t + 1) * TILE)
        for side, branch, scale in ((0, V, 1.0 / SPAN), (HD, K, HALF / SPAN)):
            cols = slice(side, side + HD)
            d = own_ref[rows, cols] * scale + far_ref[rows, cols].astype(F32)
            d = d.astype(BF16).astype(F32) * slope_ref[rows, branch].astype(F32)
            d = d.astype(BF16)
            rows_ref[rows, cols] = d
            cols_ref[cols, rows] = d.T


def joined(ref, part):
    return jnp.concatenate([ref[h, :, part * HD : (part + 1) * HD] for h in range(HEADS)], axis=1)


def through(x, w_ref, branch):
    width = w_ref.shape[0]
    return lax.dot_general(x, w_ref[:, branch * width : (branch + 1) * width], NT, preferred_element_type=F32)


def rows_kernel(attn_ref, dg_ref, u_ref, slope_ref, tokens_ref, w_out_ref, w_in_ref, out_ref, dn_ref):
    attn = joined(attn_ref, 0).astype(F32)
    n = attn * lax.rsqrt(jnp.mean(attn * attn, axis=-1, keepdims=True) + eps)
    gated = (n * u_ref[...].astype(F32)).astype(BF16)
    y = jnp.dot(gated, w_out_ref[...], preferred_element_type=F32)
    out_ref[...] = (tokens_ref[...].astype(F32) + y).astype(BF16)
    du = (joined(dg_ref, 0).astype(F32) * n).astype(BF16).astype(F32)
    du = (du * slope_ref[...].astype(F32)).astype(BF16)
    dn_ref[...] = through(du, w_in_ref, 0)


def last_kernel(q_ref, kv_ref, dn_ref, tokens_ref, grad_ref, w_in_ref, out_ref):
    dn = dn_ref[...] + through(joined(q_ref, 0), w_in_ref, 2)
    dn += through(joined(kv_ref, 0), w_in_ref, 1)
    dn += through(joined(kv_ref, 1), w_in_ref, 3)
    x = tokens_ref[...].astype(F32)
    r = lax.rsqrt(jnp.mean(x * x, axis=-1, keepdims=True) + eps)
    n = x * r
    dx = r * (dn - n * jnp.mean(dn * n, axis=-1, keepdims=True))
    out_ref[...] = (grad_ref[...].astype(F32) + dx).astype(BF16)


def sum_kernel(own_ref, *refs):
    total = own_ref[...].astype(F32)
    for ref in refs[:-2]:
        total += ref[...].astype(F32)
    refs[-1][...] = total


def call(kernel, scalars, arrays, outs, scratch=(), flops=0, specs=None, aliases=None, limit=16):
    smem = pl.BlockSpec(memory_space=pltpu.SMEM)
    vmem = pl.BlockSpec(memory_space=pltpu.VMEM)
    outs = [jax.ShapeDtypeStruct(*out) for out in outs]
    return pl.pallas_call(
        kernel,
        out_shape=outs,
        in_specs=[smem] * len(scalars) + [vmem if spec is None else spec for spec in specs or [None] * len(arrays)],
        out_specs=[vmem] * len(outs),
        scratch_shapes=list(scratch),
        input_output_aliases=aliases or {},
        compiler_params=pltpu.CompilerParams(vmem_limit_bytes=limit * 2**20),
        cost_estimate=pl.CostEstimate(flops=flops, bytes_accessed=2**20, transcendentals=0),
    )(*scalars, *arrays)


def per_device(groups, tokens, w_in, w_out, block_counts, tails, grad_out):
    count, width = tokens.shape
    group = lax.axis_index("g")
    h = lax.axis_index("h")
    head = h.astype(jnp.int32).reshape(1)
    info = block_info(block_counts, tails, group * MAXB, MAXB)

    def swap(x, mask):
        return lax.ppermute(x, "h", [(i, i ^ mask) for i in range(HEADS)])

    def exchange(x):
        x = x.reshape(HEADS, -1, x.shape[-1])
        return lax.all_to_all(x, "h", 0, 0, tiled=True)

    anywhere = pl.BlockSpec(memory_space=pl.ANY)

    x_rows, y_rows = swap(tokens, 2), swap(tokens, 4)
    other = swap(tokens, 1)
    d_gated_rows, u, slope_u = call(
        own_rows_kernel,
        (),
        (tokens, grad_out, w_in, w_out),
        [((HEADS, count, HD), BF16), ((count, width), BF16), ((count, width), BF16)],
    )
    d_gated = exchange(d_gated_rows).reshape(SPAN, HD)
    corner = swap(x_rows[:BLK], 4), swap(y_rows[BLK:], 2)

    def onward(x):
        return lax.ppermute(x, "g", [(i, i + 1) for i in range(groups - 1)])

    *kept, kv, w_head = project(head, (0, 1), (tokens, other), w_in, ())
    far_kv = [onward(kv)]
    chunks = (x_rows, swap(x_rows, 1), y_rows, swap(y_rows, 1))
    *kept, kv = project(head, (2, 3, 4, 5), chunks, w_head, kept)
    far_kv.append(onward(kv))
    corner = call(join_kernel, (), (*corner, kv), [((count, width), BF16)], specs=[None, None, anywhere])[0]
    *kept, kv = project(head, (6, 7), (corner, swap(corner, 1)), w_head, kept)
    far_kv.append(onward(kv))
    normed, act, slope = kept

    tall, wide = (SPAN, HD), (SPAN, 2 * HD)
    near_attn, kt = call(fwd_own_kernel, info, (act,), [(tall, F32), ((HD, SPAN), BF16)])
    attn, sums = call(
        fwd_far_kernel,
        (head, *info),
        (act, *far_kv, near_attn, d_gated),
        [(tall, BF16), ((HEADS, 2 * TILES, TILE), F32)],
        [pltpu.VMEM(wide, BF16)],
    )
    sums = exchange(sums)

    dq_far, dkv_far = call(
        bwd_far_kernel,
        (head, *info),
        (sums, act, attn, d_gated, *far_kv),
        [(tall, F32), (wide, BF16)],
        [pltpu.VMEM(wide, BF16), pltpu.VMEM((HD, SPAN), BF16), pltpu.VMEM(wide, F32)],
    )
    attn_rows, _ = lax.optimization_barrier((attn, sums))
    attn_rows = exchange(attn_rows)
    dkv_far = lax.ppermute(dkv_far, "g", [(i + 1, i) for i in range(groups - 1)])
    d_q, cols_a, dkv = call(
        bwd_own_kernel,
        info,
        (sums, act, slope, attn, d_gated, kt, dq_far),
        [(tall, BF16), ((2 * HD, SPAN), BF16), (wide, F32)],
        [pltpu.VMEM(tall, BF16)],
    )
    d_q = exchange(d_q)
    layer_out, d_normed = call(
        rows_kernel,
        (),
        (attn_rows, d_gated_rows, u, slope_u, tokens, w_out, w_in),
        [((count, width), BF16), ((count, width), F32)],
    )
    d_kv, cols_b = call(key_kernel, (), (dkv, dkv_far, slope), [(wide, BF16), ((2 * HD, SPAN), BF16)])
    d_kv = exchange(d_kv)
    grad_tokens = call(
        last_kernel,
        (),
        (d_q, d_kv, d_normed, tokens, grad_out, w_in),
        [((count, width), BF16)],
    )[0]

    share_a = jnp.dot(cols_a, normed, preferred_element_type=F32).astype(BF16)
    share_b = jnp.dot(cols_b, normed, preferred_element_type=F32).astype(BF16)
    share = jnp.concatenate([share_a[:HD], share_b[:HD], share_a[HD:], share_b[HD:]], axis=0)
    share = share.reshape(groups, -1, width)
    pieces = [lax.dynamic_index_in_dim(share, group, 0, keepdims=False)]
    for mask in range(1, groups):
        piece = lax.dynamic_index_in_dim(share, group ^ mask, 0, keepdims=False)
        pieces.append(lax.ppermute(piece, "g", [(i, i ^ mask) for i in range(groups)]))
    specs = [None] * len(pieces) + [anywhere]
    grad_w_in = call(sum_kernel, (), (*pieces, grad_tokens), [(pieces[0].shape, F32)], specs=specs)[0]
    parts = groups // 4
    if parts > 1:
        perm = [
            (i * HEADS + j, ((i // parts) * HEADS + j) * parts + i % parts)
            for i in range(groups)
            for j in range(HEADS)
        ]
        grad_w_in = lax.ppermute(grad_w_in, ("g", "h"), perm)
    return (layer_out, grad_tokens, grad_w_in)


def solution(mesh):
    groups = mesh.shape["seq"] // HEADS
    split = Mesh(mesh.devices.reshape(groups, HEADS), ("g", "h"))
    rows = P(("g", "h"), None)
    return jax.shard_map(
        functools.partial(per_device, groups),
        mesh=split,
        in_specs=(rows, P(), P(), P(), P(), rows),
        out_specs=(rows, rows, rows),
        check_vma=False,
    )
```

```python
import functools

import jax
import jax.numpy as jnp
from jax import lax
from jax.experimental import pallas as pl
from jax.experimental.pallas import tpu as pltpu
from jax.sharding import Mesh, PartitionSpec as P

HEADS = 8
HD = 128
BLK = 128
MAXB = 16
SPAN = MAXB * BLK
TILE = 256
TILES = SPAN // TILE
HALF = 0.5 * HD ** (-0.5)

eps = 1e-05

NT = (((1,), (1,)), ((), ()))
F32, BF16 = jnp.float32, jnp.bfloat16

U, Q, V, K = (slice(i * HD, (i + 1) * HD) for i in range(4))
PLACE = (0, 2, 1, 3)
UQ, VK = slice(0, 2 * HD), slice(2 * HD, 4 * HD)


def block_info(counts, tails, base, blocks):
    ends = jnp.cumsum(counts)
    starts = ends - counts
    at = base + jnp.arange(blocks + 1, dtype=jnp.int32)
    user = jnp.sum((at[:, None] >= ends[None, :]).astype(jnp.int32), axis=1)
    pick = user[:, None] == jnp.arange(counts.shape[0], dtype=jnp.int32)[None, :]
    start = jnp.sum(jnp.where(pick, starts[None, :], 0), axis=1)
    last = jnp.sum(jnp.where(pick, ends[None, :] - 1, 0), axis=1)
    tail = jnp.sum(jnp.where(pick, tails[None, :], 0), axis=1)
    start = jnp.where(at < ends[-1], start, at)
    return (start - base) * BLK, jnp.where(at == last, tail, BLK)


def by_half(t, ref, shape, dim):
    side = lax.broadcasted_iota(jnp.int32, shape, dim)
    return jnp.where(side < BLK, ref[2 * t], ref[2 * t + 1])


def valid_rows(t, nv_ref):
    row = lax.broadcasted_iota(jnp.int32, (TILE, 1), 0)
    return (row & (BLK - 1)) < by_half(t, nv_ref, (TILE, 1), 0)


def rows_at(t):
    return pl.ds(pl.multiple_of(t * TILE, TILE), TILE)


def far_tiles(lo_ref):
    return sum((lo_ref[2 * t] < 0).astype(jnp.int32) for t in range(TILES))


class Copies:
    def __init__(self, sems):
        self.sems, self.used, self.open = sems, 0, []

    def __call__(self, src, dst):
        copy = pltpu.make_async_copy(src, dst, self.sems.at[self.used])
        self.used += 1
        copy.start()
        return copy

    def out(self, src, dst):
        self.open.append(self(src, dst))

    def finish(self):
        for copy in self.open:
            copy.wait()


class Tiled:
    def __init__(self, src, dst, sems, at, src_cols=slice(None), dst_cols=slice(None)):
        self.args = src, dst, sems, at, src_cols, dst_cols

    def tile(self, t):
        src, dst, sems, at, src_cols, dst_cols = self.args
        rows = rows_at(t) if not isinstance(t, int) else slice(t * TILE, (t + 1) * TILE)
        return pltpu.make_async_copy(src.at[rows, src_cols], dst.at[rows, dst_cols], sems.at[at + t])

    def start(self, t):
        self.tile(t).start()

    def start_all(self):
        for t in range(TILES):
            self.start(t)

    def wait(self, t):
        self.tile(t).wait()

    def wait_all(self):
        for t in range(TILES):
            self.wait(t)


def norm_rows(x):
    return x * lax.rsqrt(jnp.mean(x * x, axis=-1, keepdims=True) + eps)


def silu_and_slope(pre):
    s = 0.5 + 0.5 * jnp.tanh(0.5 * pre)
    return (pre * s).astype(BF16), (s * (1.0 + pre * (1.0 - s))).astype(BF16)


def proj_kernel(masks, pieces, head_ref, *refs):
    x_refs, w_ref = refs[: sum(pieces)], refs[sum(pieces)]
    normed_ref, act_ref, slope_ref, kv_ref, x_s, w_s, normed_s, act_s, slope_s, sems = refs[-10:]
    copies = Copies(sems)
    width = w_ref.shape[0]
    weights = [
        copies(w_ref.at[:, pl.ds(pl.multiple_of(PLACE[i] * width + head_ref[0] * HD, HD), HD)], w_s.at[:, i * HD : (i + 1) * HD])
        for i in range(4)
    ]
    loads, at = [], 0
    for i, count in enumerate(pieces):
        size = TILE // count
        loads.append([copies(x_refs[at + j], x_s.at[i, j * size : (j + 1) * size, :]) for j in range(count)])
        at += count
    for copy in weights:
        copy.wait()
    for i, mask in enumerate(masks):
        for copy in loads[i]:
            copy.wait()
        rows = rows_at(head_ref[0] ^ mask)
        xn = norm_rows(x_s[i].astype(F32)).astype(BF16)
        normed_s[i] = xn
        copies.out(normed_s.at[i], normed_ref.at[rows, :])
        act_s[i], slope_s[i] = silu_and_slope(jnp.dot(xn, w_s[...], preferred_element_type=F32))
        copies.out(act_s.at[i, :, VK], kv_ref.at[i * TILE : (i + 1) * TILE, :])
        copies.out(act_s.at[i], act_ref.at[rows, :])
        copies.out(slope_s.at[i], slope_ref.at[rows, :])
    copies.finish()


def project(head, masks, chunks, w, kept):
    width, n = w.shape[0], len(masks)
    pieces = tuple(len(chunk) for chunk in chunks)
    flat = [piece for chunk in chunks for piece in chunk]
    start = 2 + len(flat)
    return call(
        functools.partial(proj_kernel, masks, pieces),
        (head,),
        (*flat, w, *kept),
        [((SPAN, width), BF16), ((SPAN, 4 * HD), BF16), ((SPAN, 4 * HD), BF16), ((n * TILE, 2 * HD), BF16)],
        [
            pltpu.VMEM((n, TILE, width), BF16),
            pltpu.VMEM((width, 4 * HD), BF16),
            pltpu.VMEM((n, TILE, width), BF16),
            pltpu.VMEM((n, TILE, 4 * HD), BF16),
            pltpu.VMEM((n, TILE, 4 * HD), BF16),
        ],
        4 + len(flat) + 4 * n,
        {start + i: i for i in range(len(kept))},
    )


def cut_kernel(x_ref, y_ref, a_ref, b_ref, x_out, y_out, x_half, y_half, x_s, y_s, sems):
    copies = Copies(sems)
    x, y = copies(x_ref.at[:BLK, :], x_s), copies(y_ref.at[BLK:, :], y_s)
    x.wait()
    copies.out(x_s, x_half)
    y.wait()
    copies.out(y_s, y_half)
    copies.finish()


def gate_kernel(a_ref, b_ref, after_ref, a_out, b_out, sems):
    pass


def d_gated_kernel(g_ref, w_ref, after_ref, out_ref, g_s, w_s, out_s, sems):
    copies = Copies(sems)
    g = copies(g_ref, g_s)
    half = w_s.shape[0] // 2
    loads = [copies(w_ref.at[i * half : (i + 1) * half, :], w_s.at[i * half : (i + 1) * half, :]) for i in range(2)]
    g.wait()
    for i in range(2):
        loads[i].wait()
        d = lax.dot_general(g_s[...], w_s[i * half : (i + 1) * half, :], NT, preferred_element_type=F32).astype(BF16)
        for h in range(HEADS // 2):
            out_s[i * HEADS // 2 + h] = d[:, h * HD : (h + 1) * HD]
    copies.out(out_s, out_ref)
    copies.finish()


def turned(x):
    n = x.shape[1]
    eye = lax.broadcasted_iota(jnp.int32, (n, n), 0) == lax.broadcasted_iota(jnp.int32, (n, n), 1)
    return lax.dot_general(eye.astype(BF16), x, NT, preferred_element_type=F32).astype(BF16)


def sweep(first, last, one, carry):
    count = last - first
    carry = lax.fori_loop(0, count // 2, lambda i, c: one(first + 2 * i + 1, one(first + 2 * i, c)), carry)
    return lax.fori_loop(last - count % 2, last, one, carry)


def weigh(q, k, v, mask):
    half = lax.dot_general(q, k, NT, preferred_element_type=F32) * HALF
    w = half + half * jnp.tanh(half)
    w = jnp.where(mask, w, 0.0).astype(BF16)
    return jnp.dot(w, v, preferred_element_type=F32)


def fwd_own_kernel(lo_ref, nv_ref, act_ref, out_ref, act_s, out_s, sems):
    loads = Tiled(act_ref, act_s, sems, 0)
    stores = Tiled(out_s, out_ref, sems, TILES)
    loads.start_all()
    row = lax.broadcasted_iota(jnp.int32, (TILE, TILE), 0)
    col = lax.broadcasted_iota(jnp.int32, (TILE, TILE), 1)

    def q_tile(t, carry):
        loads.wait(t)
        lo = by_half(t, lo_ref, (TILE, 1), 0) - t * TILE
        q = act_s[rows_at(t), Q]
        acc = weigh(q, act_s[rows_at(t), K], act_s[rows_at(t), V], (col <= row) & (col >= lo))

        def k_tile(s, acc):
            return acc + weigh(q, act_s[rows_at(s), K], act_s[rows_at(s), V], col >= lo + (t - s) * TILE)

        first = jnp.maximum(lo_ref[2 * t], 0) // TILE
        acc = sweep(first, t, k_tile, acc)
        out_s[rows_at(t), :] = jnp.where(valid_rows(t, nv_ref), acc, 0.0)
        stores.start(t)
        return carry

    lax.fori_loop(0, TILES, q_tile, 0)
    stores.wait_all()


def load_far(head_ref, kv_refs, kv_s, copies):
    loads, slot = [], 0
    for ref in kv_refs:
        for at in range(0, ref.shape[0], TILE):
            loads.append(copies(ref.at[at : at + TILE, :], kv_s.at[rows_at(slot ^ head_ref[0]), :]))
            slot += 1
    return loads


def fwd_far_kernel(
    head_ref, lo_ref, nv_ref, act_ref, kva_ref, kvb_ref, kvc_ref, near_ref, dg_ref, out_ref, sum_ref,
    uq_s, kv_s, near_s, dg_s, out_s, sum_s, sems,
):
    uqs = Tiled(act_ref, uq_s, sems, 0, src_cols=UQ)
    nears = Tiled(near_ref, near_s, sems, TILES)
    dgs = Tiled(dg_ref, dg_s, sems, 2 * TILES)
    stores = Tiled(out_s, out_ref, sems, 3 * TILES)
    copies = Copies(sems)
    copies.used = 4 * TILES
    far = load_far(head_ref, (kva_ref, kvb_ref, kvc_ref), kv_s, copies)
    for t in reversed(range(TILES)):
        for loads in (uqs, nears, dgs):
            loads.start(t)
    col = lax.broadcasted_iota(jnp.int32, (TILE, TILE), 1)

    def finish(t, acc):
        attn = acc * (1.0 / SPAN)
        out_s[rows_at(t), :] = attn.astype(BF16)
        stores.start(t)
        d_n = dg_s[rows_at(t), :].astype(F32) * uq_s[rows_at(t), U].astype(F32)
        ones = jnp.ones((8, HD), BF16)
        square = lax.dot_general(ones, (attn * attn).astype(BF16), NT, preferred_element_type=F32)[:1]
        cross = lax.dot_general(ones, (attn * d_n).astype(BF16), NT, preferred_element_type=F32)[:1]
        for h in range(HEADS):
            sum_s[h, pl.ds(t, 1), :] = square
            sum_s[h, pl.ds(TILES + t, 1), :] = cross

    def wait(t):
        for loads in (uqs, nears, dgs):
            loads.wait(t)

    def near_tile(i, carry):
        t = TILES - 1 - i
        wait(t)
        finish(t, near_s[rows_at(t), :])
        return carry

    def far_tile(t, carry):
        wait(t)
        lo = by_half(t, lo_ref, (TILE, 1), 0) + SPAN
        q = uq_s[rows_at(t), Q]

        def k_tile(s, acc):
            return acc + weigh(q, kv_s[rows_at(s), HD:], kv_s[rows_at(s), :HD], col >= lo - s * TILE)

        first = (lo_ref[2 * t] + SPAN) // TILE
        acc = sweep(first, TILES, k_tile, jnp.zeros((TILE, HD), F32))
        finish(t, jnp.where(valid_rows(t, nv_ref), acc, 0.0) + near_s[rows_at(t), :])
        return carry

    count = far_tiles(lo_ref)
    lax.fori_loop(0, TILES - count, near_tile, 0)
    for copy in far:
        copy.wait()
    lax.fori_loop(0, count, far_tile, 0)
    copies.out(sum_s, sum_ref)
    copies.finish()
    stores.wait_all()


def row_scales(sum_s, scale_s):
    width = HEADS * HD
    total = jnp.sum(sum_s[...], axis=0)
    r = lax.rsqrt(total[:TILES] * (1.0 / width) + eps)
    c = total[TILES:] * (1.0 / width) * r
    scales = jnp.concatenate([r, c, jnp.zeros((HD - 2 * TILES, TILE), F32)], axis=0).T
    high = scales.astype(BF16)
    scale_s[:, :HD] = high
    scale_s[:, HD:] = (scales - high.astype(F32)).astype(BF16)


def spread(scale_s, i):
    row = lax.broadcasted_iota(jnp.int32, (2 * HD, HD), 0) & (HD - 1)
    return jnp.dot(scale_s[...], (row == i).astype(BF16), preferred_element_type=F32)


def cotangent(t, scale_s, nv_ref, u, attn, d_gated):
    r, c = spread(scale_s, t), spread(scale_s, TILES + t)
    n = attn.astype(F32) * r
    g = r * (d_gated * u.astype(F32) - n * c)
    return n, jnp.where(valid_rows(t, nv_ref), g, 0.0).astype(BF16)


def back(q, k, kt, v, g, mask):
    half = lax.dot_general(k, q, NT, preferred_element_type=F32) * HALF
    up = jnp.where(mask, 1.0 + jnp.tanh(half), 0.0)
    w = (half * up).astype(BF16)
    dw = lax.dot_general(v, g, NT, preferred_element_type=F32)
    ds = (dw * up * (1.0 + half * (2.0 - up))).astype(BF16)
    dv = jnp.dot(w, g, preferred_element_type=F32)
    dk = jnp.dot(ds, q, preferred_element_type=F32)
    dqt = jnp.dot(kt, ds, preferred_element_type=F32)
    return dv, dk, dqt


def bwd_far_kernel(
    head_ref, lo_ref, nv_ref, sum_ref, act_ref, attn_ref, dg_ref, kva_ref, kvb_ref, kvc_ref, dq_ref, dkv_ref,
    sum_s, uq_s, attn_s, dg_s, kv_s, kt_s, acc_s, scale_s, dq_s, dkv_s, sems,
):
    uqs = Tiled(act_ref, uq_s, sems, 0, src_cols=UQ)
    attns = Tiled(attn_ref, attn_s, sems, TILES)
    dgs = Tiled(dg_ref, dg_s, sems, 2 * TILES)
    dkvs = Tiled(dkv_s, dkv_ref, sems, 4 * TILES)
    copies = Copies(sems)
    copies.used = 5 * TILES
    count = far_tiles(lo_ref)
    first = jnp.minimum(lo_ref[0] + SPAN, SPAN) // TILE

    @pl.when(count > 0)
    def _():
        sums = copies(sum_ref, sum_s)
        far = load_far(head_ref, (kva_ref, kvb_ref, kvc_ref), kv_s, copies)

        def start(t, carry):
            for loads in (uqs, attns, dgs):
                loads.start(t)
            return carry

        lax.fori_loop(0, count, start, 0)
        sums.wait()
        row_scales(sum_s, scale_s)
        for copy in far:
            copy.wait()

        def prepare(s, carry):
            acc_s[rows_at(s), :] = jnp.zeros((TILE, 2 * HD), F32)
            kt_s[:, rows_at(s)] = turned(kv_s[rows_at(s), HD:])
            return carry

        lax.fori_loop(first, TILES, prepare, 0)

        def q_tile(t, carry):
            for loads in (uqs, attns, dgs):
                loads.wait(t)
            lo = by_half(t, lo_ref, (1, TILE), 1) + SPAN
            q = uq_s[rows_at(t), Q]
            d_gated = dg_s[rows_at(t), :].astype(F32)
            g = cotangent(t, scale_s, nv_ref, uq_s[rows_at(t), U], attn_s[rows_at(t), :], d_gated)[1]
            key = lax.broadcasted_iota(jnp.int32, (TILE, TILE), 0)

            def k_tile(s, dqt):
                k, v = kv_s[rows_at(s), HD:], kv_s[rows_at(s), :HD]
                dv, dk, dqt_part = back(q, k, kt_s[:, rows_at(s)], v, g, key >= lo - s * TILE)
                acc_s[rows_at(s), :HD] += dv
                acc_s[rows_at(s), HD:] += dk
                return dqt + dqt_part

            start = (lo_ref[2 * t] + SPAN) // TILE
            dqt = sweep(start, TILES, k_tile, jnp.zeros((HD, TILE), F32))
            dq_s[:, rows_at(t)] = dqt
            return carry

        lax.fori_loop(0, count, q_tile, 0)
        copies.out(dq_s, dq_ref)

        def store(s, carry):
            dkv_s[rows_at(s), :HD] = (acc_s[rows_at(s), :HD] * (1.0 / SPAN)).astype(BF16)
            dkv_s[rows_at(s), HD:] = (acc_s[rows_at(s), HD:] * (HALF / SPAN)).astype(BF16)
            dkvs.start(s)
            return carry

        lax.fori_loop(first, TILES, store, 0)
        lax.fori_loop(first, TILES, lambda s, carry: dkvs.wait(s) or carry, 0)
        copies.finish()


def bwd_own_kernel(
    lo_ref, nv_ref, sum_ref, act_ref, slope_ref, attn_ref, dg_ref, far_ref, rows_ref, cols_ref, dkv_ref,
    sum_s, act_s, slope_s, attn_s, dg_s, far_s, kt_s, acc_s, scale_s, rows_s, cols_s, dkv_s, sems,
):
    acts = Tiled(act_ref, act_s, sems, 0)
    slopes = Tiled(slope_ref, slope_s, sems, TILES, src_cols=UQ)
    attns = Tiled(attn_ref, attn_s, sems, 2 * TILES)
    dgs = Tiled(dg_ref, dg_s, sems, 3 * TILES)
    stores = Tiled(rows_s, rows_ref, sems, 5 * TILES)
    dkvs = Tiled(dkv_s, dkv_ref, sems, 6 * TILES)
    copies = Copies(sems)
    copies.used = 7 * TILES
    sums = copies(sum_ref, sum_s)
    for t in range(TILES):
        for loads in (acts, attns, dgs, slopes):
            loads.start(t)
    count = far_tiles(lo_ref)
    far = copies(far_ref, far_s)
    sums.wait()
    row_scales(sum_s, scale_s)

    def q_tile(t, carry):
        for loads in (acts, attns, dgs, slopes):
            loads.wait(t)
        lo = by_half(t, lo_ref, (1, TILE), 1) - t * TILE
        q, k, v = act_s[rows_at(t), Q], act_s[rows_at(t), K], act_s[rows_at(t), V]
        kt_s[:, rows_at(t)] = turned(k)
        d_gated = dg_s[rows_at(t), :].astype(F32)
        n, g = cotangent(t, scale_s, nv_ref, act_s[rows_at(t), U], attn_s[rows_at(t), :], d_gated)
        du = (d_gated * n).astype(BF16).astype(F32)
        cols_s[:HD, rows_at(t)] = turned((du * slope_s[rows_at(t), U].astype(F32)).astype(BF16))
        key = lax.broadcasted_iota(jnp.int32, (TILE, TILE), 0)
        query = lax.broadcasted_iota(jnp.int32, (TILE, TILE), 1)
        mask = (key <= query) & (key >= lo)
        dv, dk, dqt = back(q, k, kt_s[:, rows_at(t)], v, g, mask)
        acc_s[rows_at(t), :HD] = dv
        acc_s[rows_at(t), HD:] = dk

        def k_tile(s, dqt):
            mask = key >= lo + (t - s) * TILE
            dv, dk, dqt_part = back(q, act_s[rows_at(s), K], kt_s[:, rows_at(s)], act_s[rows_at(s), V], g, mask)
            acc_s[rows_at(s), :HD] += dv
            acc_s[rows_at(s), HD:] += dk
            return dqt + dqt_part

        first = jnp.maximum(lo_ref[2 * t], 0) // TILE
        dqt = sweep(first, t, k_tile, dqt)

        dq = dqt + jnp.where(t < count, far_s[:, rows_at(t)], 0.0)
        dq = (dq * (HALF / SPAN)).astype(BF16).astype(F32)
        dq = (dq * turned(slope_s[rows_at(t), Q]).astype(F32)).astype(BF16)
        cols_s[HD:, rows_at(t)] = dq
        rows_s[rows_at(t), :] = turned(dq)
        stores.start(t)
        return carry

    far.wait()
    lax.fori_loop(0, TILES, q_tile, 0)
    copies.out(cols_s, cols_ref)

    def store(s, carry):
        dkv_s[rows_at(s), :HD] = (acc_s[rows_at(s), :HD] * (1.0 / SPAN)).astype(BF16)
        dkv_s[rows_at(s), HD:] = (acc_s[rows_at(s), HD:] * (HALF / SPAN)).astype(BF16)
        dkvs.start(s)
        return carry

    lax.fori_loop(0, TILES, store, 0)
    copies.finish()
    stores.wait_all()
    dkvs.wait_all()


def key_kernel(lo_ref, nv_ref, own_ref, far_ref, slope_ref, rows_ref, cols_ref, own_s, far_s, slope_s, rows_s, cols_s, sems):
    owns = Tiled(own_ref, own_s, sems, 0)
    fars = Tiled(far_ref, far_s, sems, TILES)
    slopes = Tiled(slope_ref, slope_s, sems, 2 * TILES, src_cols=VK)
    stores = Tiled(rows_s, rows_ref, sems, 3 * TILES)
    copies = Copies(sems)
    copies.used = 4 * TILES
    first = jnp.minimum(lo_ref[2 * TILES], SPAN) // TILE
    for t in range(TILES):
        owns.start(t)
        slopes.start(t)
    lax.fori_loop(first, TILES, lambda t, carry: fars.start(t) or carry, 0)

    def tile(t, carry):
        owns.wait(t)
        slopes.wait(t)

        @pl.when(t >= first)
        def _():
            fars.wait(t)

        far = jnp.where(t >= first, far_s[rows_at(t), :].astype(F32), 0.0)
        d = (own_s[rows_at(t), :].astype(F32) + far).astype(BF16).astype(F32)
        d = (d * slope_s[rows_at(t), :].astype(F32)).astype(BF16)
        rows_s[rows_at(t), :] = d
        stores.start(t)
        cols_s[:, rows_at(t)] = turned(d)
        return carry

    lax.fori_loop(0, TILES, tile, 0)
    copies.out(cols_s, cols_ref)
    copies.finish()
    stores.wait_all()


def joined(ref, part):
    return jnp.concatenate([ref[h, :, part * HD : (part + 1) * HD] for h in range(HEADS)], axis=1)


def rows_kernel(
    attn_ref, q_ref, dg_ref, tokens_ref, w_out_ref, w_in_ref, out_ref, dn_ref,
    attn_s, q_s, dg_s, x_s, wo_s, wu_s, wq_s, out_s, dn_s, sems,
):
    width = w_out_ref.shape[0]
    copies = Copies(sems)
    first = [copies(tokens_ref, x_s), copies(w_in_ref.at[:, :width], wu_s)]
    second = [copies(*pair) for pair in ((attn_ref, attn_s), (w_out_ref, wo_s), (dg_ref, dg_s))]
    third = [copies(q_ref, q_s), copies(w_in_ref.at[:, 2 * width : 3 * width], wq_s)]
    for copy in first:
        copy.wait()
    x = x_s[...].astype(F32)
    u, slope = silu_and_slope(jnp.dot(norm_rows(x).astype(BF16), wu_s[...], preferred_element_type=F32))
    for copy in second:
        copy.wait()
    n = norm_rows(joined(attn_s, 0).astype(F32))
    gated = (n * u.astype(F32)).astype(BF16)
    y = jnp.dot(gated, wo_s[...], preferred_element_type=F32)
    out_s[...] = (x + y).astype(BF16)
    copies.out(out_s, out_ref)
    du = (joined(dg_s, 0).astype(F32) * n).astype(BF16).astype(F32)
    du = (du * slope.astype(F32)).astype(BF16)
    dn_s[...] = lax.dot_general(du, wu_s[...], NT, preferred_element_type=F32)
    for copy in third:
        copy.wait()
    dn_s[...] += lax.dot_general(joined(q_s, 0), wq_s[...], NT, preferred_element_type=F32)
    copies.out(dn_s, dn_ref)
    copies.finish()


def pieces_kernel(groups, group_ref, a_ref, b_ref, normed_ref, *refs):
    outs, (a_s, b_s, normed_s, all_s, sems) = refs[:groups], refs[groups:]
    copies = Copies(sems)
    parts = [slice(i * 2 * TILE, (i + 1) * 2 * TILE) for i in range(TILES // 2)]
    sides = copies(a_ref, a_s), copies(b_ref, b_s)
    loads = [copies(normed_ref.at[part, :], normed_s.at[part, :]) for part in parts]
    for copy in sides:
        copy.wait()
    totals = [0.0, 0.0]
    for part, load in zip(parts, loads):
        load.wait()
        for i, side in enumerate((a_s, b_s)):
            totals[i] += jnp.dot(side[:, part], normed_s[part, :], preferred_element_type=F32)
    for i in range(2):
        all_s[i * HD : (i + 1) * HD, :] = totals[i][:HD].astype(BF16)
        all_s[(2 + i) * HD : (3 + i) * HD, :] = totals[i][HD:].astype(BF16)
    rows = 4 * HD // groups
    for mask in range(groups):
        at = pl.multiple_of((group_ref[0] ^ mask) * rows, rows)
        copies.out(all_s.at[pl.ds(at, rows), :], outs[mask])
    copies.finish()


def last_kernel(groups, kv_ref, dn_ref, tokens_ref, grad_ref, w_in_ref, *refs):
    pieces, (out_ref, share_ref) = refs[:groups], refs[groups : groups + 2]
    kv_s, dn_s, x_s, g_s, wv_s, wk_s, pieces_s, out_s, share_s, sems = refs[groups + 2 :]
    width = w_in_ref.shape[0]
    copies = Copies(sems)
    kv = copies(kv_ref, kv_s)
    wv = copies(w_in_ref.at[:, width : 2 * width], wv_s)
    wk = copies(w_in_ref.at[:, 3 * width :], wk_s)
    rest = [copies(*pair) for pair in ((dn_ref, dn_s), (tokens_ref, x_s), (grad_ref, g_s))]
    loads = [copies(ref, pieces_s.at[i]) for i, ref in enumerate(pieces)]
    kv.wait()
    wv.wait()
    dn = lax.dot_general(joined(kv_s, 0), wv_s[...], NT, preferred_element_type=F32)
    wk.wait()
    dn += lax.dot_general(joined(kv_s, 1), wk_s[...], NT, preferred_element_type=F32)
    for copy in rest:
        copy.wait()
    dn += dn_s[...]
    x = x_s[...].astype(F32)
    r = lax.rsqrt(jnp.mean(x * x, axis=-1, keepdims=True) + eps)
    n = x * r
    dx = r * (dn - n * jnp.mean(dn * n, axis=-1, keepdims=True))
    out_s[...] = (g_s[...].astype(F32) + dx).astype(BF16)
    copies.out(out_s, out_ref)
    for copy in loads:
        copy.wait()
    total = pieces_s[0].astype(F32)
    for i in range(1, groups):
        total += pieces_s[i].astype(F32)
    share_s[...] = total
    copies.out(share_s, share_ref)
    copies.finish()


def call(kernel, scalars, arrays, outs, scratch=(), sems=1, aliases=None, limit=52):
    smem = pl.BlockSpec(memory_space=pltpu.SMEM)
    anywhere = pl.BlockSpec(memory_space=pl.ANY)
    return pl.pallas_call(
        kernel,
        out_shape=[jax.ShapeDtypeStruct(*out) for out in outs],
        in_specs=[smem] * len(scalars) + [anywhere] * len(arrays),
        out_specs=[anywhere] * len(outs),
        scratch_shapes=[*scratch, pltpu.SemaphoreType.DMA((sems,))],
        input_output_aliases=aliases or {},
        compiler_params=pltpu.CompilerParams(vmem_limit_bytes=limit * 2**20),
        cost_estimate=pl.CostEstimate(flops=0, bytes_accessed=0, transcendentals=0),
    )(*scalars, *arrays)


def per_device(groups, tokens, w_in, w_out, block_counts, tails, grad_out):
    count, width = tokens.shape
    group = lax.axis_index("g").astype(jnp.int32)
    head = lax.axis_index("h").astype(jnp.int32).reshape(1)
    info = block_info(block_counts, tails, group * MAXB, MAXB)

    def swap(x, mask):
        return lax.ppermute(x, "h", [(i, i ^ mask) for i in range(HEADS)])

    def exchange(x):
        x = x.reshape(HEADS, -1, x.shape[-1])
        return lax.all_to_all(x, "h", 0, 0, tiled=True)

    def onward(x):
        return lax.ppermute(x, "g", [(i, i + 1) for i in range(groups - 1)])

    def vmem(shape, dtype=BF16):
        return pltpu.VMEM(shape, dtype)

    own, tall, wide = (count, width), (SPAN, HD), (SPAN, 2 * HD)
    across, by_head, square = (2 * HD, SPAN), (HEADS, count, HD), (width, width)
    sum_shape = (HEADS, 2 * TILES, TILE)

    half = ((BLK, width), BF16)
    x_rows, y_rows = swap(tokens, 2), swap(tokens, 4)
    other = swap(tokens, 1)
    *kept, kv = project(head, (0, 1), ((tokens,), (other,)), w_in, ())
    far_kv = [onward(kv)]
    d_gated_rows = call(
        d_gated_kernel, (), (grad_out, w_out, kv), [(by_head, BF16)], [vmem(own), vmem(square), vmem(by_head)], 4
    )[0]
    d_gated = exchange(d_gated_rows).reshape(SPAN, HD)
    x_rows, y_rows, x_half, y_half = call(
        cut_kernel,
        (),
        (x_rows, y_rows, far_kv[0], d_gated_rows),
        [(own, BF16), (own, BF16), half, half],
        [vmem((BLK, width)), vmem((BLK, width))],
        4,
        {0: 0, 1: 1},
        4,
    )
    corner = swap(x_half, 4), swap(y_half, 2)
    chunks = ((x_rows,), (swap(x_rows, 1),), (y_rows,), (swap(y_rows, 1),))
    *kept, kv = project(head, (2, 3, 4, 5), chunks, w_in, kept)
    far_kv.append(onward(kv))
    corner = call(gate_kernel, (), (*corner, kv), [half, half], aliases={0: 0, 1: 1}, limit=4)
    *kept, kv = project(head, (6, 7), (corner, [swap(x, 1) for x in corner]), w_in, kept)
    far_kv.append(onward(kv))
    normed, act, slope = kept

    near = call(fwd_own_kernel, info, (act,), [(tall, F32)], [vmem((SPAN, 4 * HD)), vmem(tall, F32)], 2 * TILES)[0]
    attn, sums = call(
        fwd_far_kernel,
        (head, *info),
        (act, *far_kv, near, d_gated),
        [(tall, BF16), (sum_shape, F32)],
        [vmem(wide), vmem(wide), vmem(tall, F32), vmem(tall), vmem(tall), vmem(sum_shape, F32)],
        4 * TILES + HEADS + 1,
    )
    sums = exchange(sums)

    dq_far, dkv_far = call(
        bwd_far_kernel,
        (head, *info),
        (sums, act, attn, d_gated, *far_kv),
        [((HD, SPAN), F32), (wide, BF16)],
        [vmem(sum_shape, F32), vmem(wide), vmem(tall), vmem(tall), vmem(wide), vmem((HD, SPAN)), vmem(wide, F32)]
        + [vmem((TILE, 2 * HD)), vmem((HD, SPAN), F32), vmem(wide)],
        5 * TILES + HEADS + 2,
    )
    dkv_far = lax.ppermute(dkv_far, "g", [(i + 1, i) for i in range(groups - 1)])
    attn_rows = exchange(attn)
    d_q, cols_a, dkv = call(
        bwd_own_kernel,
        info,
        (sums, act, slope, attn, d_gated, dq_far),
        [(tall, BF16), (across, BF16), (wide, BF16)],
        [vmem(sum_shape, F32), vmem((SPAN, 4 * HD)), vmem(wide), vmem(tall), vmem(tall), vmem((HD, SPAN), F32), vmem((HD, SPAN))]
        + [vmem(wide, F32), vmem((TILE, 2 * HD)), vmem(tall), vmem(across), vmem(wide)],
        7 * TILES + 3,
    )
    d_q = exchange(d_q)
    layer_out, d_normed = call(
        rows_kernel,
        (),
        (attn_rows, d_q, d_gated_rows, tokens, w_out, w_in),
        [(own, BF16), (own, F32)],
        [vmem(by_head), vmem(by_head), vmem(by_head), vmem(own), vmem(square), vmem(square), vmem(square)]
        + [vmem(own), vmem(own, F32)],
        9,
    )
    d_kv, cols_b = call(
        key_kernel,
        info,
        (dkv, dkv_far, slope),
        [(wide, BF16), (across, BF16)],
        [vmem(wide), vmem(wide), vmem(wide), vmem(wide), vmem(across)],
        4 * TILES + 1,
    )
    d_kv = exchange(d_kv)
    rows = 4 * HD // groups
    pieces = call(
        functools.partial(pieces_kernel, groups),
        (group.reshape(1),),
        (cols_a, cols_b, normed),
        [((rows, width), BF16)] * groups,
        [vmem(across), vmem(across), vmem((SPAN, width)), vmem((4 * HD, width))],
        TILES // 2 + 2 + groups,
    )
    pieces = [pieces[0]] + [
        lax.ppermute(pieces[mask], "g", [(i, i ^ mask) for i in range(groups)]) for mask in range(1, groups)
    ]
    grad_tokens, grad_w_in = call(
        functools.partial(last_kernel, groups),
        (),
        (d_kv, d_normed, tokens, grad_out, w_in, *pieces),
        [(own, BF16), ((rows, width), F32)],
        [vmem((HEADS, count, 2 * HD)), vmem(own, F32), vmem(own), vmem(own), vmem(square), vmem(square)]
        + [vmem((groups, rows, width)), vmem(own), vmem((rows, width), F32)],
        8 + groups,
    )
    parts = groups // 4
    if parts > 1:
        perm = [
            (i * HEADS + j, ((i // parts) * HEADS + j) * parts + i % parts)
            for i in range(groups)
            for j in range(HEADS)
        ]
        grad_w_in = lax.ppermute(grad_w_in, ("g", "h"), perm)
    return (layer_out, grad_tokens, grad_w_in)


def solution(mesh):
    groups = mesh.shape["seq"] // HEADS
    split = Mesh(mesh.devices.reshape(groups, HEADS), ("g", "h"))
    rows = P(("g", "h"), None)
    return jax.shard_map(
        functools.partial(per_device, groups),
        mesh=split,
        in_specs=(rows, P(), P(), P(), P(), rows),
        out_specs=(rows, rows, rows),
        check_vma=False,
    )
```

```python
import functools

import jax
import jax.numpy as jnp
from jax import lax
from jax.experimental import pallas as pl
from jax.experimental.pallas import tpu as pltpu
from jax.sharding import Mesh, PartitionSpec as P

HEADS = 8
HD = 128
BLK = 128
MAXB = 16
SPAN = MAXB * BLK
TILE = 256
TILES = SPAN // TILE
CHUNK = 512
CHUNKS = SPAN // CHUNK
HALF = 0.5 * HD ** (-0.5)

eps = 1e-05

NT = (((1,), (1,)), ((), ()))
F32, BF16 = jnp.float32, jnp.bfloat16

U, Q, V, K = (slice(i * HD, (i + 1) * HD) for i in range(4))
PLACE = (0, 2, 1, 3)
UQ, VK = slice(0, 2 * HD), slice(2 * HD, 4 * HD)


def info_kernel(counts_ref, tails_ref, lo_ref, nv_ref, at_ref):
    group = lax.axis_index("g").astype(jnp.int32)
    at_ref[0] = group
    at_ref[1] = lax.axis_index("h").astype(jnp.int32)
    base = group * MAXB
    for j in range(MAXB + 1):
        lo_ref[j] = j * BLK
        nv_ref[j] = BLK

    def user(n, start):
        end = start + counts_ref[n]

        def block(j, carry):
            lo_ref[j] = (start - base) * BLK
            nv_ref[j] = jnp.where(j == end - 1 - base, tails_ref[n], BLK)
            return carry

        lax.fori_loop(jnp.maximum(start - base, 0), jnp.minimum(end - base, MAXB + 1), block, 0)
        return end

    lax.fori_loop(0, counts_ref.shape[0], user, jnp.int32(0))


def by_half(t, ref, shape, dim):
    side = lax.broadcasted_iota(jnp.int32, shape, dim)
    return jnp.where(side < BLK, ref[2 * t], ref[2 * t + 1])


def valid_rows(t, nv_ref):
    row = lax.broadcasted_iota(jnp.int32, (TILE, 1), 0)
    return (row & (BLK - 1)) < by_half(t, nv_ref, (TILE, 1), 0)


def rows_at(t):
    return pl.ds(pl.multiple_of(t * TILE, TILE), TILE)


def chunk_at(c):
    return pl.ds(pl.multiple_of(c * CHUNK, CHUNK), CHUNK)


def lanes_at(i):
    return pl.ds(pl.multiple_of(i * HD, HD), HD)


def norm_rows(x):
    return x * lax.rsqrt(jnp.mean(x * x, axis=-1, keepdims=True) + eps)


def silu_and_slope(pre):
    s = 0.5 + 0.5 * jnp.tanh(0.5 * pre)
    return (pre * s).astype(BF16), (s * (1.0 + pre * (1.0 - s))).astype(BF16)


def proj_kernel(masks, pieces, first, at_ref, *refs):
    x_refs, w_ref = refs[: sum(pieces)], refs[sum(pieces)]
    head, width = at_ref[1], w_ref.shape[0]
    if first:
        normed_ref, act_ref, slope_ref, kv_ref, wh_ref = refs[-5:]
        for i in range(4):
            wh_ref[:, i * HD : (i + 1) * HD] = w_ref[:, lanes_at(PLACE[i] * (width // HD) + head)]
    else:
        normed_ref, act_ref, slope_ref, kv_ref = refs[-4:]
        wh_ref = w_ref
    for i, mask in enumerate(masks):
        parts = [ref[...] for ref in x_refs[sum(pieces[:i]) : sum(pieces[: i + 1])]]
        x = parts[0] if len(parts) == 1 else jnp.concatenate(parts, axis=0)
        rows = rows_at(head ^ mask)
        xn = norm_rows(x.astype(F32)).astype(BF16)
        normed_ref[rows, :] = xn
        act, slope = silu_and_slope(jnp.dot(xn, wh_ref[...], preferred_element_type=F32))
        act_ref[rows, :] = act
        slope_ref[rows, :] = slope
        kv_ref[i * TILE : (i + 1) * TILE, :] = act[:, VK]


def project(info, masks, chunks, w, kept):
    width, n = w.shape[0], len(masks)
    first = not kept
    pieces = tuple(len(chunk) for chunk in chunks)
    flat = [piece for chunk in chunks for piece in chunk]
    start = 2 + len(flat)
    outs = [((SPAN, width), BF16), ((SPAN, 4 * HD), BF16), ((SPAN, 4 * HD), BF16), ((n * TILE, 2 * HD), BF16)]
    if first:
        outs.append(((width, 4 * HD), BF16))
    return call(
        functools.partial(proj_kernel, masks, pieces, first),
        (info[2],),
        (*flat, w),
        outs,
        after=kept,
        aliases={start + i: i for i in range(len(kept))},
    )


def cut_kernel(x_ref, y_ref, a_ref, b_ref, x_out, y_out, x_half, y_half):
    x_half[...] = x_ref[:BLK, :]
    y_half[...] = y_ref[BLK:, :]


def gate_kernel(a_ref, b_ref, after_ref, a_out, b_out):
    pass


def d_gated_kernel(at_ref, g_ref, w_ref, after_ref, *refs):
    outs, d_s = refs[:-1], refs[-1]
    d_s[...] = lax.dot_general(g_ref[...], w_ref[...], NT, preferred_element_type=F32).astype(BF16)
    for mask in range(HEADS):
        outs[mask][...] = d_s[:, lanes_at(at_ref[1] ^ mask)]


def weigh(q, kt, v, mask):
    half = jnp.dot(q, kt, preferred_element_type=F32) * HALF
    w = half + half * jnp.tanh(half)
    w = jnp.where(mask, w, 0.0).astype(BF16)
    return jnp.dot(w, v, preferred_element_type=F32)


def fwd_own_kernel(lo_ref, nv_ref, act_ref, slope_ref, out_ref, kt_ref, qt_ref, slope_qt_ref):
    for t in range(TILES):
        rows = slice(t * TILE, (t + 1) * TILE)
        kt_ref[:, rows] = act_ref[rows, K].T
    row = lax.broadcasted_iota(jnp.int32, (TILE, CHUNK), 0)
    col = lax.broadcasted_iota(jnp.int32, (TILE, CHUNK), 1)

    def q_tile(t, carry):
        lo = by_half(t, lo_ref, (TILE, 1), 0)
        q = act_ref[rows_at(t), Q]

        def k_chunk(c, acc):
            mask = (col >= lo - c * CHUNK) & (col - row <= t * TILE - c * CHUNK)
            return acc + weigh(q, kt_ref[:, chunk_at(c)], act_ref[chunk_at(c), V], mask)

        first = jnp.maximum(lo_ref[2 * t], 0) // CHUNK
        acc = lax.fori_loop(first, t // 2 + 1, k_chunk, jnp.zeros((TILE, HD), F32))
        out_ref[rows_at(t), :] = jnp.where(valid_rows(t, nv_ref), acc, 0.0)
        return carry

    lax.fori_loop(0, TILES, q_tile, 0)
    for t in range(TILES):
        rows = slice(t * TILE, (t + 1) * TILE)
        qt_ref[:, rows] = act_ref[rows, Q].T
        slope_qt_ref[:, rows] = slope_ref[rows, Q].T


def fwd_far_kernel(
    lo_ref, nv_ref, at_ref, act_ref, kva_ref, kvb_ref, kvc_ref, near_ref, *refs
):
    dg_refs, (out_ref, sum_ref, kv_ref, kt_ref), pieces, (attn_s, dg_s) = refs[:HEADS], refs[HEADS : HEADS + 4], refs[HEADS + 4 : -2], refs[-2:]
    head = at_ref[1]
    slot = 0
    for ref in (kva_ref, kvb_ref, kvc_ref):
        for at in range(0, ref.shape[0], TILE):
            kv_ref[rows_at(slot ^ head), :] = ref[at : at + TILE, :]
            slot += 1
    for mask in range(HEADS):
        dg_s[rows_at(head ^ mask), :] = dg_refs[mask][...]
    first = jnp.minimum(lo_ref[0] + SPAN, SPAN) // CHUNK
    for t in range(TILES):
        rows = slice(t * TILE, (t + 1) * TILE)

        @pl.when(t // 2 >= first)
        def _():
            kt_ref[:, rows] = kv_ref[rows, HD:].T

    attn_s[...] = near_ref[...]
    col = lax.broadcasted_iota(jnp.int32, (TILE, CHUNK), 1)

    def q_tile(t, carry):
        lo = by_half(t, lo_ref, (TILE, 1), 0) + SPAN
        q = act_ref[rows_at(t), Q]

        def k_chunk(c, acc):
            return acc + weigh(q, kt_ref[:, chunk_at(c)], kv_ref[chunk_at(c), :HD], col >= lo - c * CHUNK)

        start = (lo_ref[2 * t] + SPAN) // CHUNK
        acc = lax.fori_loop(start, CHUNKS, k_chunk, jnp.zeros((TILE, HD), F32))
        attn_s[rows_at(t), :] += jnp.where(valid_rows(t, nv_ref), acc, 0.0)
        return carry

    lax.fori_loop(0, far_tiles(lo_ref), q_tile, 0)
    ones = jnp.ones((8, HD), BF16)
    for t in range(TILES):
        rows = slice(t * TILE, (t + 1) * TILE)
        attn = attn_s[rows, :] * (1.0 / SPAN)
        out_ref[rows, :] = attn.astype(BF16)
        d_n = dg_s[rows, :].astype(F32) * act_ref[rows, U].astype(F32)
        square = lax.dot_general(ones, (attn * attn).astype(BF16), NT, preferred_element_type=F32)
        cross = lax.dot_general(ones, (attn * d_n).astype(BF16), NT, preferred_element_type=F32)
        sum_ref[t : t + 1, :] = square[:1]
        sum_ref[TILES + t : TILES + t + 1, :] = cross[:1]
    for mask in range(HEADS):
        pieces[mask][...] = out_ref[rows_at(head ^ mask), :]


def far_tiles(lo_ref):
    return sum((lo_ref[2 * t] < 0).astype(jnp.int32) for t in range(TILES))


def row_scales(sum_refs):
    width = HEADS * HD
    total = sum_refs[0][...]
    for ref in sum_refs[1:]:
        total += ref[...]
    r = lax.rsqrt(total[:TILES] * (1.0 / width) + eps)
    c = total[TILES:] * (1.0 / width) * r
    return jnp.concatenate([r, c], axis=0).T


def place_d_gated(at_ref, dg_refs, dg_s):
    for mask in range(HEADS):
        dg_s[rows_at(at_ref[1] ^ mask), :] = dg_refs[mask][...]


def cotangent(t, scales, nv_ref, u, attn, d_gated):
    r, c = scales[:, t : t + 1], scales[:, TILES + t : TILES + t + 1]
    n = attn.astype(F32) * r
    g = r * (d_gated * u.astype(F32) - n * c)
    return n, jnp.where(valid_rows(t, nv_ref), g, 0.0).astype(BF16)


def back(q, qt, k, kt, v, g, gt, mask):
    half = jnp.dot(k, qt, preferred_element_type=F32) * HALF
    up = jnp.where(mask, 1.0 + jnp.tanh(half), 0.0)
    w = (half * up).astype(BF16)
    dw = jnp.dot(v, gt, preferred_element_type=F32)
    ds = (dw * up * (1.0 + half * (2.0 - up))).astype(BF16)
    dv = jnp.dot(w, g, preferred_element_type=F32)
    dk = jnp.dot(ds, q, preferred_element_type=F32)
    dqt = jnp.dot(kt, ds, preferred_element_type=F32)
    return dv, dk, dqt


def bwd_far_kernel(lo_ref, nv_ref, at_ref, act_ref, qt_ref, attn_ref, kv_ref, kt_ref, *refs):
    sum_refs, dg_refs, (dqt_ref, dkv_ref, dg_s, acc_s) = refs[:HEADS], refs[HEADS : 2 * HEADS], refs[2 * HEADS :]
    first = jnp.minimum(lo_ref[0] + SPAN, SPAN) // CHUNK

    @pl.when(first < CHUNKS)
    def _():
        place_d_gated(at_ref, dg_refs, dg_s)
        scales = row_scales(sum_refs)

        def clear(c, carry):
            acc_s[chunk_at(c), :] = jnp.zeros((CHUNK, 2 * HD), F32)
            return carry

        lax.fori_loop(first, CHUNKS, clear, 0)
        for t in range(TILES):

            @pl.when(lo_ref[2 * t] < 0)
            def _():
                lo = by_half(t, lo_ref, (1, TILE), 1) + SPAN
                rows = slice(t * TILE, (t + 1) * TILE)
                q, qt = act_ref[rows, Q], qt_ref[:, rows]
                g = cotangent(t, scales, nv_ref, act_ref[rows, U], attn_ref[rows, :], dg_s[rows, :].astype(F32))[1]
                gt = g.T
                key = lax.broadcasted_iota(jnp.int32, (CHUNK, TILE), 0)

                def k_chunk(c, dqt):
                    at = chunk_at(c)
                    dv, dk, part = back(q, qt, kv_ref[at, HD:], kt_ref[:, at], kv_ref[at, :HD], g, gt, key >= lo - c * CHUNK)
                    acc_s[at, :HD] += dv
                    acc_s[at, HD:] += dk
                    return dqt + part

                start = (lo_ref[2 * t] + SPAN) // CHUNK
                dqt_ref[:, rows] = lax.fori_loop(start, CHUNKS, k_chunk, jnp.zeros((HD, TILE), F32))

        def store(c, carry):
            dkv_ref[chunk_at(c), :HD] = (acc_s[chunk_at(c), :HD] * (1.0 / SPAN)).astype(BF16)
            dkv_ref[chunk_at(c), HD:] = (acc_s[chunk_at(c), HD:] * (HALF / SPAN)).astype(BF16)
            return carry

        lax.fori_loop(first, CHUNKS, store, 0)


def bwd_own_kernel(lo_ref, nv_ref, at_ref, act_ref, slope_ref, slope_qt_ref, attn_ref, qt_ref, kt_ref, far_ref, *refs):
    sum_refs, dg_refs, (cols_ref, dkv_ref) = refs[:HEADS], refs[HEADS : 2 * HEADS], refs[2 * HEADS : 2 * HEADS + 2]
    pieces, (dg_s, g_s, gt_s, rows_s) = refs[2 * HEADS + 2 : -4], refs[-4:]
    place_d_gated(at_ref, dg_refs, dg_s)
    scales = row_scales(sum_refs)
    count = far_tiles(lo_ref)
    for t in range(TILES):
        rows = slice(t * TILE, (t + 1) * TILE)
        d_gated = dg_s[rows, :].astype(F32)
        n, g = cotangent(t, scales, nv_ref, act_ref[rows, U], attn_ref[rows, :], d_gated)
        g_s[rows, :] = g
        gt_s[:, rows] = g.T
        du = (d_gated * n).astype(BF16).astype(F32)
        cols_ref[:HD, rows] = (du * slope_ref[rows, U].astype(F32)).astype(BF16).T
    for c in range(CHUNKS):
        dkv_ref[c * CHUNK : (c + 1) * CHUNK, :] = jnp.zeros((CHUNK, 2 * HD), F32)
    key = lax.broadcasted_iota(jnp.int32, (CHUNK, TILE), 0)
    query = lax.broadcasted_iota(jnp.int32, (CHUNK, TILE), 1)

    def q_tile(t, carry):
        lo = by_half(t, lo_ref, (1, TILE), 1)
        q, qt = act_ref[rows_at(t), Q], qt_ref[:, rows_at(t)]
        g, gt = g_s[rows_at(t), :], gt_s[:, rows_at(t)]

        def k_chunk(c, dqt):
            at = chunk_at(c)
            mask = (key >= lo - c * CHUNK) & (key - query <= t * TILE - c * CHUNK)
            dv, dk, part = back(q, qt, act_ref[at, K], kt_ref[:, at], act_ref[at, V], g, gt, mask)
            dkv_ref[at, :HD] += dv
            dkv_ref[at, HD:] += dk
            return dqt + part

        first = jnp.maximum(lo_ref[2 * t], 0) // CHUNK
        dqt = lax.fori_loop(first, t // 2 + 1, k_chunk, jnp.zeros((HD, TILE), F32))
        dq = dqt + jnp.where(t < count, far_ref[:, rows_at(t)], 0.0)
        dq = (dq * (HALF / SPAN)).astype(BF16).astype(F32)
        dq = (dq * slope_qt_ref[:, rows_at(t)].astype(F32)).astype(BF16)
        cols_ref[HD:, rows_at(t)] = dq
        rows_s[rows_at(t), :] = dq.T
        return carry

    lax.fori_loop(0, TILES, q_tile, 0)
    for mask in range(HEADS):
        pieces[mask][...] = rows_s[rows_at(at_ref[1] ^ mask), :]


def key_kernel(groups, lo_ref, at_ref, own_ref, far_ref, slope_ref, cols_ref, normed_ref, *refs):
    pieces, shares, (cols_s, all_s) = refs[:HEADS], refs[HEADS:-2], refs[-2:]
    first = jnp.minimum(lo_ref[2 * TILES], SPAN) // CHUNK
    scale = jnp.where(lax.broadcasted_iota(jnp.int32, (1, 2 * HD), 1) < HD, 1.0 / SPAN, HALF / SPAN)
    for mask in range(HEADS):
        t = at_ref[1] ^ mask
        rows = rows_at(t)
        far = jnp.where(t // 2 >= first, far_ref[rows, :].astype(F32), 0.0)
        d = (own_ref[rows, :] * scale + far).astype(BF16).astype(F32)
        d = (d * slope_ref[rows, VK].astype(F32)).astype(BF16)
        pieces[mask][...] = d
        cols_s[:, rows] = d.T
    share = jnp.dot(cols_ref[...], normed_ref[...], preferred_element_type=F32).astype(BF16)
    all_s[:HD, :], all_s[2 * HD : 3 * HD, :] = share[:HD], share[HD:]
    share = jnp.dot(cols_s[...], normed_ref[...], preferred_element_type=F32).astype(BF16)
    all_s[HD : 2 * HD, :], all_s[3 * HD :, :] = share[:HD], share[HD:]
    size = 4 * HD // groups
    for mask in range(groups):
        at = pl.multiple_of((at_ref[0] ^ mask) * size, size)
        shares[mask][...] = all_s[pl.ds(at, size), :]


def assemble(at_ref, refs, cols, out_s):
    for mask in range(HEADS):
        out_s[:, lanes_at(at_ref[1] ^ mask)] = refs[mask][:, cols]
    return out_s[...]


def through(x, w_ref, branch):
    width = w_ref.shape[0]
    return lax.dot_general(x, w_ref[:, branch * width : (branch + 1) * width], NT, preferred_element_type=F32)


def rows_kernel(at_ref, *refs):
    attn_refs, q_refs, dg_refs = refs[:HEADS], refs[HEADS : 2 * HEADS], refs[2 * HEADS : 3 * HEADS]
    tokens_ref, w_out_ref, w_in_ref, out_ref, dn_ref, row_s = refs[3 * HEADS :]
    width = w_out_ref.shape[0]
    x = tokens_ref[...].astype(F32)
    u, slope = silu_and_slope(jnp.dot(norm_rows(x).astype(BF16), w_in_ref[:, :width], preferred_element_type=F32))
    n = norm_rows(assemble(at_ref, attn_refs, slice(None), row_s).astype(F32))
    gated = (n * u.astype(F32)).astype(BF16)
    y = jnp.dot(gated, w_out_ref[...], preferred_element_type=F32)
    out_ref[...] = (x + y).astype(BF16)
    du = (assemble(at_ref, dg_refs, slice(None), row_s).astype(F32) * n).astype(BF16).astype(F32)
    du = (du * slope.astype(F32)).astype(BF16)
    dn_ref[...] = through(du, w_in_ref, 0) + through(assemble(at_ref, q_refs, slice(None), row_s), w_in_ref, 2)


def last_kernel(groups, at_ref, *refs):
    vk_refs, shares, (dn_ref, tokens_ref, grad_ref, w_in_ref) = refs[:HEADS], refs[HEADS : HEADS + groups], refs[HEADS + groups : -3]
    out_ref, share_ref, row_s = refs[-3:]
    dn = dn_ref[...] + through(assemble(at_ref, vk_refs, slice(HD), row_s), w_in_ref, 1)
    dn += through(assemble(at_ref, vk_refs, slice(HD, 2 * HD), row_s), w_in_ref, 3)
    x = tokens_ref[...].astype(F32)
    r = lax.rsqrt(jnp.mean(x * x, axis=-1, keepdims=True) + eps)
    n = x * r
    dx = r * (dn - n * jnp.mean(dn * n, axis=-1, keepdims=True))
    out_ref[...] = (grad_ref[...].astype(F32) + dx).astype(BF16)
    total = shares[0][...].astype(F32)
    for ref in shares[1:]:
        total += ref[...].astype(F32)
    share_ref[...] = total


def call(kernel, scalars, arrays, outs, scratch=(), after=(), aliases=None, limit=16):
    smem = pl.BlockSpec(memory_space=pltpu.SMEM)
    vmem = pl.BlockSpec(memory_space=pltpu.VMEM)
    anywhere = pl.BlockSpec(memory_space=pl.ANY)
    return pl.pallas_call(
        kernel,
        out_shape=[jax.ShapeDtypeStruct(*out) for out in outs],
        in_specs=[smem] * len(scalars) + [vmem] * len(arrays) + [anywhere] * len(after),
        out_specs=[smem if out[1] == jnp.int32 else vmem for out in outs],
        scratch_shapes=[pltpu.VMEM(*shape) for shape in scratch],
        input_output_aliases=aliases or {},
        compiler_params=pltpu.CompilerParams(vmem_limit_bytes=limit * 2**20),
        cost_estimate=pl.CostEstimate(flops=0, bytes_accessed=0, transcendentals=0),
    )(*scalars, *arrays, *after)


def per_device(groups, tokens, w_in, w_out, block_counts, tails, grad_out):
    count, width = tokens.shape
    own, tall, wide, tall_t = (count, width), (SPAN, HD), (SPAN, 2 * HD), (HD, SPAN)
    piece, half, sums_shape = (count, HD), (BLK, width), (2 * TILES, TILE)

    def swap(x, mask):
        return lax.ppermute(x, "h", [(i, i ^ mask) for i in range(HEADS)])

    def trade(pieces):
        return [pieces[0]] + [swap(pieces[mask], mask) for mask in range(1, HEADS)]

    def onward(x):
        return lax.ppermute(x, "g", [(i, i + 1) for i in range(groups - 1)])

    info = call(info_kernel, (block_counts, tails), (), [((MAXB + 1,), jnp.int32)] * 2 + [((2,), jnp.int32)])

    x_rows, y_rows = swap(tokens, 2), swap(tokens, 4)
    *kept, kv, w_head = project(info, (0, 1), ((tokens,), (swap(tokens, 1),)), w_in, ())
    far_kv = [onward(kv)]
    dg_own = call(d_gated_kernel, (info[2],), (grad_out, w_out), [(piece, BF16)] * HEADS, [(own, BF16)], (kv,))
    d_gated = trade(dg_own)
    x_rows, y_rows, x_half, y_half = call(
        cut_kernel,
        (),
        (x_rows, y_rows),
        [(own, BF16), (own, BF16), (half, BF16), (half, BF16)],
        after=(far_kv[0], dg_own[0]),
        aliases={0: 0, 1: 1},
        limit=4,
    )
    corner = swap(x_half, 4), swap(y_half, 2)
    chunks = ((x_rows,), (swap(x_rows, 1),), (y_rows,), (swap(y_rows, 1),))
    *kept, kv = project(info, (2, 3, 4, 5), chunks, w_head, kept)
    far_kv.append(onward(kv))
    corner = call(gate_kernel, (), (), [(half, BF16), (half, BF16)], after=(*corner, kv), aliases={0: 0, 1: 1}, limit=4)
    *kept, kv = project(info, (6, 7), (corner, [swap(x, 1) for x in corner]), w_head, kept)
    far_kv.append(onward(kv))
    normed, act, slope = kept

    near, kt, qt, slope_qt = call(fwd_own_kernel, info[:2], (act, slope), [(tall, F32)] + [(tall_t, BF16)] * 3)
    attn, sums, kv, far_kt, *attn_pieces = call(
        fwd_far_kernel,
        info,
        (act, *far_kv, near, *d_gated),
        [(tall, BF16), (sums_shape, F32), (wide, BF16), (tall_t, BF16)] + [(piece, BF16)] * HEADS,
        [(tall, F32), (tall, BF16)],
    )
    sums = trade([sums] * HEADS)

    dqt_far, dkv_far = call(
        bwd_far_kernel,
        info,
        (act, qt, attn, kv, far_kt, *sums, *d_gated),
        [(tall_t, F32), (wide, BF16)],
        [(tall, BF16), (wide, F32)],
    )
    dkv_far = lax.ppermute(dkv_far, "g", [(i + 1, i) for i in range(groups - 1)])
    attn_rows = trade(attn_pieces)
    cols, dkv, *d_q = call(
        bwd_own_kernel,
        info,
        (act, slope, slope_qt, attn, qt, kt, dqt_far, *sums, *d_gated),
        [((2 * HD, SPAN), BF16), (wide, F32)] + [(piece, BF16)] * HEADS,
        [(tall, BF16), (tall, BF16), (tall_t, BF16), (tall, BF16)],
    )
    d_q = trade(d_q)
    rows = 4 * HD // groups
    outs = call(
        functools.partial(key_kernel, groups),
        (info[0], info[2]),
        (dkv, dkv_far, slope, cols, normed),
        [((count, 2 * HD), BF16)] * HEADS + [((rows, width), BF16)] * groups,
        [((2 * HD, SPAN), BF16), ((4 * HD, width), BF16)],
    )
    d_vk, shares = outs[:HEADS], outs[HEADS:]
    shares = [shares[0]] + [
        lax.ppermute(shares[mask], "g", [(i, i ^ mask) for i in range(groups)]) for mask in range(1, groups)
    ]
    d_vk = trade(d_vk)
    layer_out, d_normed = call(
        rows_kernel,
        (info[2],),
        (*attn_rows, *d_q, *dg_own, tokens, w_out, w_in),
        [(own, BF16), (own, F32)],
        [(own, BF16)],
    )
    grad_tokens, grad_w_in = call(
        functools.partial(last_kernel, groups),
        (info[2],),
        (*d_vk, *shares, d_normed, tokens, grad_out, w_in),
        [(own, BF16), ((rows, width), F32)],
        [(own, BF16)],
    )
    parts = groups // 4
    if parts > 1:
        perm = [
            (i * HEADS + j, ((i // parts) * HEADS + j) * parts + i % parts)
            for i in range(groups)
            for j in range(HEADS)
        ]
        grad_w_in = lax.ppermute(grad_w_in, ("g", "h"), perm)
    return (layer_out, grad_tokens, grad_w_in)


def solution(mesh):
    groups = mesh.shape["seq"] // HEADS
    split = Mesh(mesh.devices.reshape(groups, HEADS), ("g", "h"))
    rows = P(("g", "h"), None)
    return jax.shard_map(
        functools.partial(per_device, groups),
        mesh=split,
        in_specs=(rows, P(), P(), P(), P(), rows),
        out_specs=(rows, rows, rows),
        check_vma=False,
    )
```

```python
import functools

import jax
import jax.numpy as jnp
from jax import lax
from jax.experimental import pallas as pl
from jax.experimental.pallas import tpu as pltpu
from jax.sharding import Mesh, PartitionSpec as P

HEADS = 8
HD = 128
BLK = 128
MAXB = 16
SPAN = MAXB * BLK
TILE = 256
TILES = SPAN // TILE
CHUNK = 512
CHUNKS = SPAN // CHUNK
SCALE = HD ** (-0.5)
LOG2E = 1.4426950408889634

eps = 1e-05

NT = (((1,), (1,)), ((), ()))
F32, BF16 = jnp.float32, jnp.bfloat16

U, Q, V, K = (slice(i * HD, (i + 1) * HD) for i in range(4))
PLACE = (0, 2, 1, 3)
UQ, VK = slice(0, 2 * HD), slice(2 * HD, 4 * HD)


def info_kernel(counts_ref, tails_ref, lo_ref, nv_ref, at_ref):
    group = lax.axis_index("g").astype(jnp.int32)
    at_ref[0] = group
    at_ref[1] = lax.axis_index("h").astype(jnp.int32)
    base = group * MAXB
    for j in range(2 * MAXB):
        lo_ref[j] = j * BLK
        nv_ref[j] = BLK

    def user(n, start):
        end = start + counts_ref[n]

        def block(j, carry):
            lo_ref[j] = (start - base) * BLK
            nv_ref[j] = jnp.where(j == end - 1 - base, tails_ref[n], BLK)
            return carry

        lax.fori_loop(jnp.maximum(start - base, 0), jnp.minimum(end - base, 2 * MAXB), block, 0)
        return end

    lax.fori_loop(0, counts_ref.shape[0], user, jnp.int32(0))


def by_half(t, ref, shape, dim):
    side = lax.broadcasted_iota(jnp.int32, shape, dim)
    return jnp.where(side < BLK, ref[2 * t], ref[2 * t + 1])


def from_start(t, lo_ref, at, keys, dim):
    parts = [part >= lo_ref[2 * t + i] - at for i, part in enumerate(jnp.split(keys, 2, axis=1 - dim))]
    return jnp.concatenate(parts, axis=1 - dim)


def valid_rows(t, nv_ref):
    row = lax.broadcasted_iota(jnp.int32, (TILE, 1), 0)
    return (row & (BLK - 1)) < by_half(t, nv_ref, (TILE, 1), 0)


def rows_at(t):
    return pl.ds(pl.multiple_of(t * TILE, TILE), TILE)


def chunk_at(c):
    return pl.ds(pl.multiple_of(c * CHUNK, CHUNK), CHUNK)


def lanes_at(i):
    return pl.ds(pl.multiple_of(i * HD, HD), HD)


def norm_rows(x):
    return x * lax.rsqrt(jnp.mean(x * x, axis=-1, keepdims=True) + eps)


def silu_and_slope(pre):
    s = 0.5 + 0.5 * jnp.tanh(0.5 * pre)
    return (pre * s).astype(BF16), (s * (1.0 + pre * (1.0 - s))).astype(BF16)


def store_rows(x, place, wh_ref, normed_ref, act_ref, slope_ref, kv_ref, i):
    rows = rows_at(place)
    xn = norm_rows(x.astype(F32)).astype(BF16)
    normed_ref[rows, :] = xn
    act, slope = silu_and_slope(jnp.dot(xn, wh_ref[...], preferred_element_type=F32))
    act_ref[rows, :] = act
    slope_ref[rows, :] = slope
    kv_ref[i * TILE : (i + 1) * TILE, :] = act[:, VK]


def first_kernel(other_ref, tokens_ref, w_ref, normed_ref, act_ref, slope_ref, kv_ref, wh_ref, x_s, sems):
    head, width = lax.axis_index("h").astype(jnp.int32), w_ref.shape[0]
    copies = [pltpu.make_async_copy(tokens_ref, x_s, sems.at[4])]
    for i in range(4):
        source = w_ref.at[:, lanes_at(PLACE[i] * (width // HD) + head)]
        copies.append(pltpu.make_async_copy(source, wh_ref.at[:, i * HD : (i + 1) * HD], sems.at[i]))
    for copy in copies:
        copy.start()
    for copy in copies:
        copy.wait()
    outs = wh_ref, normed_ref, act_ref, slope_ref, kv_ref
    store_rows(x_s[...], head, *outs, 0)
    store_rows(other_ref[...], head ^ 1, *outs, 1)


def proj_kernel(masks, pieces, last, at_ref, *refs):
    x_refs, wh_ref = refs[: sum(pieces)], refs[sum(pieces)]
    outs = refs[-5:-1] if last else refs[-4:]
    for i, mask in enumerate(masks):
        parts = [ref[...] for ref in x_refs[sum(pieces[:i]) : sum(pieces[: i + 1])]]
        x = parts[0] if len(parts) == 1 else jnp.concatenate(parts, axis=0)
        store_rows(x, at_ref[1] ^ mask, wh_ref, *outs, i)
    if last:
        refs[-1][...] = outs[1][:, Q]


def proj_outs(width, n):
    return [((SPAN, width), BF16), ((SPAN, 4 * HD), BF16), ((SPAN, 4 * HD), BF16), ((n * TILE, 2 * HD), BF16)]


def project(info, masks, chunks, w, kept, last=False):
    pieces = tuple(len(chunk) for chunk in chunks)
    flat = [piece for chunk in chunks for piece in chunk]
    start = 2 + len(flat)
    return call(
        functools.partial(proj_kernel, masks, pieces, last),
        (info[2],),
        (*flat, w),
        proj_outs(w.shape[0], len(masks)) + ([((SPAN, HD), BF16)] if last else []),
        after=kept,
        aliases={start + i: i for i in range(len(kept))},
    )


def cut_kernel(x_ref, y_ref, *refs):
    x_half, y_half = refs[-2:]
    x_half[...] = x_ref[:BLK, :]
    y_half[...] = y_ref[BLK:, :]


def gate_kernel(*refs):
    pass


def d_gated_kernel(g_ref, w_ref, after_ref, *refs):
    outs, d_s = refs[:-1], refs[-1]
    d_s[...] = lax.dot_general(g_ref[...], w_ref[...], NT, preferred_element_type=F32).astype(BF16)
    for mask in range(HEADS):
        outs[mask][...] = d_s[:, lanes_at(lax.axis_index("h").astype(jnp.int32) ^ mask)]


def sigmoid(s):
    return pl.reciprocal(1.0 + jnp.exp2(s * (-SCALE * LOG2E)), approx=True)


def weigh(q, kt, v, mask):
    s = jnp.dot(q, kt, preferred_element_type=F32)
    w = jnp.where(mask, s * sigmoid(s), 0.0).astype(BF16)
    return jnp.dot(w, v, preferred_element_type=F32)


def fwd_own_kernel(lo_ref, nv_ref, act_ref, slope_ref, out_ref, kt_ref, qt_ref, slope_qt_ref):
    for t in range(TILES):
        rows = slice(t * TILE, (t + 1) * TILE)
        kt_ref[:, rows] = act_ref[rows, K].T
    row = lax.broadcasted_iota(jnp.int32, (TILE, CHUNK), 0)
    col = lax.broadcasted_iota(jnp.int32, (TILE, CHUNK), 1)

    def q_tile(t, carry):
        q = act_ref[rows_at(t), Q]

        def k_chunk(c, acc):
            mask = from_start(t, lo_ref, c * CHUNK, col, 1) & (col - row <= t * TILE - c * CHUNK)
            return acc + weigh(q, kt_ref[:, chunk_at(c)], act_ref[chunk_at(c), V], mask)

        first = jnp.maximum(lo_ref[2 * t], 0) // CHUNK
        acc = lax.fori_loop(first, t // 2 + 1, k_chunk, jnp.zeros((TILE, HD), F32))
        out_ref[rows_at(t), :] = jnp.where(valid_rows(t, nv_ref), acc, 0.0)
        return carry

    lax.fori_loop(0, TILES, q_tile, 0)
    for t in range(TILES):
        rows = slice(t * TILE, (t + 1) * TILE)
        qt_ref[:, rows] = act_ref[rows, Q].T
        slope_qt_ref[:, rows] = slope_ref[rows, Q].T


def fwd_far_kernel(
    lo_ref, nv_ref, at_ref, act_ref, kva_ref, kvb_ref, kvc_ref, near_ref, *refs,
):
    dg_refs, (out_ref, kv_ref, kt_ref), pieces, (sum_s, attn_s, dg_s) = refs[:HEADS], refs[HEADS : HEADS + 3], refs[HEADS + 3 : -3], refs[-3:]
    head = at_ref[1]
    slot = 0
    for ref in (kva_ref, kvb_ref, kvc_ref):
        for at in range(0, ref.shape[0], TILE):
            kv_ref[rows_at(slot ^ head), :] = ref[at : at + TILE, :]
            slot += 1
    for mask in range(HEADS):
        dg_s[rows_at(head ^ mask), :] = dg_refs[mask][...]
    first = jnp.minimum(lo_ref[0] + SPAN, SPAN) // CHUNK
    for t in range(TILES):
        rows = slice(t * TILE, (t + 1) * TILE)

        @pl.when(t // 2 >= first)
        def _():
            kt_ref[:, rows] = kv_ref[rows, HD:].T

    attn_s[...] = near_ref[...]
    col = lax.broadcasted_iota(jnp.int32, (TILE, CHUNK), 1)

    def q_tile(t, carry):
        q = act_ref[rows_at(t), Q]

        def k_chunk(c, acc):
            mask = from_start(t, lo_ref, c * CHUNK - SPAN, col, 1)
            return acc + weigh(q, kt_ref[:, chunk_at(c)], kv_ref[chunk_at(c), :HD], mask)

        start = (lo_ref[2 * t] + SPAN) // CHUNK
        acc = lax.fori_loop(start, CHUNKS, k_chunk, jnp.zeros((TILE, HD), F32))
        attn_s[rows_at(t), :] += jnp.where(valid_rows(t, nv_ref), acc, 0.0)
        return carry

    lax.fori_loop(0, far_tiles(lo_ref), q_tile, 0)
    ones = jnp.ones((8, HD), BF16)
    for t in range(TILES):
        rows = slice(t * TILE, (t + 1) * TILE)
        attn = attn_s[rows, :] * (SCALE / SPAN)
        out_ref[rows, :] = attn.astype(BF16)
        d_n = dg_s[rows, :].astype(F32) * act_ref[rows, U].astype(F32)
        square = lax.dot_general(ones, (attn * attn).astype(BF16), NT, preferred_element_type=F32)
        cross = lax.dot_general(ones, (attn * d_n).astype(BF16), NT, preferred_element_type=F32)
        sum_s[t : t + 1, :] = square[:1]
        sum_s[TILES + t : TILES + t + 1, :] = cross[:1]
    sums = sum_s[...]
    high = sums.astype(BF16)
    low = (sums - high.astype(F32)).astype(BF16)
    sums = jnp.concatenate([high[:, :HD], high[:, HD:], low[:, :HD], low[:, HD:]], axis=0)
    for mask in range(HEADS):
        pieces[mask][:TILE, :] = out_ref[rows_at(head ^ mask), :]
        pieces[mask][TILE:, :] = sums


def far_tiles(lo_ref):
    return sum((lo_ref[2 * t] < 0).astype(jnp.int32) for t in range(TILES))


def row_scales(sum_refs):
    width = HEADS * HD
    total = 0.0
    for ref in sum_refs:
        total += ref[TILE:, :].astype(F32)
    n = 2 * TILES
    total = jnp.concatenate([total[:n] + total[2 * n : 3 * n], total[n : 2 * n] + total[3 * n :]], axis=1)
    r = lax.rsqrt(total[:TILES] * (1.0 / width) + eps)
    c = total[TILES:] * (1.0 / width) * r
    return jnp.concatenate([r, c], axis=0).T


def cotangent(t, scales, nv_ref, u, attn, d_gated):
    r, c = scales[:, t : t + 1], scales[:, TILES + t : TILES + t + 1]
    n = attn.astype(F32) * r
    g = r * (d_gated * u.astype(F32) - n * c)
    return n, jnp.where(valid_rows(t, nv_ref), g, 0.0).astype(BF16)


def back_scores(qt, k, v, gt, mask):
    s = jnp.dot(k, qt, preferred_element_type=F32)
    sig = jnp.where(mask, sigmoid(s), 0.0)
    dw = jnp.dot(v, gt, preferred_element_type=F32)
    ds = dw * sig * (1.0 + (s * SCALE) * (1.0 - sig))
    return (s * sig).astype(BF16), ds.astype(BF16)


def cotangent_kernel(nv_ref, at_ref, act_ref, slope_ref, attn_ref, *refs):
    sum_refs, dg_refs, (g_ref, cols_ref, dg_s) = refs[:HEADS], refs[HEADS : 2 * HEADS], refs[-3:]
    for mask in range(HEADS):
        dg_s[rows_at(at_ref[1] ^ mask), :] = dg_refs[mask][...]
    scales = row_scales(sum_refs)
    for t in range(TILES):
        rows = slice(t * TILE, (t + 1) * TILE)
        d_gated = dg_s[rows, :].astype(F32)
        n, g = cotangent(t, scales, nv_ref, act_ref[rows, U], attn_ref[rows, :], d_gated)
        g_ref[rows, :] = g
        du = (d_gated * n).astype(BF16).astype(F32)
        cols_ref[:, rows] = (du * slope_ref[rows, U].astype(F32)).astype(BF16).T


def queries_kernel(lo_ref, act_ref, slope_qt_ref, qt_ref, kt_ref, g_ref, kv_ref, far_kt_ref, cols_ref, rows_ref, dkv_ref, gt_s):
    for t in range(TILES):
        rows = slice(t * TILE, (t + 1) * TILE)
        gt_s[:, rows] = g_ref[rows, :].T
    for c in range(CHUNKS):
        dkv_ref[c * CHUNK : (c + 1) * CHUNK, :] = jnp.zeros((CHUNK, 2 * HD), F32)
    key = lax.broadcasted_iota(jnp.int32, (CHUNK, TILE), 0)
    query = lax.broadcasted_iota(jnp.int32, (CHUNK, TILE), 1)

    def q_tile(t, carry):
        q, qt = act_ref[rows_at(t), Q], qt_ref[:, rows_at(t)]
        g, gt = g_ref[rows_at(t), :], gt_s[:, rows_at(t)]

        def far_chunk(c, dqt):
            at = chunk_at(c)
            mask = from_start(t, lo_ref, c * CHUNK - SPAN, key, 0)
            ds = back_scores(qt, kv_ref[at, HD:], kv_ref[at, :HD], gt, mask)[1]
            return dqt + jnp.dot(far_kt_ref[:, at], ds, preferred_element_type=F32)

        def k_chunk(c, dqt):
            at = chunk_at(c)
            mask = from_start(t, lo_ref, c * CHUNK, key, 0) & (key - query <= t * TILE - c * CHUNK)
            w, ds = back_scores(qt, act_ref[at, K], act_ref[at, V], gt, mask)
            dkv_ref[at, :HD] += jnp.dot(w, g, preferred_element_type=F32)
            dkv_ref[at, HD:] += jnp.dot(ds, q, preferred_element_type=F32)
            return dqt + jnp.dot(kt_ref[:, at], ds, preferred_element_type=F32)

        first = lo_ref[2 * t]
        start = jnp.minimum(first + SPAN, SPAN) // CHUNK
        dqt = lax.fori_loop(start, CHUNKS, far_chunk, jnp.zeros((HD, TILE), F32))
        dqt = lax.fori_loop(jnp.maximum(first, 0) // CHUNK, t // 2 + 1, k_chunk, dqt)
        dq = (dqt * (SCALE / SPAN)).astype(BF16).astype(F32)
        dq = (dq * slope_qt_ref[:, rows_at(t)].astype(F32)).astype(BF16)
        cols_ref[:, rows_at(t)] = dq
        rows_ref[rows_at(t), :] = dq.T
        return carry

    lax.fori_loop(0, TILES, q_tile, 0)


def halving(groups):
    return [0] if groups == 1 else [2 * i for i in halving(groups // 2)] + [2 * i + 1 for i in halving(groups // 2)]


def keys_kernel(
    groups, lo_ref, at_ref, own_ref, act_ref, slope_ref, q_ref, g_ref, u_cols_ref, q_cols_ref, dq_ref, normed_ref, *refs
):
    own_piece, other, pairs, (keep, send, cols_s, all_s, acc_s) = refs[0], refs[1], refs[2:5], refs[5:]
    first = jnp.minimum(lo_ref[2 * TILES], SPAN) // CHUNK
    key = lax.broadcasted_iota(jnp.int32, (CHUNK, TILE), 0)

    def clear(c, carry):
        acc_s[chunk_at(c), :] = jnp.zeros((CHUNK, 2 * HD), F32)
        return carry

    lax.fori_loop(first, CHUNKS, clear, 0)

    def q_tile(t, carry):
        q, g = q_ref[rows_at(t), :], g_ref[rows_at(t), :]
        qt, gt = q.T, g.T

        def k_chunk(c, carry):
            at = chunk_at(c)
            mask = from_start(TILES + t, lo_ref, c * CHUNK, key, 0)
            w, ds = back_scores(qt, act_ref[at, K], act_ref[at, V], gt, mask)
            acc_s[at, :HD] += jnp.dot(w, g, preferred_element_type=F32)
            acc_s[at, HD:] += jnp.dot(ds, q, preferred_element_type=F32)
            return carry

        return lax.fori_loop(lo_ref[2 * (TILES + t)] // CHUNK, CHUNKS, k_chunk, carry)

    count = sum((lo_ref[2 * (TILES + t)] < SPAN).astype(jnp.int32) for t in range(TILES))
    lax.fori_loop(0, count, q_tile, 0)
    places = {0: (own_piece, 0)}
    for i in range(4):
        places[2 * i + 1] = other, i * TILE
    for i in range(3):
        places[2 * i + 2] = pairs[i], 0
    for mask in range(HEADS):
        t = at_ref[1] ^ mask
        rows = rows_at(t)
        d = own_ref[rows, :] + jnp.where(t // 2 >= first, acc_s[rows, :], 0.0)
        d = (d * (SCALE / SPAN)).astype(BF16).astype(F32)
        d = (d * slope_ref[rows, VK].astype(F32)).astype(BF16)
        ref, at = places[mask]
        ref[at : at + TILE, :HD] = dq_ref[rows, :]
        ref[at : at + TILE, HD:] = d
        cols_s[:, rows] = d.T
    share = jnp.dot(cols_s[...], normed_ref[...], preferred_element_type=F32).astype(BF16)
    all_s[HD : 2 * HD, :], all_s[3 * HD :, :] = share[:HD], share[HD:]
    all_s[:HD, :] = jnp.dot(u_cols_ref[...], normed_ref[...], preferred_element_type=F32).astype(BF16)
    all_s[2 * HD : 3 * HD, :] = jnp.dot(q_cols_ref[...], normed_ref[...], preferred_element_type=F32).astype(BF16)
    size = 4 * HD // groups
    for i, mask in enumerate(halving(groups)):
        at = pl.multiple_of((at_ref[0] ^ mask) * size, size)
        part = all_s[pl.ds(at, size), :]
        if i < groups // 2:
            keep[i * size : (i + 1) * size, :] = part.astype(F32)
        else:
            send[(i - groups // 2) * size : (i + 1 - groups // 2) * size, :] = part


def merge_kernel(other_ref, *refs):
    for i, ref in enumerate(refs[-3:]):
        ref[TILE:, :] = other_ref[(i + 1) * TILE : (i + 2) * TILE, :]


def assemble(at_ref, refs, cols, out_s):
    for mask in range(HEADS):
        out_s[:, lanes_at(at_ref[1] ^ mask)] = refs[mask][:TILE, cols]
    return out_s[...]


def through(x, w_ref, branch):
    width = w_ref.shape[0]
    return lax.dot_general(x, w_ref[:, branch * width : (branch + 1) * width], NT, preferred_element_type=F32)


def rows_kernel(at_ref, *refs):
    attn_refs, dg_refs = refs[:HEADS], refs[HEADS : 2 * HEADS]
    tokens_ref, w_out_ref, w_in_ref, out_ref, dn_ref, row_s = refs[2 * HEADS :]
    width = w_out_ref.shape[0]
    x = tokens_ref[...].astype(F32)
    u, slope = silu_and_slope(jnp.dot(norm_rows(x).astype(BF16), w_in_ref[:, :width], preferred_element_type=F32))
    n = norm_rows(assemble(at_ref, attn_refs, slice(None), row_s).astype(F32))
    gated = (n * u.astype(F32)).astype(BF16)
    y = jnp.dot(gated, w_out_ref[...], preferred_element_type=F32)
    out_ref[...] = (x + y).astype(BF16)
    du = (assemble(at_ref, dg_refs, slice(None), row_s).astype(F32) * n).astype(BF16).astype(F32)
    du = (du * slope.astype(F32)).astype(BF16)
    dn_ref[...] = through(du, w_in_ref, 0)


def half_kernel(keep_ref, got_ref, *refs):
    half = keep_ref.shape[0] // len(refs)
    refs[0][...] = keep_ref[:half, :] + got_ref[:half, :].astype(F32)
    if len(refs) > 1:
        refs[1][...] = (keep_ref[half:, :] + got_ref[half:, :].astype(F32)).astype(BF16)


def last_kernel(at_ref, own_ref, other_ref, *refs):
    pairs, (dn_ref, tokens_ref, grad_ref, w_in_ref, after_ref, out_ref, row_s) = refs[:3], refs[3:]
    pieces = [(own_ref, 0), (other_ref, 0)] + [(ref, at) for ref in pairs for at in (0, TILE)]
    dn = dn_ref[...]
    for i, branch in enumerate((2, 1, 3)):
        for mask, (ref, at) in enumerate(pieces):
            row_s[:, lanes_at(at_ref[1] ^ mask)] = ref[at : at + TILE, i * HD : (i + 1) * HD]
        dn += through(row_s[...], w_in_ref, branch)
    x = tokens_ref[...].astype(F32)
    r = lax.rsqrt(jnp.mean(x * x, axis=-1, keepdims=True) + eps)
    n = x * r
    dx = r * (dn - n * jnp.mean(dn * n, axis=-1, keepdims=True))
    out_ref[...] = (grad_ref[...].astype(F32) + dx).astype(BF16)


def call(kernel, scalars, arrays, outs, scratch=(), after=(), aliases=None, limit=16, sems=0):
    smem = pl.BlockSpec(memory_space=pltpu.SMEM)
    vmem = pl.BlockSpec(memory_space=pltpu.VMEM)
    anywhere = pl.BlockSpec(memory_space=pl.ANY)
    return pl.pallas_call(
        kernel,
        out_shape=[jax.ShapeDtypeStruct(*out) for out in outs],
        in_specs=[smem] * len(scalars) + [vmem] * len(arrays) + [anywhere] * len(after),
        out_specs=[smem if out[1] == jnp.int32 else vmem for out in outs],
        scratch_shapes=[pltpu.VMEM(*shape) for shape in scratch] + ([pltpu.SemaphoreType.DMA((sems,))] if sems else []),
        input_output_aliases=aliases or {},
        compiler_params=pltpu.CompilerParams(vmem_limit_bytes=limit * 2**20),
        cost_estimate=pl.CostEstimate(flops=0, bytes_accessed=0, transcendentals=0),
    )(*scalars, *arrays, *after)


def per_device(groups, tokens, w_in, w_out, block_counts, tails, grad_out):
    count, width = tokens.shape
    own, tall, wide, tall_t = (count, width), (SPAN, HD), (SPAN, 2 * HD), (HD, SPAN)
    piece, half, sums_shape = (count, HD), (BLK, width), (2 * TILES, TILE)

    def swap(x, mask):
        return lax.ppermute(x, "h", [(i, i ^ mask) for i in range(HEADS)])

    def trade(pieces):
        return [pieces[0]] + [swap(pieces[mask], mask) for mask in range(1, HEADS)]

    def onward(x):
        return lax.ppermute(x, "g", [(i, i + 1) for i in range(groups - 1)])

    def backward(x):
        return lax.ppermute(x, "g", [(i + 1, i) for i in range(groups - 1)])

    x_rows, y_rows = swap(tokens, 2), swap(tokens, 4)
    *kept, kv, w_head = call(
        first_kernel,
        (),
        (swap(tokens, 1),),
        proj_outs(width, 2) + [((width, 4 * HD), BF16)],
        [(own, BF16)],
        (tokens, w_in),
        limit=48,
        sems=5,
    )
    far_kv = [onward(kv)]
    dg_own = call(d_gated_kernel, (), (grad_out, w_out), [(piece, BF16)] * HEADS, [(own, BF16)], (kv,))
    d_gated = trade(dg_own)
    info = call(info_kernel, (block_counts, tails), (), [((2 * MAXB,), jnp.int32)] * 2 + [((2,), jnp.int32)])
    x_rows, y_rows, x_half, y_half = call(
        cut_kernel,
        (),
        (x_rows, y_rows),
        [(own, BF16), (own, BF16), (half, BF16), (half, BF16)],
        after=(far_kv[0], *d_gated[1:5]),
        aliases={0: 0, 1: 1},
        limit=4,
    )
    corner = swap(x_half, 4), swap(y_half, 2)
    chunks = ((x_rows,), (swap(x_rows, 1),), (y_rows,), (swap(y_rows, 1),))
    *kept, kv = project(info, (2, 3, 4, 5), chunks, w_head, kept)
    far_kv.append(onward(kv))
    corner = call(gate_kernel, (), (), [(half, BF16), (half, BF16)], after=(*corner, kv, *d_gated[5:]), aliases={0: 0, 1: 1}, limit=4)
    *kept, kv, q = project(info, (6, 7), (corner, [swap(x, 1) for x in corner]), w_head, kept, True)
    far_kv.append(onward(kv))
    q_next = backward(q)
    normed, act, slope = kept

    near, kt, qt, slope_qt = call(fwd_own_kernel, info[:2], (act, slope), [(tall, F32)] + [(tall_t, BF16)] * 3)
    attn, kv, far_kt, *sums = call(
        fwd_far_kernel,
        info,
        (act, *far_kv, near, *d_gated),
        [(tall, BF16), (wide, BF16), (tall_t, BF16)] + [((count + 8 * TILES, HD), BF16)] * HEADS,
        [(sums_shape, F32), (tall, F32), (tall, BF16)],
    )
    sums = trade(sums)

    g, u_cols = call(
        cotangent_kernel,
        info[1:],
        (act, slope, attn, *sums, *d_gated),
        [(tall, BF16), (tall_t, BF16)],
        [(tall, BF16)],
        (q_next,),
    )
    g_next = backward(g)
    q_cols, d_q, dkv = call(
        queries_kernel,
        info[:1],
        (act, slope_qt, qt, kt, g, kv, far_kt),
        [(tall_t, BF16), (tall, BF16), (wide, F32)],
        [(tall_t, BF16)],
    )
    rows, cols = 4 * HD // groups, 3 * HD
    half_rows = rows * groups // 2
    mine, other, *pairs, keep, send = call(
        functools.partial(keys_kernel, groups),
        (info[0], info[2]),
        (dkv, act, slope, q_next, g_next, u_cols, q_cols, d_q, normed),
        [((count, cols), BF16), ((4 * count, cols), BF16)]
        + [((2 * count, cols), BF16)] * 3
        + [((half_rows, width), F32), ((half_rows, width), BF16)],
        [((2 * HD, SPAN), BF16), ((4 * HD, width), BF16), (wide, F32)],
    )
    other = swap(other, 1)
    pairs = call(
        merge_kernel, (), (other,), [((2 * count, cols), BF16)] * 3, after=pairs, aliases={1: 0, 2: 1, 3: 2}, limit=4
    )
    pairs = [swap(x, mask) for x, mask in zip(pairs, (2, 4, 6))]
    layer_out, d_normed = call(
        rows_kernel,
        (info[2],),
        (*sums, *dg_own, tokens, w_out, w_in),
        [(own, BF16), (own, F32)],
        [(own, BF16)],
    )
    mask = 1
    while mask < groups:
        send = lax.ppermute(send, "g", [(i, i ^ mask) for i in range(groups)])
        mask, half_rows = 2 * mask, half_rows // 2
        outs = [((half_rows, width), F32), ((half_rows, width), BF16)] if mask < groups else [((rows, width), F32)]
        keep, *send = call(half_kernel, (), (keep, send), outs)
        send = send[0] if send else None
    grad_w_in = keep
    grad_tokens = call(
        last_kernel,
        (info[2],),
        (mine, other, *pairs, d_normed, tokens, grad_out, w_in),
        [(own, BF16)],
        [(own, BF16)],
        (grad_w_in,),
    )[0]
    parts = groups // 4
    if parts > 1:
        perm = [
            (i * HEADS + j, ((i // parts) * HEADS + j) * parts + i % parts)
            for i in range(groups)
            for j in range(HEADS)
        ]
        grad_w_in = lax.ppermute(grad_w_in, ("g", "h"), perm)
    return (layer_out, grad_tokens, grad_w_in)


def solution(mesh):
    groups = mesh.shape["seq"] // HEADS
    split = Mesh(mesh.devices.reshape(groups, HEADS), ("g", "h"))
    rows = P(("g", "h"), None)
    return jax.shard_map(
        functools.partial(per_device, groups),
        mesh=split,
        in_specs=(rows, P(), P(), P(), P(), rows),
        out_specs=(rows, rows, rows),
        check_vma=False,
    )
```

```python
import functools

import jax
import jax.numpy as jnp
from jax import lax
from jax.experimental import pallas as pl
from jax.experimental.pallas import tpu as pltpu
from jax.sharding import Mesh, PartitionSpec as P

HEADS = 8
HD = 128
BLK = 128
MAXB = 16
SPAN = MAXB * BLK
TILE = 256
TILES = SPAN // TILE
CHUNK = 512
CHUNKS = SPAN // CHUNK
SCALE = HD ** (-0.5)
LOG2E = 1.4426950408889634

eps = 1e-05

NT = (((1,), (1,)), ((), ()))
F32, BF16 = jnp.float32, jnp.bfloat16

U, Q, V, K = (slice(i * HD, (i + 1) * HD) for i in range(4))
PLACE = (0, 2, 1, 3)
UQ, VK = slice(0, 2 * HD), slice(2 * HD, 4 * HD)


def start_kernel(counts_ref, tails_ref, w_ref, lo_ref, nv_ref, at_ref, wh_ref, sems):
    group = lax.axis_index("g").astype(jnp.int32)
    at_ref[0] = group
    head = lax.axis_index("h").astype(jnp.int32)
    at_ref[1] = head
    copies = []
    for i in range(4):
        source = w_ref.at[:, lanes_at(PLACE[i] * (w_ref.shape[0] // HD) + head)]
        copies.append(pltpu.make_async_copy(source, wh_ref.at[:, i * HD : (i + 1) * HD], sems.at[i]))
        copies[i].start()
    base = group * MAXB
    for j in range(2 * MAXB):
        lo_ref[j] = j * BLK
        nv_ref[j] = BLK

    def user(n, start):
        end = start + counts_ref[n]

        def block(j, carry):
            lo_ref[j] = (start - base) * BLK
            nv_ref[j] = jnp.where(j == end - 1 - base, tails_ref[n], BLK)
            return carry

        lax.fori_loop(jnp.maximum(start - base, 0), jnp.minimum(end - base, 2 * MAXB), block, 0)
        return end

    lax.fori_loop(0, counts_ref.shape[0], user, jnp.int32(0))
    for copy in copies:
        copy.wait()


def by_half(t, ref, shape, dim):
    side = lax.broadcasted_iota(jnp.int32, shape, dim)
    return jnp.where(side < BLK, ref[2 * t], ref[2 * t + 1])


def from_start(t, lo_ref, at, keys, dim):
    parts = [part >= lo_ref[2 * t + i] - at for i, part in enumerate(jnp.split(keys, 2, axis=1 - dim))]
    return jnp.concatenate(parts, axis=1 - dim)


def valid_rows(t, nv_ref):
    row = lax.broadcasted_iota(jnp.int32, (TILE, 1), 0)
    return (row & (BLK - 1)) < by_half(t, nv_ref, (TILE, 1), 0)


def rows_at(t):
    return pl.ds(pl.multiple_of(t * TILE, TILE), TILE)


def chunk_at(c):
    return pl.ds(pl.multiple_of(c * CHUNK, CHUNK), CHUNK)


def lanes_at(i):
    return pl.ds(pl.multiple_of(i * HD, HD), HD)


def norm_rows(x):
    return x * lax.rsqrt(jnp.mean(x * x, axis=-1, keepdims=True) + eps)


def silu_and_slope(pre):
    s = 0.5 + 0.5 * jnp.tanh(0.5 * pre)
    return (pre * s).astype(BF16), (s * (1.0 + pre * (1.0 - s))).astype(BF16)


def store_rows(x, place, wh_ref, normed_ref, act_ref, slope_ref, kv_ref, i):
    rows = rows_at(place)
    xn = norm_rows(x.astype(F32)).astype(BF16)
    normed_ref[rows, :] = xn
    act, slope = silu_and_slope(jnp.dot(xn, wh_ref[...], preferred_element_type=F32))
    act_ref[rows, :] = act
    slope_ref[rows, :] = slope
    kv_ref[i * TILE : (i + 1) * TILE, :] = act[:, VK]


def proj_kernel(masks, pieces, last, at_ref, *refs):
    x_refs, wh_ref = refs[: sum(pieces)], refs[sum(pieces)]
    outs = refs[-5:-1] if last else refs[-4:]
    for i, mask in enumerate(masks):
        parts = [ref[...] for ref in x_refs[sum(pieces[:i]) : sum(pieces[: i + 1])]]
        x = parts[0] if len(parts) == 1 else jnp.concatenate(parts, axis=0)
        store_rows(x, at_ref[1] ^ mask, wh_ref, *outs, i)
    if last:
        refs[-1][...] = outs[1][:, Q]


def proj_outs(width, n):
    return [((SPAN, width), BF16), ((SPAN, 4 * HD), BF16), ((SPAN, 4 * HD), BF16), ((n * TILE, 2 * HD), BF16)]


def project(info, masks, chunks, w, kept, last=False):
    pieces = tuple(len(chunk) for chunk in chunks)
    flat = [piece for chunk in chunks for piece in chunk]
    start = 2 + len(flat)
    return call(
        functools.partial(proj_kernel, masks, pieces, last),
        (info[2],),
        (*flat, w),
        proj_outs(w.shape[0], len(masks)) + ([((SPAN, HD), BF16)] if last else []),
        after=kept,
        aliases={start + i: i for i in range(len(kept))},
    )


def cut_kernel(x_ref, y_ref, *refs):
    x_half, y_half = refs[-2:]
    x_half[...] = x_ref[:BLK, :]
    y_half[...] = y_ref[BLK:, :]


def gate_kernel(*refs):
    pass


def merge_kernel(other_ref, *refs):
    for i, ref in enumerate(refs[-3:]):
        ref[TILE:, :] = other_ref[(i + 1) * TILE : (i + 2) * TILE, :]


def places(refs):
    mine, other, *pairs = refs
    return [(mine, 0), (other, 0)] + [(ref, at) for ref in pairs for at in (0, TILE)]


def outgoing(refs):
    mine, other, *pairs = refs
    found = [(mine, 0)] * HEADS
    for i in range(4):
        found[2 * i + 1] = other, i * TILE
    for i in range(3):
        found[2 * i + 2] = pairs[i], 0
    return found


def trade_outs(cols):
    return [((TILE, cols), BF16), ((4 * TILE, cols), BF16)] + [((2 * TILE, cols), BF16)] * 3


def d_gated_kernel(at_ref, g_ref, w_ref, *refs):
    pieces, d_ref = refs[-6:-1], refs[-1]
    d_ref[...] = lax.dot_general(g_ref[...], w_ref[...], NT, preferred_element_type=F32).astype(BF16)
    for mask, (ref, at) in enumerate(outgoing(pieces)):
        ref[at : at + TILE, :] = d_ref[:, lanes_at(at_ref[1] ^ mask)]


def sigmoid(s):
    return pl.reciprocal(1.0 + jnp.exp2(s * (-SCALE * LOG2E)), approx=True)


def weigh(q, kt, v, mask):
    s = jnp.dot(q, kt, preferred_element_type=F32)
    w = jnp.where(mask, s * sigmoid(s), 0.0).astype(BF16)
    return jnp.dot(w, v, preferred_element_type=F32)


def fwd_own_kernel(lo_ref, nv_ref, act_ref, slope_ref, out_ref, kt_ref, qt_ref, slope_qt_ref):
    for t in range(TILES):
        rows = slice(t * TILE, (t + 1) * TILE)
        kt_ref[:, rows] = act_ref[rows, K].T
    row = lax.broadcasted_iota(jnp.int32, (TILE, CHUNK), 0)
    col = lax.broadcasted_iota(jnp.int32, (TILE, CHUNK), 1)

    def q_tile(t, carry):
        q = act_ref[rows_at(t), Q]

        def k_chunk(c, acc):
            mask = from_start(t, lo_ref, c * CHUNK, col, 1) & (col - row <= t * TILE - c * CHUNK)
            return acc + weigh(q, kt_ref[:, chunk_at(c)], act_ref[chunk_at(c), V], mask)

        first = jnp.maximum(lo_ref[2 * t], 0) // CHUNK
        acc = lax.fori_loop(first, t // 2 + 1, k_chunk, jnp.zeros((TILE, HD), F32))
        out_ref[rows_at(t), :] = jnp.where(valid_rows(t, nv_ref), acc, 0.0)
        return carry

    lax.fori_loop(0, TILES, q_tile, 0)
    for t in range(TILES):
        rows = slice(t * TILE, (t + 1) * TILE)
        qt_ref[:, rows] = act_ref[rows, Q].T
        slope_qt_ref[:, rows] = slope_ref[rows, Q].T


def fwd_far_kernel(
    lo_ref, nv_ref, at_ref, act_ref, kva_ref, kvb_ref, kvc_ref, near_ref, *refs,
):
    dg_refs, (out_ref, kv_ref, kt_ref, sum_ref), pieces, (attn_s, dg_s) = refs[:5], refs[5:9], refs[9:14], refs[14:]
    head = at_ref[1]
    slot = 0
    for ref in (kva_ref, kvb_ref, kvc_ref):
        for at in range(0, ref.shape[0], TILE):
            kv_ref[rows_at(slot ^ head), :] = ref[at : at + TILE, :]
            slot += 1
    for mask, (ref, at) in enumerate(places(dg_refs)):
        dg_s[rows_at(head ^ mask), :] = ref[at : at + TILE, :]
    first = jnp.minimum(lo_ref[0] + SPAN, SPAN) // CHUNK
    for t in range(TILES):
        rows = slice(t * TILE, (t + 1) * TILE)

        @pl.when(t // 2 >= first)
        def _():
            kt_ref[:, rows] = kv_ref[rows, HD:].T

    attn_s[...] = near_ref[...]
    col = lax.broadcasted_iota(jnp.int32, (TILE, CHUNK), 1)

    def q_tile(t, carry):
        q = act_ref[rows_at(t), Q]

        def k_chunk(c, acc):
            mask = from_start(t, lo_ref, c * CHUNK - SPAN, col, 1)
            return acc + weigh(q, kt_ref[:, chunk_at(c)], kv_ref[chunk_at(c), :HD], mask)

        start = (lo_ref[2 * t] + SPAN) // CHUNK
        acc = lax.fori_loop(start, CHUNKS, k_chunk, jnp.zeros((TILE, HD), F32))
        attn_s[rows_at(t), :] += jnp.where(valid_rows(t, nv_ref), acc, 0.0)
        return carry

    lax.fori_loop(0, far_tiles(lo_ref), q_tile, 0)
    ones = jnp.ones((8, HD), BF16)
    for t in range(TILES):
        rows = slice(t * TILE, (t + 1) * TILE)
        attn = attn_s[rows, :] * (SCALE / SPAN)
        out_ref[rows, :] = attn.astype(BF16)
        d_n = dg_s[rows, :].astype(F32) * act_ref[rows, U].astype(F32)
        square = lax.dot_general(ones, (attn * attn).astype(BF16), NT, preferred_element_type=F32)
        cross = lax.dot_general(ones, (attn * d_n).astype(BF16), NT, preferred_element_type=F32)
        sum_ref[t : t + 1, :] = square[:1]
        sum_ref[TILES + t : TILES + t + 1, :] = cross[:1]
    for mask, (ref, at) in enumerate(outgoing(pieces)):
        ref[at : at + TILE, :] = out_ref[rows_at(head ^ mask), :]


def add_kernel(a_ref, b_ref, out_ref):
    out_ref[...] = a_ref[...] + b_ref[...]


def far_tiles(lo_ref):
    return sum((lo_ref[2 * t] < 0).astype(jnp.int32) for t in range(TILES))


def row_scales(sum_refs):
    width = HEADS * HD
    total = sum_refs[0][...]
    for ref in sum_refs[1:]:
        total += ref[...]
    r = lax.rsqrt(total[:TILES] * (1.0 / width) + eps)
    c = total[TILES:] * (1.0 / width) * r
    return jnp.concatenate([r, c], axis=0).T


def cotangent(t, scales, nv_ref, u, attn, d_gated):
    r, c = scales[:, t : t + 1], scales[:, TILES + t : TILES + t + 1]
    n = attn.astype(F32) * r
    g = r * (d_gated * u.astype(F32) - n * c)
    return n, jnp.where(valid_rows(t, nv_ref), g, 0.0).astype(BF16)


def back_scores(qt, k, v, gt, mask):
    s = jnp.dot(k, qt, preferred_element_type=F32)
    sig = jnp.where(mask, sigmoid(s), 0.0)
    dw = jnp.dot(v, gt, preferred_element_type=F32)
    ds = dw * sig * (1.0 + (s * SCALE) * (1.0 - sig))
    return (s * sig).astype(BF16), ds.astype(BF16)


def cotangent_kernel(nv_ref, at_ref, act_ref, slope_ref, attn_ref, *refs):
    sum_refs, dg_refs, (g_ref, cols_ref, dg_s) = refs[:4], refs[4:9], refs[-3:]
    for mask, (ref, at) in enumerate(places(dg_refs)):
        dg_s[rows_at(at_ref[1] ^ mask), :] = ref[at : at + TILE, :]
    scales = row_scales(sum_refs)
    for t in range(TILES):
        rows = slice(t * TILE, (t + 1) * TILE)
        d_gated = dg_s[rows, :].astype(F32)
        n, g = cotangent(t, scales, nv_ref, act_ref[rows, U], attn_ref[rows, :], d_gated)
        g_ref[rows, :] = g
        du = (d_gated * n).astype(BF16).astype(F32)
        cols_ref[:, rows] = (du * slope_ref[rows, U].astype(F32)).astype(BF16).T


def queries_kernel(lo_ref, act_ref, slope_qt_ref, qt_ref, kt_ref, g_ref, kv_ref, far_kt_ref, cols_ref, rows_ref, dkv_ref, gt_s):
    for t in range(TILES):
        rows = slice(t * TILE, (t + 1) * TILE)
        gt_s[:, rows] = g_ref[rows, :].T
    for c in range(CHUNKS):
        dkv_ref[c * CHUNK : (c + 1) * CHUNK, :] = jnp.zeros((CHUNK, 2 * HD), F32)
    key = lax.broadcasted_iota(jnp.int32, (CHUNK, TILE), 0)
    query = lax.broadcasted_iota(jnp.int32, (CHUNK, TILE), 1)

    def q_tile(t, carry):
        q, qt = act_ref[rows_at(t), Q], qt_ref[:, rows_at(t)]
        g, gt = g_ref[rows_at(t), :], gt_s[:, rows_at(t)]

        def far_chunk(c, dqt):
            at = chunk_at(c)
            mask = from_start(t, lo_ref, c * CHUNK - SPAN, key, 0)
            ds = back_scores(qt, kv_ref[at, HD:], kv_ref[at, :HD], gt, mask)[1]
            return dqt + jnp.dot(far_kt_ref[:, at], ds, preferred_element_type=F32)

        def k_chunk(c, dqt):
            at = chunk_at(c)
            mask = from_start(t, lo_ref, c * CHUNK, key, 0) & (key - query <= t * TILE - c * CHUNK)
            w, ds = back_scores(qt, act_ref[at, K], act_ref[at, V], gt, mask)
            dkv_ref[at, :HD] += jnp.dot(w, g, preferred_element_type=F32)
            dkv_ref[at, HD:] += jnp.dot(ds, q, preferred_element_type=F32)
            return dqt + jnp.dot(kt_ref[:, at], ds, preferred_element_type=F32)

        first = lo_ref[2 * t]
        start = jnp.minimum(first + SPAN, SPAN) // CHUNK
        dqt = lax.fori_loop(start, CHUNKS, far_chunk, jnp.zeros((HD, TILE), F32))
        dqt = lax.fori_loop(jnp.maximum(first, 0) // CHUNK, t // 2 + 1, k_chunk, dqt)
        dq = (dqt * (SCALE / SPAN)).astype(BF16).astype(F32)
        dq = (dq * slope_qt_ref[:, rows_at(t)].astype(F32)).astype(BF16)
        cols_ref[:, rows_at(t)] = dq
        rows_ref[rows_at(t), :] = dq.T
        return carry

    lax.fori_loop(0, TILES, q_tile, 0)


def halving(groups):
    return [0] if groups == 1 else [2 * i for i in halving(groups // 2)] + [2 * i + 1 for i in halving(groups // 2)]


def keys_kernel(
    groups, lo_ref, at_ref, own_ref, act_ref, slope_ref, q_ref, g_ref, u_cols_ref, q_cols_ref, dq_ref, normed_ref, *refs
):
    pieces, (keep, send, cols_s, all_s, acc_s) = refs[:5], refs[5:]
    first = jnp.minimum(lo_ref[2 * TILES], SPAN) // CHUNK
    key = lax.broadcasted_iota(jnp.int32, (CHUNK, TILE), 0)

    def clear(c, carry):
        acc_s[chunk_at(c), :] = jnp.zeros((CHUNK, 2 * HD), F32)
        return carry

    lax.fori_loop(first, CHUNKS, clear, 0)

    def q_tile(t, carry):
        q, g = q_ref[rows_at(t), :], g_ref[rows_at(t), :]
        qt, gt = q.T, g.T

        def k_chunk(c, carry):
            at = chunk_at(c)
            mask = from_start(TILES + t, lo_ref, c * CHUNK, key, 0)
            w, ds = back_scores(qt, act_ref[at, K], act_ref[at, V], gt, mask)
            acc_s[at, :HD] += jnp.dot(w, g, preferred_element_type=F32)
            acc_s[at, HD:] += jnp.dot(ds, q, preferred_element_type=F32)
            return carry

        return lax.fori_loop(lo_ref[2 * (TILES + t)] // CHUNK, CHUNKS, k_chunk, carry)

    count = sum((lo_ref[2 * (TILES + t)] < SPAN).astype(jnp.int32) for t in range(TILES))
    lax.fori_loop(0, count, q_tile, 0)
    for mask, (ref, at) in enumerate(outgoing(pieces)):
        t = at_ref[1] ^ mask
        rows = rows_at(t)
        d = own_ref[rows, :] + jnp.where(t // 2 >= first, acc_s[rows, :], 0.0)
        d = (d * (SCALE / SPAN)).astype(BF16).astype(F32)
        d = (d * slope_ref[rows, VK].astype(F32)).astype(BF16)
        ref[at : at + TILE, :HD] = dq_ref[rows, :]
        ref[at : at + TILE, HD:] = d
        cols_s[:, rows] = d.T
    share = jnp.dot(cols_s[...], normed_ref[...], preferred_element_type=F32).astype(BF16)
    all_s[HD : 2 * HD, :], all_s[3 * HD :, :] = share[:HD], share[HD:]
    all_s[:HD, :] = jnp.dot(u_cols_ref[...], normed_ref[...], preferred_element_type=F32).astype(BF16)
    all_s[2 * HD : 3 * HD, :] = jnp.dot(q_cols_ref[...], normed_ref[...], preferred_element_type=F32).astype(BF16)
    size = 4 * HD // groups
    for i, mask in enumerate(halving(groups)):
        at = pl.multiple_of((at_ref[0] ^ mask) * size, size)
        part = all_s[pl.ds(at, size), :]
        if i < groups // 2:
            keep[i * size : (i + 1) * size, :] = part.astype(F32)
        else:
            send[(i - groups // 2) * size : (i + 1 - groups // 2) * size, :] = part


def assemble(at_ref, refs, part, out_s):
    for mask, (ref, at) in enumerate(places(refs)):
        out_s[:, lanes_at(at_ref[1] ^ mask)] = ref[at : at + TILE, part * HD : (part + 1) * HD]
    return out_s[...]


def through(x, w_ref, branch):
    width = w_ref.shape[0]
    return lax.dot_general(x, w_ref[:, branch * width : (branch + 1) * width], NT, preferred_element_type=F32)


def rows_kernel(at_ref, *refs):
    attn_refs, (dg_ref, tokens_ref, w_out_ref, w_in_ref, out_ref, dn_ref, row_s) = refs[:5], refs[5:]
    width = w_out_ref.shape[0]
    x = tokens_ref[...].astype(F32)
    u, slope = silu_and_slope(jnp.dot(norm_rows(x).astype(BF16), w_in_ref[:, :width], preferred_element_type=F32))
    n = norm_rows(assemble(at_ref, attn_refs, 0, row_s).astype(F32))
    gated = (n * u.astype(F32)).astype(BF16)
    y = jnp.dot(gated, w_out_ref[...], preferred_element_type=F32)
    out_ref[...] = (x + y).astype(BF16)
    du = (dg_ref[...].astype(F32) * n).astype(BF16).astype(F32)
    du = (du * slope.astype(F32)).astype(BF16)
    dn_ref[...] = through(du, w_in_ref, 0)


def half_kernel(later, keep_ref, got_ref, *refs):
    refs = refs[later:]
    half = keep_ref.shape[0] // len(refs)
    refs[0][...] = keep_ref[:half, :] + got_ref[:half, :].astype(F32)
    if len(refs) > 1:
        refs[1][...] = (keep_ref[half:, :] + got_ref[half:, :].astype(F32)).astype(BF16)


def last_kernel(at_ref, *refs):
    pieces, (dn_ref, tokens_ref, grad_ref, w_in_ref, out_ref, end_ref, row_s) = refs[:5], refs[5:]
    end_ref[...] = jnp.zeros(end_ref.shape, F32)
    dn = dn_ref[...]
    for i, branch in enumerate((2, 1, 3)):
        dn += through(assemble(at_ref, pieces, i, row_s), w_in_ref, branch)
    x = tokens_ref[...].astype(F32)
    r = lax.rsqrt(jnp.mean(x * x, axis=-1, keepdims=True) + eps)
    n = x * r
    dx = r * (dn - n * jnp.mean(dn * n, axis=-1, keepdims=True))
    out_ref[...] = (grad_ref[...].astype(F32) + dx).astype(BF16)


def call(kernel, scalars, arrays, outs, scratch=(), after=(), aliases=None, limit=16, sems=0):
    smem = pl.BlockSpec(memory_space=pltpu.SMEM)
    vmem = pl.BlockSpec(memory_space=pltpu.VMEM)
    anywhere = pl.BlockSpec(memory_space=pl.ANY)
    return pl.pallas_call(
        kernel,
        out_shape=[jax.ShapeDtypeStruct(*out) for out in outs],
        in_specs=[smem] * len(scalars) + [vmem] * len(arrays) + [anywhere] * len(after),
        out_specs=[smem if out[1] == jnp.int32 else vmem for out in outs],
        scratch_shapes=[pltpu.VMEM(*shape) for shape in scratch] + ([pltpu.SemaphoreType.DMA((sems,))] if sems else []),
        input_output_aliases=aliases or {},
        compiler_params=pltpu.CompilerParams(vmem_limit_bytes=limit * 2**20),
        cost_estimate=pl.CostEstimate(flops=0, bytes_accessed=0, transcendentals=0),
    )(*scalars, *arrays, *after)


def per_device(groups, tokens, w_in, w_out, block_counts, tails, grad_out):
    count, width = tokens.shape
    own, tall, wide, tall_t = (count, width), (SPAN, HD), (SPAN, 2 * HD), (HD, SPAN)
    piece, half, sums_shape = (count, HD), (BLK, width), (2 * TILES, TILE)

    def swap(x, mask):
        return lax.ppermute(x, "h", [(i, i ^ mask) for i in range(HEADS)])

    def onward(x):
        return lax.ppermute(x, "g", [(i, i + 1) for i in range(groups - 1)])

    def backward(x):
        return lax.ppermute(x, "g", [(i + 1, i) for i in range(groups - 1)])

    def trade(pieces, after=(), merged=None):
        mine, other, *pairs = pieces
        other = swap(other, 1)
        pairs = call(
            merge_kernel,
            (),
            (other,),
            [(x.shape, BF16) for x in pairs],
            after=(*pairs, *after),
            aliases={1: 0, 2: 1, 3: 2},
            limit=4,
        )
        if merged is not None:
            merged.extend(pairs)
        return [mine, other] + [swap(x, mask) for x, mask in zip(pairs, (2, 4, 6))]

    x_rows, y_rows = swap(tokens, 2), swap(tokens, 4)
    other = swap(tokens, 1)
    *info, w_head = call(
        start_kernel,
        (block_counts, tails),
        (),
        [((2 * MAXB,), jnp.int32)] * 2 + [((2,), jnp.int32), ((width, 4 * HD), BF16)],
        after=(w_in,),
        limit=51,
        sems=4,
    )
    *kept, kv = project(info, (0, 1), ((tokens,), (other,)), w_head, ())
    far_kv = [onward(kv)]
    *dg_pieces, dg_own = call(
        d_gated_kernel, info[2:], (grad_out, w_out), trade_outs(HD) + [(own, BF16)], after=(kv,)
    )
    merged = []
    d_gated = trade(dg_pieces, merged=merged)
    x_rows, y_rows, x_half, y_half = call(
        cut_kernel,
        (),
        (x_rows, y_rows),
        [(own, BF16), (own, BF16), (half, BF16), (half, BF16)],
        after=(far_kv[0], merged[0]),
        aliases={0: 0, 1: 1},
        limit=4,
    )
    corner = swap(x_half, 4), swap(y_half, 2)
    chunks = ((x_rows,), (swap(x_rows, 1),), (y_rows,), (swap(y_rows, 1),))
    *kept, kv = project(info, (2, 3, 4, 5), chunks, w_head, kept)
    far_kv.append(onward(kv))
    corner = call(gate_kernel, (), (), [(half, BF16), (half, BF16)], after=(*corner, kv, *d_gated[2:]), aliases={0: 0, 1: 1}, limit=4)
    *kept, kv, q = project(info, (6, 7), (corner, [swap(x, 1) for x in corner]), w_head, kept, True)
    far_kv.append(onward(kv))
    q_next = backward(q)
    normed, act, slope = kept

    near, kt, qt, slope_qt = call(fwd_own_kernel, info[:2], (act, slope), [(tall, F32)] + [(tall_t, BF16)] * 3)
    attn, kv, far_kt, sums, *attn_pieces = call(
        fwd_far_kernel,
        info,
        (act, *far_kv, near, *d_gated),
        [(tall, BF16), (wide, BF16), (tall_t, BF16), (sums_shape, F32)] + trade_outs(HD),
        [(tall, F32), (tall, BF16)],
    )
    sums = call(add_kernel, (), (sums, swap(sums, 1)), [(sums_shape, F32)], limit=4)[0]
    sums = [sums] + [swap(sums, mask) for mask in (2, 4, 6)]

    g, u_cols = call(
        cotangent_kernel,
        info[1:],
        (act, slope, attn, *sums, *d_gated),
        [(tall, BF16), (tall_t, BF16)],
        [(tall, BF16)],
        (q_next,),
    )
    g_next = backward(g)
    q_cols, d_q, dkv = call(
        queries_kernel,
        info[:1],
        (act, slope_qt, qt, kt, g, kv, far_kt),
        [(tall_t, BF16), (tall, BF16), (wide, F32)],
        [(tall_t, BF16)],
    )
    rows, cols = 4 * HD // groups, 3 * HD
    half_rows = rows * groups // 2
    attn_rows = trade(attn_pieces, (d_q,))
    *pieces, keep, send = call(
        functools.partial(keys_kernel, groups),
        (info[0], info[2]),
        (dkv, act, slope, q_next, g_next, u_cols, q_cols, d_q, normed),
        trade_outs(cols) + [((half_rows, width), F32), ((half_rows, width), BF16)],
        [((2 * HD, SPAN), BF16), ((4 * HD, width), BF16), (wide, F32)],
    )
    pieces = trade(pieces)
    layer_out, d_normed = call(
        rows_kernel,
        info[2:],
        (*attn_rows, dg_own, tokens, w_out, w_in),
        [(own, BF16), (own, F32)],
        [(own, BF16)],
    )
    grad_tokens, end = call(
        last_kernel,
        info[2:],
        (*pieces, d_normed, tokens, grad_out, w_in),
        [(own, BF16), ((8, HD), F32)],
        [(own, BF16)],
    )
    mask = 1
    while mask < groups:
        send = lax.ppermute(send, "g", [(i, i ^ mask) for i in range(groups)])
        mask, half_rows = 2 * mask, half_rows // 2
        more = mask < groups
        outs = [((half_rows, width), F32), ((half_rows, width), BF16)] if more else [((rows, width), F32)]
        keep, *send = call(
            functools.partial(half_kernel, 0 if more else 1), (), (keep, send), outs, after=() if more else (end,)
        )
        send = send[0] if send else None
    grad_w_in = keep
    parts = groups // 4
    if parts > 1:
        perm = [
            (i * HEADS + j, ((i // parts) * HEADS + j) * parts + i % parts)
            for i in range(groups)
            for j in range(HEADS)
        ]
        grad_w_in = lax.ppermute(grad_w_in, ("g", "h"), perm)
    return (layer_out, grad_tokens, grad_w_in)


def solution(mesh):
    groups = mesh.shape["seq"] // HEADS
    split = Mesh(mesh.devices.reshape(groups, HEADS), ("g", "h"))
    rows = P(("g", "h"), None)
    return jax.shard_map(
        functools.partial(per_device, groups),
        mesh=split,
        in_specs=(rows, P(), P(), P(), P(), rows),
        out_specs=(rows, rows, rows),
        check_vma=False,
    )
```

```python
import functools

import jax
import jax.numpy as jnp
from jax import lax
from jax.experimental import pallas as pl
from jax.experimental.pallas import tpu as pltpu
from jax.sharding import Mesh, PartitionSpec as P

HEADS = 8
HD = 128
BLK = 128
MAXB = 16
SPAN = MAXB * BLK
TILE = 256
TILES = SPAN // TILE
CHUNK = 512
CHUNKS = SPAN // CHUNK
SCALE = HD ** (-0.5)
LOG2E = 1.4426950408889634

eps = 1e-05

NT = (((1,), (1,)), ((), ()))
F32, BF16 = jnp.float32, jnp.bfloat16

U, Q, V, K = (slice(i * HD, (i + 1) * HD) for i in range(4))
PLACE = (0, 2, 1, 3)
UQ, VK = slice(0, 2 * HD), slice(2 * HD, 4 * HD)


def start_kernel(counts_ref, tails_ref, w_ref, lo_ref, nv_ref, at_ref, wh_ref, sems):
    group = lax.axis_index("g").astype(jnp.int32)
    at_ref[0] = group
    head = lax.axis_index("h").astype(jnp.int32)
    at_ref[1] = head
    copies = []
    for i in range(4):
        source = w_ref.at[:, lanes_at(PLACE[i] * (w_ref.shape[0] // HD) + head)]
        copies.append(pltpu.make_async_copy(source, wh_ref.at[:, i * HD : (i + 1) * HD], sems.at[i]))
        copies[i].start()
    base = group * MAXB
    for j in range(2 * MAXB):
        lo_ref[j] = j * BLK
        nv_ref[j] = BLK

    def user(n, start):
        end = start + counts_ref[n]

        def block(j, carry):
            lo_ref[j] = (start - base) * BLK
            nv_ref[j] = jnp.where(j == end - 1 - base, tails_ref[n], BLK)
            return carry

        lax.fori_loop(jnp.maximum(start - base, 0), jnp.minimum(end - base, 2 * MAXB), block, 0)
        return end

    lax.fori_loop(0, counts_ref.shape[0], user, jnp.int32(0))
    for copy in copies:
        copy.wait()


def by_half(t, ref, shape, dim):
    side = lax.broadcasted_iota(jnp.int32, shape, dim)
    return jnp.where(side < BLK, ref[2 * t], ref[2 * t + 1])


def from_start(t, lo_ref, at, keys, dim):
    parts = [part >= lo_ref[2 * t + i] - at for i, part in enumerate(jnp.split(keys, 2, axis=1 - dim))]
    return jnp.concatenate(parts, axis=1 - dim)


def valid_rows(t, nv_ref):
    row = lax.broadcasted_iota(jnp.int32, (TILE, 1), 0)
    return (row & (BLK - 1)) < by_half(t, nv_ref, (TILE, 1), 0)


def rows_at(t):
    return pl.ds(pl.multiple_of(t * TILE, TILE), TILE)


def chunk_at(c):
    return pl.ds(pl.multiple_of(c * CHUNK, CHUNK), CHUNK)


def lanes_at(i):
    return pl.ds(pl.multiple_of(i * HD, HD), HD)


def norm_rows(x):
    return x * lax.rsqrt(jnp.mean(x * x, axis=-1, keepdims=True) + eps)


def silu_and_slope(pre):
    s = 0.5 + 0.5 * jnp.tanh(0.5 * pre)
    return (pre * s).astype(BF16), (s * (1.0 + pre * (1.0 - s))).astype(BF16)


def store_rows(x, place, wh_ref, normed_ref, act_ref, slope_ref, kv_ref, i):
    rows = rows_at(place)
    xn = norm_rows(x.astype(F32)).astype(BF16)
    normed_ref[rows, :] = xn
    act, slope = silu_and_slope(jnp.dot(xn, wh_ref[...], preferred_element_type=F32))
    act_ref[rows, :] = act
    slope_ref[rows, :] = slope
    kv_ref[i * TILE : (i + 1) * TILE, :] = act[:, VK]


def proj_kernel(masks, pieces, last, ahead, at_ref, *refs):
    x_refs, wh_ref = refs[: sum(pieces)], refs[sum(pieces)]
    outs = refs[-5:-1] if last else refs[-4:]
    if ahead:
        outs[3][: ahead * TILE, :] = refs[sum(pieces) + 1][...]
    for i, mask in enumerate(masks):
        parts = [ref[...] for ref in x_refs[sum(pieces[:i]) : sum(pieces[: i + 1])]]
        x = parts[0] if len(parts) == 1 else jnp.concatenate(parts, axis=0)
        store_rows(x, at_ref[1] ^ mask, wh_ref, *outs, ahead + i)
    if last:
        refs[-1][...] = outs[1][:, Q]


def proj_outs(width, n):
    return [((SPAN, width), BF16), ((SPAN, 4 * HD), BF16), ((SPAN, 4 * HD), BF16), ((n * TILE, 2 * HD), BF16)]


def project(info, masks, chunks, w, kept, last=False, kv=None):
    pieces = tuple(len(chunk) for chunk in chunks)
    flat = [piece for chunk in chunks for piece in chunk]
    lead = () if kv is None else (kv,)
    ahead = 0 if kv is None else kv.shape[0] // TILE
    start = 2 + len(flat) + len(lead)
    return call(
        functools.partial(proj_kernel, masks, pieces, last, ahead),
        (info[2],),
        (*flat, w, *lead),
        proj_outs(w.shape[0], ahead + len(masks)) + ([((SPAN, HD), BF16)] if last else []),
        after=kept,
        aliases={start + i: i for i in range(len(kept))},
    )


def cut_kernel(x_ref, y_ref, *refs):
    x_half, y_half = refs[-2:]
    x_half[...] = x_ref[:BLK, :]
    y_half[...] = y_ref[BLK:, :]


def gate_kernel(*refs):
    pass


def merge_kernel(other_ref, *refs):
    for i, ref in enumerate(refs[-3:]):
        ref[TILE:, :] = other_ref[(i + 1) * TILE : (i + 2) * TILE, :]


def places(refs):
    mine, other, *pairs = refs
    return [(mine, 0), (other, 0)] + [(ref, at) for ref in pairs for at in (0, TILE)]


def outgoing(refs):
    mine, other, *pairs = refs
    found = [(mine, 0)] * HEADS
    for i in range(4):
        found[2 * i + 1] = other, i * TILE
    for i in range(3):
        found[2 * i + 2] = pairs[i], 0
    return found


def trade_outs(cols):
    return [((TILE, cols), BF16), ((4 * TILE, cols), BF16)] + [((2 * TILE, cols), BF16)] * 3


def d_gated_kernel(at_ref, g_ref, w_ref, *refs):
    pieces, d_ref = refs[-6:-1], refs[-1]
    d_ref[...] = lax.dot_general(g_ref[...], w_ref[...], NT, preferred_element_type=F32).astype(BF16)
    for mask, (ref, at) in enumerate(outgoing(pieces)):
        ref[at : at + TILE, :] = d_ref[:, lanes_at(at_ref[1] ^ mask)]


def sigmoid(s):
    return pl.reciprocal(1.0 + jnp.exp2(s * (-SCALE * LOG2E)), approx=True)


def weigh(q, kt, v, mask):
    s = jnp.dot(q, kt, preferred_element_type=F32)
    w = jnp.where(mask, s * sigmoid(s), 0.0).astype(BF16)
    return jnp.dot(w, v, preferred_element_type=F32)


def fwd_own_kernel(lo_ref, nv_ref, act_ref, slope_ref, out_ref, kt_ref, qt_ref, slope_qt_ref):
    for t in range(TILES):
        rows = slice(t * TILE, (t + 1) * TILE)
        kt_ref[:, rows] = act_ref[rows, K].T
    row = lax.broadcasted_iota(jnp.int32, (TILE, CHUNK), 0)
    col = lax.broadcasted_iota(jnp.int32, (TILE, CHUNK), 1)

    def q_tile(t, carry):
        q = act_ref[rows_at(t), Q]

        def k_chunk(c, acc):
            mask = from_start(t, lo_ref, c * CHUNK, col, 1) & (col - row <= t * TILE - c * CHUNK)
            return acc + weigh(q, kt_ref[:, chunk_at(c)], act_ref[chunk_at(c), V], mask)

        first = jnp.maximum(lo_ref[2 * t], 0) // CHUNK
        acc = lax.fori_loop(first, t // 2 + 1, k_chunk, jnp.zeros((TILE, HD), F32))
        out_ref[rows_at(t), :] = jnp.where(valid_rows(t, nv_ref), acc, 0.0)
        return carry

    lax.fori_loop(0, TILES, q_tile, 0)
    for t in range(TILES):
        rows = slice(t * TILE, (t + 1) * TILE)
        qt_ref[:, rows] = act_ref[rows, Q].T
        slope_qt_ref[:, rows] = slope_ref[rows, Q].T


def fwd_far_kernel(
    lo_ref, nv_ref, at_ref, act_ref, kva_ref, kvb_ref, near_ref, *refs,
):
    dg_refs, (out_ref, kv_ref, kt_ref, sum_ref), pieces, (attn_s, dg_s) = refs[:5], refs[5:9], refs[9:14], refs[14:]
    head = at_ref[1]
    slot = 0
    for ref in (kva_ref, kvb_ref):
        for at in range(0, ref.shape[0], TILE):
            kv_ref[rows_at(slot ^ head), :] = ref[at : at + TILE, :]
            slot += 1
    for mask, (ref, at) in enumerate(places(dg_refs)):
        dg_s[rows_at(head ^ mask), :] = ref[at : at + TILE, :]
    first = jnp.minimum(lo_ref[0] + SPAN, SPAN) // CHUNK
    for t in range(TILES):
        rows = slice(t * TILE, (t + 1) * TILE)

        @pl.when(t // 2 >= first)
        def _():
            kt_ref[:, rows] = kv_ref[rows, HD:].T

    attn_s[...] = near_ref[...]
    col = lax.broadcasted_iota(jnp.int32, (TILE, CHUNK), 1)

    def q_tile(t, carry):
        q = act_ref[rows_at(t), Q]

        def k_chunk(c, acc):
            mask = from_start(t, lo_ref, c * CHUNK - SPAN, col, 1)
            return acc + weigh(q, kt_ref[:, chunk_at(c)], kv_ref[chunk_at(c), :HD], mask)

        start = (lo_ref[2 * t] + SPAN) // CHUNK
        acc = lax.fori_loop(start, CHUNKS, k_chunk, jnp.zeros((TILE, HD), F32))
        attn_s[rows_at(t), :] += jnp.where(valid_rows(t, nv_ref), acc, 0.0)
        return carry

    lax.fori_loop(0, far_tiles(lo_ref), q_tile, 0)
    ones = jnp.ones((8, HD), BF16)
    for t in range(TILES):
        rows = slice(t * TILE, (t + 1) * TILE)
        attn = attn_s[rows, :] * (SCALE / SPAN)
        out_ref[rows, :] = attn.astype(BF16)
        d_n = dg_s[rows, :].astype(F32) * act_ref[rows, U].astype(F32)
        square = lax.dot_general(ones, (attn * attn).astype(BF16), NT, preferred_element_type=F32)
        cross = lax.dot_general(ones, (attn * d_n).astype(BF16), NT, preferred_element_type=F32)
        sum_ref[t : t + 1, :] = square[:1]
        sum_ref[TILES + t : TILES + t + 1, :] = cross[:1]
    for mask, (ref, at) in enumerate(outgoing(pieces)):
        ref[at : at + TILE, :] = out_ref[rows_at(head ^ mask), :]


def add_kernel(a_ref, b_ref, out_ref):
    out_ref[...] = a_ref[...] + b_ref[...]


def far_tiles(lo_ref):
    return sum((lo_ref[2 * t] < 0).astype(jnp.int32) for t in range(TILES))


def row_scales(sum_refs):
    width = HEADS * HD
    total = sum_refs[0][...]
    for ref in sum_refs[1:]:
        total += ref[...]
    r = lax.rsqrt(total[:TILES] * (1.0 / width) + eps)
    c = total[TILES:] * (1.0 / width) * r
    return jnp.concatenate([r, c], axis=0).T


def cotangent(t, scales, nv_ref, u, attn, d_gated):
    r, c = scales[:, t : t + 1], scales[:, TILES + t : TILES + t + 1]
    n = attn.astype(F32) * r
    g = r * (d_gated * u.astype(F32) - n * c)
    return n, jnp.where(valid_rows(t, nv_ref), g, 0.0).astype(BF16)


def back_scores(qt, k, v, gt, mask):
    s = jnp.dot(k, qt, preferred_element_type=F32)
    sig = jnp.where(mask, sigmoid(s), 0.0)
    dw = jnp.dot(v, gt, preferred_element_type=F32)
    ds = dw * sig * (1.0 + (s * SCALE) * (1.0 - sig))
    return (s * sig).astype(BF16), ds.astype(BF16)


def cotangent_kernel(nv_ref, at_ref, act_ref, slope_ref, attn_ref, *refs):
    sum_refs, dg_refs, (g_ref, cols_ref, dg_s) = refs[:4], refs[4:9], refs[-3:]
    for mask, (ref, at) in enumerate(places(dg_refs)):
        dg_s[rows_at(at_ref[1] ^ mask), :] = ref[at : at + TILE, :]
    scales = row_scales(sum_refs)
    for t in range(TILES):
        rows = slice(t * TILE, (t + 1) * TILE)
        d_gated = dg_s[rows, :].astype(F32)
        n, g = cotangent(t, scales, nv_ref, act_ref[rows, U], attn_ref[rows, :], d_gated)
        g_ref[rows, :] = g
        du = (d_gated * n).astype(BF16).astype(F32)
        cols_ref[:, rows] = (du * slope_ref[rows, U].astype(F32)).astype(BF16).T


def queries_kernel(lo_ref, act_ref, slope_qt_ref, qt_ref, kt_ref, g_ref, kv_ref, far_kt_ref, cols_ref, rows_ref, dkv_ref, gt_s):
    for t in range(TILES):
        rows = slice(t * TILE, (t + 1) * TILE)
        gt_s[:, rows] = g_ref[rows, :].T
    for c in range(CHUNKS):
        dkv_ref[c * CHUNK : (c + 1) * CHUNK, :] = jnp.zeros((CHUNK, 2 * HD), F32)
    key = lax.broadcasted_iota(jnp.int32, (CHUNK, TILE), 0)
    query = lax.broadcasted_iota(jnp.int32, (CHUNK, TILE), 1)

    def q_tile(t, carry):
        q, qt = act_ref[rows_at(t), Q], qt_ref[:, rows_at(t)]
        g, gt = g_ref[rows_at(t), :], gt_s[:, rows_at(t)]

        def far_chunk(c, dqt):
            at = chunk_at(c)
            mask = from_start(t, lo_ref, c * CHUNK - SPAN, key, 0)
            ds = back_scores(qt, kv_ref[at, HD:], kv_ref[at, :HD], gt, mask)[1]
            return dqt + jnp.dot(far_kt_ref[:, at], ds, preferred_element_type=F32)

        def k_chunk(c, dqt):
            at = chunk_at(c)
            mask = from_start(t, lo_ref, c * CHUNK, key, 0) & (key - query <= t * TILE - c * CHUNK)
            w, ds = back_scores(qt, act_ref[at, K], act_ref[at, V], gt, mask)
            dkv_ref[at, :HD] += jnp.dot(w, g, preferred_element_type=F32)
            dkv_ref[at, HD:] += jnp.dot(ds, q, preferred_element_type=F32)
            return dqt + jnp.dot(kt_ref[:, at], ds, preferred_element_type=F32)

        first = lo_ref[2 * t]
        start = jnp.minimum(first + SPAN, SPAN) // CHUNK
        dqt = lax.fori_loop(start, CHUNKS, far_chunk, jnp.zeros((HD, TILE), F32))
        dqt = lax.fori_loop(jnp.maximum(first, 0) // CHUNK, t // 2 + 1, k_chunk, dqt)
        dq = (dqt * (SCALE / SPAN)).astype(BF16).astype(F32)
        dq = (dq * slope_qt_ref[:, rows_at(t)].astype(F32)).astype(BF16)
        cols_ref[:, rows_at(t)] = dq
        rows_ref[rows_at(t), :] = dq.T
        return carry

    lax.fori_loop(0, TILES, q_tile, 0)


def halving(groups):
    return [0] if groups == 1 else [2 * i for i in halving(groups // 2)] + [2 * i + 1 for i in halving(groups // 2)]


def keys_kernel(
    groups, lo_ref, at_ref, own_ref, act_ref, slope_ref, q_ref, g_ref, u_cols_ref, q_cols_ref, dq_ref, normed_ref, *refs
):
    pieces, (keep, send, cols_s, all_s, acc_s) = refs[:5], refs[5:]
    first = jnp.minimum(lo_ref[2 * TILES], SPAN) // CHUNK
    key = lax.broadcasted_iota(jnp.int32, (CHUNK, TILE), 0)

    def clear(c, carry):
        acc_s[chunk_at(c), :] = jnp.zeros((CHUNK, 2 * HD), F32)
        return carry

    lax.fori_loop(first, CHUNKS, clear, 0)

    def q_tile(t, carry):
        q, g = q_ref[rows_at(t), :], g_ref[rows_at(t), :]
        qt, gt = q.T, g.T

        def k_chunk(c, carry):
            at = chunk_at(c)
            mask = from_start(TILES + t, lo_ref, c * CHUNK, key, 0)
            w, ds = back_scores(qt, act_ref[at, K], act_ref[at, V], gt, mask)
            acc_s[at, :HD] += jnp.dot(w, g, preferred_element_type=F32)
            acc_s[at, HD:] += jnp.dot(ds, q, preferred_element_type=F32)
            return carry

        return lax.fori_loop(lo_ref[2 * (TILES + t)] // CHUNK, CHUNKS, k_chunk, carry)

    count = sum((lo_ref[2 * (TILES + t)] < SPAN).astype(jnp.int32) for t in range(TILES))
    lax.fori_loop(0, count, q_tile, 0)
    for mask, (ref, at) in enumerate(outgoing(pieces)):
        t = at_ref[1] ^ mask
        rows = rows_at(t)
        d = own_ref[rows, :] + jnp.where(t // 2 >= first, acc_s[rows, :], 0.0)
        d = (d * (SCALE / SPAN)).astype(BF16).astype(F32)
        d = (d * slope_ref[rows, VK].astype(F32)).astype(BF16)
        ref[at : at + TILE, :HD] = dq_ref[rows, :]
        ref[at : at + TILE, HD:] = d
        cols_s[:, rows] = d.T
    share = jnp.dot(cols_s[...], normed_ref[...], preferred_element_type=F32).astype(BF16)
    all_s[HD : 2 * HD, :], all_s[3 * HD :, :] = share[:HD], share[HD:]
    all_s[:HD, :] = jnp.dot(u_cols_ref[...], normed_ref[...], preferred_element_type=F32).astype(BF16)
    all_s[2 * HD : 3 * HD, :] = jnp.dot(q_cols_ref[...], normed_ref[...], preferred_element_type=F32).astype(BF16)
    size = 4 * HD // groups
    for i, mask in enumerate(halving(groups)):
        at = pl.multiple_of((at_ref[0] ^ mask) * size, size)
        part = all_s[pl.ds(at, size), :]
        if i < groups // 2:
            keep[i * size : (i + 1) * size, :] = part.astype(F32)
        else:
            send[(i - groups // 2) * size : (i + 1 - groups // 2) * size, :] = part


def assemble(at_ref, refs, part, out_s):
    for mask, (ref, at) in enumerate(places(refs)):
        out_s[:, lanes_at(at_ref[1] ^ mask)] = ref[at : at + TILE, part * HD : (part + 1) * HD]
    return out_s[...]


def through(x, w_ref, branch):
    width = w_ref.shape[0]
    return lax.dot_general(x, w_ref[:, branch * width : (branch + 1) * width], NT, preferred_element_type=F32)


def branches_kernel(at_ref, *refs):
    pieces, (w_in_ref, dn_ref, row_s) = refs[:5], refs[5:]
    dn = through(assemble(at_ref, pieces, 0, row_s), w_in_ref, 2)
    for i, branch in ((1, 1), (2, 3)):
        dn += through(assemble(at_ref, pieces, i, row_s), w_in_ref, branch)
    dn_ref[...] = dn


def own_u_kernel(tokens_ref, w_in_ref, after_ref, u_ref, slope_ref):
    xn = norm_rows(tokens_ref[...].astype(F32)).astype(BF16)
    pre = jnp.dot(xn, w_in_ref[:, : tokens_ref.shape[1]], preferred_element_type=F32)
    u_ref[...], slope_ref[...] = silu_and_slope(pre)


def rows_kernel(at_ref, *refs):
    attn_refs, (dn_ref, dg_ref, u_ref, slope_ref, tokens_ref, grad_ref, w_out_ref, w_in_ref) = refs[:5], refs[5:-4]
    out_ref, dx_ref, end_ref, row_s = refs[-4:]
    end_ref[...] = jnp.zeros(end_ref.shape, F32)
    x = tokens_ref[...].astype(F32)
    attn_n = norm_rows(assemble(at_ref, attn_refs, 0, row_s).astype(F32))
    gated = (attn_n * u_ref[...].astype(F32)).astype(BF16)
    y = jnp.dot(gated, w_out_ref[...], preferred_element_type=F32)
    out_ref[...] = (x + y).astype(BF16)
    du = (dg_ref[...].astype(F32) * attn_n).astype(BF16).astype(F32)
    du = (du * slope_ref[...].astype(F32)).astype(BF16)
    dn = dn_ref[...] + through(du, w_in_ref, 0)
    r = lax.rsqrt(jnp.mean(x * x, axis=-1, keepdims=True) + eps)
    n = x * r
    dx = r * (dn - n * jnp.mean(dn * n, axis=-1, keepdims=True))
    dx_ref[...] = (grad_ref[...].astype(F32) + dx).astype(BF16)


def half_kernel(keep_ref, got_ref, *refs):
    half = refs[-1].shape[0]
    if half == keep_ref.shape[0]:
        refs = refs[-1:]
    refs[0][...] = keep_ref[:half, :] + got_ref[:half, :].astype(F32)
    if len(refs) > 1:
        refs[1][...] = (keep_ref[half:, :] + got_ref[half:, :].astype(F32)).astype(BF16)


def last_kernel(at_ref, *refs):
    pieces, (dn_ref, tokens_ref, grad_ref, w_in_ref, out_ref, end_ref, row_s) = refs[:5], refs[5:]
    end_ref[...] = jnp.zeros(end_ref.shape, F32)
    dn = dn_ref[...]
    for i, branch in enumerate((2, 1, 3)):
        dn += through(assemble(at_ref, pieces, i, row_s), w_in_ref, branch)
    x = tokens_ref[...].astype(F32)
    r = lax.rsqrt(jnp.mean(x * x, axis=-1, keepdims=True) + eps)
    n = x * r
    dx = r * (dn - n * jnp.mean(dn * n, axis=-1, keepdims=True))
    out_ref[...] = (grad_ref[...].astype(F32) + dx).astype(BF16)


def call(kernel, scalars, arrays, outs, scratch=(), after=(), aliases=None, limit=16, sems=0):
    smem = pl.BlockSpec(memory_space=pltpu.SMEM)
    vmem = pl.BlockSpec(memory_space=pltpu.VMEM)
    anywhere = pl.BlockSpec(memory_space=pl.ANY)
    return pl.pallas_call(
        kernel,
        out_shape=[jax.ShapeDtypeStruct(*out) for out in outs],
        in_specs=[smem] * len(scalars) + [vmem] * len(arrays) + [anywhere] * len(after),
        out_specs=[smem if out[1] == jnp.int32 else vmem for out in outs],
        scratch_shapes=[pltpu.VMEM(*shape) for shape in scratch] + ([pltpu.SemaphoreType.DMA((sems,))] if sems else []),
        input_output_aliases=aliases or {},
        compiler_params=pltpu.CompilerParams(vmem_limit_bytes=limit * 2**20),
        cost_estimate=pl.CostEstimate(flops=0, bytes_accessed=0, transcendentals=0),
    )(*scalars, *arrays, *after)


def per_device(groups, tokens, w_in, w_out, block_counts, tails, grad_out):
    count, width = tokens.shape
    own, tall, wide, tall_t = (count, width), (SPAN, HD), (SPAN, 2 * HD), (HD, SPAN)
    piece, half, sums_shape = (count, HD), (BLK, width), (2 * TILES, TILE)

    def swap(x, mask):
        return lax.ppermute(x, "h", [(i, i ^ mask) for i in range(HEADS)])

    def onward(x):
        return lax.ppermute(x, "g", [(i, i + 1) for i in range(groups - 1)])

    def backward(x):
        return lax.ppermute(x, "g", [(i + 1, i) for i in range(groups - 1)])

    def trade(pieces, after=()):
        mine, other, *pairs = pieces
        other = swap(other, 1)
        pairs = call(
            merge_kernel,
            (),
            (other,),
            [(x.shape, BF16) for x in pairs],
            after=(*pairs, *after),
            aliases={1: 0, 2: 1, 3: 2},
            limit=4,
        )
        return [mine, other] + [swap(x, mask) for x, mask in zip(pairs, (2, 4, 6))]

    x_rows, y_rows = swap(tokens, 2), swap(tokens, 4)
    other = swap(tokens, 1)
    *info, w_head = call(
        start_kernel,
        (block_counts, tails),
        (),
        [((2 * MAXB,), jnp.int32)] * 2 + [((2,), jnp.int32), ((width, 4 * HD), BF16)],
        after=(w_in,),
        limit=51,
        sems=4,
    )
    *kept, kv = project(info, (0, 1), ((tokens,), (other,)), w_head, ())
    *dg_pieces, dg_own = call(
        d_gated_kernel, info[2:], (grad_out, w_out), trade_outs(HD) + [(own, BF16)], after=(kv,)
    )
    x_rows, y_rows, x_half, y_half = call(
        cut_kernel,
        (),
        (x_rows, y_rows),
        [(own, BF16), (own, BF16), (half, BF16), (half, BF16)],
        after=(kv, dg_own),
        aliases={0: 0, 1: 1},
        limit=4,
    )
    corner = swap(x_half, 4), swap(y_half, 2)
    chunks = ((x_rows,), (swap(x_rows, 1),), (y_rows,), (swap(y_rows, 1),))
    *kept, kv = project(info, (2, 3, 4, 5), chunks, w_head, kept, kv=kv)
    far_kv = [onward(kv)]
    corner = call(gate_kernel, (), (), [(half, BF16), (half, BF16)], after=(*corner, kv), aliases={0: 0, 1: 1}, limit=4)
    *kept, kv, q = project(info, (6, 7), (corner, [swap(x, 1) for x in corner]), w_head, kept, True)
    far_kv.append(onward(kv))
    q_next = backward(q)
    normed, act, slope = kept

    near, kt, qt, slope_qt = call(fwd_own_kernel, info[:2], (act, slope), [(tall, F32)] + [(tall_t, BF16)] * 3)
    d_gated = trade(dg_pieces, (near,))
    attn, kv, far_kt, sums, *attn_pieces = call(
        fwd_far_kernel,
        info,
        (act, *far_kv, near, *d_gated),
        [(tall, BF16), (wide, BF16), (tall_t, BF16), (sums_shape, F32)] + trade_outs(HD),
        [(tall, F32), (tall, BF16)],
    )
    sums = call(add_kernel, (), (sums, swap(sums, 1)), [(sums_shape, F32)], limit=4)[0]
    sums = [sums] + [swap(sums, mask) for mask in (2, 4, 6)]

    g, u_cols = call(
        cotangent_kernel,
        info[1:],
        (act, slope, attn, *sums, *d_gated),
        [(tall, BF16), (tall_t, BF16)],
        [(tall, BF16)],
        (q_next,),
    )
    g_next = backward(g)
    q_cols, d_q, dkv = call(
        queries_kernel,
        info[:1],
        (act, slope_qt, qt, kt, g, kv, far_kt),
        [(tall_t, BF16), (tall, BF16), (wide, F32)],
        [(tall_t, BF16)],
    )
    rows, cols = 4 * HD // groups, 3 * HD
    half_rows = rows * groups // 2
    *pieces, keep, send = call(
        functools.partial(keys_kernel, groups),
        (info[0], info[2]),
        (dkv, act, slope, q_next, g_next, u_cols, q_cols, d_q, normed),
        trade_outs(cols) + [((half_rows, width), F32), ((half_rows, width), BF16)],
        [((2 * HD, SPAN), BF16), ((4 * HD, width), BF16), (wide, F32)],
    )
    pieces = trade(pieces)
    u, slope_u = call(own_u_kernel, (), (tokens, w_in), [(own, BF16), (own, BF16)], after=(pieces[0],))
    mask, attn_rows = 1, None
    while mask < groups:
        send = lax.ppermute(send, "g", [(i, i ^ mask) for i in range(groups)])
        mask, half_rows = 2 * mask, half_rows // 2
        if mask < groups:
            keep, send = call(half_kernel, (), (keep, send), [((half_rows, width), F32), ((half_rows, width), BF16)])
        if attn_rows is None:
            attn_rows = trade(attn_pieces, (send,))
    d_normed = call(branches_kernel, info[2:], (*pieces, w_in), [(own, F32)], [(own, BF16)])[0]
    layer_out, grad_tokens, end = call(
        rows_kernel,
        info[2:],
        (*attn_rows, d_normed, dg_own, u, slope_u, tokens, grad_out, w_out, w_in),
        [(own, BF16), (own, BF16), ((8, HD), F32)],
        [(own, BF16)],
    )
    grad_w_in = call(half_kernel, (), (keep, send), [((rows, width), F32)], after=(end,))[0]
    parts = groups // 4
    if parts > 1:
        perm = [
            (i * HEADS + j, ((i // parts) * HEADS + j) * parts + i % parts)
            for i in range(groups)
            for j in range(HEADS)
        ]
        grad_w_in = lax.ppermute(grad_w_in, ("g", "h"), perm)
    return (layer_out, grad_tokens, grad_w_in)


def solution(mesh):
    groups = mesh.shape["seq"] // HEADS
    split = Mesh(mesh.devices.reshape(groups, HEADS), ("g", "h"))
    rows = P(("g", "h"), None)
    return jax.shard_map(
        functools.partial(per_device, groups),
        mesh=split,
        in_specs=(rows, P(), P(), P(), P(), rows),
        out_specs=(rows, rows, rows),
        check_vma=False,
    )
```

```python
import functools

import jax
import jax.numpy as jnp
from jax import lax
from jax.experimental import pallas as pl
from jax.experimental.pallas import tpu as pltpu
from jax.sharding import Mesh, PartitionSpec as P

HEADS = 8
HD = 128
BLK = 128
MAXB = 16
SPAN = MAXB * BLK
TILE = 256
TILES = SPAN // TILE
CHUNK = 512
CHUNKS = SPAN // CHUNK
SCALE = HD ** (-0.5)
LOG2E = 1.4426950408889634

eps = 1e-05

NT = (((1,), (1,)), ((), ()))
F32, BF16 = jnp.float32, jnp.bfloat16

U, Q, V, K = (slice(i * HD, (i + 1) * HD) for i in range(4))
PLACE = (0, 2, 1, 3)
UQ, VK = slice(0, 2 * HD), slice(2 * HD, 4 * HD)


def start_kernel(counts_ref, tails_ref, w_ref, lo_ref, nv_ref, at_ref, wh_ref, sems):
    group = lax.axis_index("g").astype(jnp.int32)
    at_ref[0] = group
    head = lax.axis_index("h").astype(jnp.int32)
    at_ref[1] = head
    copies = []
    for i in range(4):
        source = w_ref.at[:, lanes_at(PLACE[i] * (w_ref.shape[0] // HD) + head)]
        copies.append(pltpu.make_async_copy(source, wh_ref.at[:, i * HD : (i + 1) * HD], sems.at[i]))
        copies[i].start()
    base = group * MAXB
    for j in range(2 * MAXB):
        lo_ref[j] = j * BLK
        nv_ref[j] = BLK

    def user(n, start):
        end = start + counts_ref[n]

        def block(j, carry):
            lo_ref[j] = (start - base) * BLK
            nv_ref[j] = jnp.where(j == end - 1 - base, tails_ref[n], BLK)
            return carry

        lax.fori_loop(jnp.maximum(start - base, 0), jnp.minimum(end - base, 2 * MAXB), block, 0)
        return end

    lax.fori_loop(0, counts_ref.shape[0], user, jnp.int32(0))
    for copy in copies:
        copy.wait()


def by_half(t, ref, shape, dim):
    side = lax.broadcasted_iota(jnp.int32, shape, dim)
    return jnp.where(side < BLK, ref[2 * t], ref[2 * t + 1])


def from_start(t, lo_ref, at, keys, dim):
    parts = [part >= lo_ref[2 * t + i] - at for i, part in enumerate(jnp.split(keys, 2, axis=1 - dim))]
    return jnp.concatenate(parts, axis=1 - dim)


def valid_rows(t, nv_ref):
    row = lax.broadcasted_iota(jnp.int32, (TILE, 1), 0)
    return (row & (BLK - 1)) < by_half(t, nv_ref, (TILE, 1), 0)


def rows_at(t):
    return pl.ds(pl.multiple_of(t * TILE, TILE), TILE)


def chunk_at(c):
    return pl.ds(pl.multiple_of(c * CHUNK, CHUNK), CHUNK)


def lanes_at(i):
    return pl.ds(pl.multiple_of(i * HD, HD), HD)


def norm_rows(x):
    return x * lax.rsqrt(jnp.mean(x * x, axis=-1, keepdims=True) + eps)


def silu_and_slope(pre):
    s = 0.5 + 0.5 * jnp.tanh(0.5 * pre)
    return (pre * s).astype(BF16), (s * (1.0 + pre * (1.0 - s))).astype(BF16)


def store_rows(x, place, wh_ref, normed_ref, act_ref, slope_ref, kv_ref, i):
    rows = rows_at(place)
    xn = norm_rows(x.astype(F32)).astype(BF16)
    normed_ref[rows, :] = xn
    act, slope = silu_and_slope(jnp.dot(xn, wh_ref[...], preferred_element_type=F32))
    act_ref[rows, :] = act
    slope_ref[rows, :] = slope
    kv_ref[i * TILE : (i + 1) * TILE, :] = act[:, VK]


def proj_kernel(masks, pieces, last, ahead, at_ref, *refs):
    x_refs, wh_ref = refs[: sum(pieces)], refs[sum(pieces)]
    outs = refs[-5:-1] if last else refs[-4:]
    if ahead:
        outs[3][: ahead * TILE, :] = refs[sum(pieces) + 1][...]
    for i, mask in enumerate(masks):
        parts = [ref[...] for ref in x_refs[sum(pieces[:i]) : sum(pieces[: i + 1])]]
        x = parts[0] if len(parts) == 1 else jnp.concatenate(parts, axis=0)
        store_rows(x, at_ref[1] ^ mask, wh_ref, *outs, ahead + i)
    if last:
        refs[-1][...] = outs[1][:, Q]


def proj_outs(width, n):
    return [((SPAN, width), BF16), ((SPAN, 4 * HD), BF16), ((SPAN, 4 * HD), BF16), ((n * TILE, 2 * HD), BF16)]


def project(info, masks, chunks, w, kept, last=False, kv=None):
    pieces = tuple(len(chunk) for chunk in chunks)
    flat = [piece for chunk in chunks for piece in chunk]
    lead = () if kv is None else (kv,)
    ahead = 0 if kv is None else kv.shape[0] // TILE
    start = 2 + len(flat) + len(lead)
    return call(
        functools.partial(proj_kernel, masks, pieces, last, ahead),
        (info[2],),
        (*flat, w, *lead),
        proj_outs(w.shape[0], ahead + len(masks)) + ([((SPAN, HD), BF16)] if last else []),
        after=kept,
        aliases={start + i: i for i in range(len(kept))},
    )


def cut_kernel(x_ref, y_ref, *refs):
    x_half, y_half = refs[-2:]
    x_half[...] = x_ref[:BLK, :]
    y_half[...] = y_ref[BLK:, :]


def gate_kernel(*refs):
    pass


def merge_kernel(other_ref, *refs):
    for i, ref in enumerate(refs[-3:]):
        ref[TILE:, :] = other_ref[(i + 1) * TILE : (i + 2) * TILE, :]


def places(refs):
    mine, other, *pairs = refs
    return [(mine, 0), (other, 0)] + [(ref, at) for ref in pairs for at in (0, TILE)]


def outgoing(refs):
    mine, other, *pairs = refs
    found = [(mine, 0)] * HEADS
    for i in range(4):
        found[2 * i + 1] = other, i * TILE
    for i in range(3):
        found[2 * i + 2] = pairs[i], 0
    return found


def trade_outs(cols):
    return [((TILE, cols), BF16), ((4 * TILE, cols), BF16)] + [((2 * TILE, cols), BF16)] * 3


def d_gated_kernel(at_ref, g_ref, w_ref, *refs):
    pieces, d_ref = refs[-6:-1], refs[-1]
    d_ref[...] = lax.dot_general(g_ref[...], w_ref[...], NT, preferred_element_type=F32).astype(BF16)
    for mask, (ref, at) in enumerate(outgoing(pieces)):
        ref[at : at + TILE, :] = d_ref[:, lanes_at(at_ref[1] ^ mask)]


def sigmoid(s):
    return pl.reciprocal(1.0 + jnp.exp2(s * (-SCALE * LOG2E)), approx=True)


def weigh(q, kt, v, mask):
    s = jnp.dot(q, kt, preferred_element_type=F32)
    w = jnp.where(mask, s * sigmoid(s), 0.0).astype(BF16)
    return jnp.dot(w, v, preferred_element_type=F32)


def fwd_own_kernel(lo_ref, nv_ref, act_ref, slope_ref, out_ref, kt_ref, qt_ref, slope_qt_ref):
    for t in range(TILES):
        rows = slice(t * TILE, (t + 1) * TILE)
        kt_ref[:, rows] = act_ref[rows, K].T
    row = lax.broadcasted_iota(jnp.int32, (TILE, CHUNK), 0)
    col = lax.broadcasted_iota(jnp.int32, (TILE, CHUNK), 1)

    def q_tile(t, carry):
        q = act_ref[rows_at(t), Q]

        def k_chunk(c, acc):
            mask = from_start(t, lo_ref, c * CHUNK, col, 1) & (col - row <= t * TILE - c * CHUNK)
            return acc + weigh(q, kt_ref[:, chunk_at(c)], act_ref[chunk_at(c), V], mask)

        first = jnp.maximum(lo_ref[2 * t], 0) // CHUNK
        acc = lax.fori_loop(first, t // 2 + 1, k_chunk, jnp.zeros((TILE, HD), F32))
        out_ref[rows_at(t), :] = jnp.where(valid_rows(t, nv_ref), acc, 0.0)
        return carry

    lax.fori_loop(0, TILES, q_tile, 0)
    for t in range(TILES):
        rows = slice(t * TILE, (t + 1) * TILE)
        qt_ref[:, rows] = act_ref[rows, Q].T
        slope_qt_ref[:, rows] = slope_ref[rows, Q].T


def fwd_far_kernel(
    lo_ref, nv_ref, at_ref, act_ref, kva_ref, kvb_ref, near_ref, *refs,
):
    dg_refs, (out_ref, kv_ref, kt_ref, sum_ref, attn_s, dg_s) = refs[:5], refs[5:]
    head = at_ref[1]
    slot = 0
    for ref in (kva_ref, kvb_ref):
        for at in range(0, ref.shape[0], TILE):
            kv_ref[rows_at(slot ^ head), :] = ref[at : at + TILE, :]
            slot += 1
    for mask, (ref, at) in enumerate(places(dg_refs)):
        dg_s[rows_at(head ^ mask), :] = ref[at : at + TILE, :]
    first = jnp.minimum(lo_ref[0] + SPAN, SPAN) // CHUNK
    for t in range(TILES):
        rows = slice(t * TILE, (t + 1) * TILE)

        @pl.when(t // 2 >= first)
        def _():
            kt_ref[:, rows] = kv_ref[rows, HD:].T

    attn_s[...] = near_ref[...]
    col = lax.broadcasted_iota(jnp.int32, (TILE, CHUNK), 1)

    def q_tile(t, carry):
        q = act_ref[rows_at(t), Q]

        def k_chunk(c, acc):
            mask = from_start(t, lo_ref, c * CHUNK - SPAN, col, 1)
            return acc + weigh(q, kt_ref[:, chunk_at(c)], kv_ref[chunk_at(c), :HD], mask)

        start = (lo_ref[2 * t] + SPAN) // CHUNK
        acc = lax.fori_loop(start, CHUNKS, k_chunk, jnp.zeros((TILE, HD), F32))
        attn_s[rows_at(t), :] += jnp.where(valid_rows(t, nv_ref), acc, 0.0)
        return carry

    lax.fori_loop(0, far_tiles(lo_ref), q_tile, 0)
    ones = jnp.ones((8, HD), BF16)
    for t in range(TILES):
        rows = slice(t * TILE, (t + 1) * TILE)
        attn = attn_s[rows, :] * (SCALE / SPAN)
        out_ref[rows, :] = attn.astype(BF16)
        d_n = dg_s[rows, :].astype(F32) * act_ref[rows, U].astype(F32)
        square = lax.dot_general(ones, (attn * attn).astype(BF16), NT, preferred_element_type=F32)
        cross = lax.dot_general(ones, (attn * d_n).astype(BF16), NT, preferred_element_type=F32)
        sum_ref[t : t + 1, :] = square[:1]
        sum_ref[TILES + t : TILES + t + 1, :] = cross[:1]


def add_kernel(a_ref, b_ref, out_ref):
    out_ref[...] = a_ref[...] + b_ref[...]


def far_tiles(lo_ref):
    return sum((lo_ref[2 * t] < 0).astype(jnp.int32) for t in range(TILES))


def row_scales(sum_refs):
    width = HEADS * HD
    total = sum_refs[0][...]
    for ref in sum_refs[1:]:
        total += ref[...]
    r = lax.rsqrt(total[:TILES] * (1.0 / width) + eps)
    c = total[TILES:] * (1.0 / width) * r
    return jnp.concatenate([r, c], axis=0).T


def cotangent(t, scales, nv_ref, u, attn, d_gated):
    r, c = scales[:, t : t + 1], scales[:, TILES + t : TILES + t + 1]
    n = attn.astype(F32) * r
    g = r * (d_gated * u.astype(F32) - n * c)
    return n, jnp.where(valid_rows(t, nv_ref), g, 0.0).astype(BF16)


def back_scores(qt, k, v, gt, mask):
    s = jnp.dot(k, qt, preferred_element_type=F32)
    sig = jnp.where(mask, sigmoid(s), 0.0)
    dw = jnp.dot(v, gt, preferred_element_type=F32)
    ds = dw * sig * (1.0 + (s * SCALE) * (1.0 - sig))
    return (s * sig).astype(BF16), ds.astype(BF16)


def cotangent_kernel(nv_ref, at_ref, act_ref, slope_ref, attn_ref, *refs):
    sum_refs, dg_refs, (g_ref, cols_ref, dg_s) = refs[:4], refs[4:9], refs[-3:]
    for mask, (ref, at) in enumerate(places(dg_refs)):
        dg_s[rows_at(at_ref[1] ^ mask), :] = ref[at : at + TILE, :]
    scales = row_scales(sum_refs)
    for t in range(TILES):
        rows = slice(t * TILE, (t + 1) * TILE)
        d_gated = dg_s[rows, :].astype(F32)
        n, g = cotangent(t, scales, nv_ref, act_ref[rows, U], attn_ref[rows, :], d_gated)
        g_ref[rows, :] = g
        du = (d_gated * n).astype(BF16).astype(F32)
        cols_ref[:, rows] = (du * slope_ref[rows, U].astype(F32)).astype(BF16).T


def queries_kernel(lo_ref, act_ref, slope_qt_ref, qt_ref, kt_ref, g_ref, kv_ref, far_kt_ref, cols_ref, rows_ref, dkv_ref, gt_s):
    for t in range(TILES):
        rows = slice(t * TILE, (t + 1) * TILE)
        gt_s[:, rows] = g_ref[rows, :].T
    for c in range(CHUNKS):
        dkv_ref[c * CHUNK : (c + 1) * CHUNK, :] = jnp.zeros((CHUNK, 2 * HD), F32)
    key = lax.broadcasted_iota(jnp.int32, (CHUNK, TILE), 0)
    query = lax.broadcasted_iota(jnp.int32, (CHUNK, TILE), 1)

    def q_tile(t, carry):
        q, qt = act_ref[rows_at(t), Q], qt_ref[:, rows_at(t)]
        g, gt = g_ref[rows_at(t), :], gt_s[:, rows_at(t)]

        def far_chunk(c, dqt):
            at = chunk_at(c)
            mask = from_start(t, lo_ref, c * CHUNK - SPAN, key, 0)
            ds = back_scores(qt, kv_ref[at, HD:], kv_ref[at, :HD], gt, mask)[1]
            return dqt + jnp.dot(far_kt_ref[:, at], ds, preferred_element_type=F32)

        def k_chunk(c, dqt):
            at = chunk_at(c)
            mask = from_start(t, lo_ref, c * CHUNK, key, 0) & (key - query <= t * TILE - c * CHUNK)
            w, ds = back_scores(qt, act_ref[at, K], act_ref[at, V], gt, mask)
            dkv_ref[at, :HD] += jnp.dot(w, g, preferred_element_type=F32)
            dkv_ref[at, HD:] += jnp.dot(ds, q, preferred_element_type=F32)
            return dqt + jnp.dot(kt_ref[:, at], ds, preferred_element_type=F32)

        first = lo_ref[2 * t]
        start = jnp.minimum(first + SPAN, SPAN) // CHUNK
        dqt = lax.fori_loop(start, CHUNKS, far_chunk, jnp.zeros((HD, TILE), F32))
        dqt = lax.fori_loop(jnp.maximum(first, 0) // CHUNK, t // 2 + 1, k_chunk, dqt)
        dq = (dqt * (SCALE / SPAN)).astype(BF16).astype(F32)
        dq = (dq * slope_qt_ref[:, rows_at(t)].astype(F32)).astype(BF16)
        cols_ref[:, rows_at(t)] = dq
        rows_ref[rows_at(t), :] = dq.T
        return carry

    lax.fori_loop(0, TILES, q_tile, 0)


def keys_kernel(
    groups, lo_ref, at_ref, own_ref, act_ref, slope_ref, q_ref, g_ref, u_cols_ref, q_cols_ref, dq_ref, attn_ref, normed_ref, *refs
):
    pieces, shares, (cols_s, all_s, acc_s) = refs[:5], refs[5:-3], refs[-3:]
    first = jnp.minimum(lo_ref[2 * TILES], SPAN) // CHUNK
    key = lax.broadcasted_iota(jnp.int32, (CHUNK, TILE), 0)

    def clear(c, carry):
        acc_s[chunk_at(c), :] = jnp.zeros((CHUNK, 2 * HD), F32)
        return carry

    lax.fori_loop(first, CHUNKS, clear, 0)

    def q_tile(t, carry):
        q, g = q_ref[rows_at(t), :], g_ref[rows_at(t), :]
        qt, gt = q.T, g.T

        def k_chunk(c, carry):
            at = chunk_at(c)
            mask = from_start(TILES + t, lo_ref, c * CHUNK, key, 0)
            w, ds = back_scores(qt, act_ref[at, K], act_ref[at, V], gt, mask)
            acc_s[at, :HD] += jnp.dot(w, g, preferred_element_type=F32)
            acc_s[at, HD:] += jnp.dot(ds, q, preferred_element_type=F32)
            return carry

        return lax.fori_loop(lo_ref[2 * (TILES + t)] // CHUNK, CHUNKS, k_chunk, carry)

    count = sum((lo_ref[2 * (TILES + t)] < SPAN).astype(jnp.int32) for t in range(TILES))
    lax.fori_loop(0, count, q_tile, 0)
    for mask, (ref, at) in enumerate(outgoing(pieces)):
        t = at_ref[1] ^ mask
        rows = rows_at(t)
        d = own_ref[rows, :] + jnp.where(t // 2 >= first, acc_s[rows, :], 0.0)
        d = (d * (SCALE / SPAN)).astype(BF16).astype(F32)
        d = (d * slope_ref[rows, VK].astype(F32)).astype(BF16)
        ref[at : at + TILE, :HD] = attn_ref[rows, :]
        ref[at : at + TILE, HD : 2 * HD] = dq_ref[rows, :]
        ref[at : at + TILE, 2 * HD :] = d
        cols_s[:, rows] = d.T
    share = jnp.dot(cols_s[...], normed_ref[...], preferred_element_type=F32).astype(BF16)
    all_s[HD : 2 * HD, :], all_s[3 * HD :, :] = share[:HD], share[HD:]
    all_s[:HD, :] = jnp.dot(u_cols_ref[...], normed_ref[...], preferred_element_type=F32).astype(BF16)
    all_s[2 * HD : 3 * HD, :] = jnp.dot(q_cols_ref[...], normed_ref[...], preferred_element_type=F32).astype(BF16)
    size = 4 * HD // groups
    for mask in range(groups):
        at = pl.multiple_of((at_ref[0] ^ mask) * size, size)
        shares[mask][...] = all_s[pl.ds(at, size), :]


def assemble(at_ref, refs, part, out_s):
    for mask, (ref, at) in enumerate(places(refs)):
        out_s[:, lanes_at(at_ref[1] ^ mask)] = ref[at : at + TILE, part * HD : (part + 1) * HD]


def branch_rows(at_ref, refs, w_ref, distances, row_s):
    width, total = w_ref.shape[0], 0.0
    for part, branch in ((1, 2), (2, 1), (3, 3)):
        assemble(at_ref, refs, part, row_s)
        for i in distances:
            at = ((at_ref[1] // 2) ^ i) * 2 * HD
            x = row_s[:, pl.ds(pl.multiple_of(at, 2 * HD), 2 * HD)]
            w = w_ref[:, pl.ds(pl.multiple_of(branch * width + at, 2 * HD), 2 * HD)]
            total += lax.dot_general(x, w, NT, preferred_element_type=F32)
    return total


def through(x, w_ref, branch):
    width = w_ref.shape[0]
    return lax.dot_general(x, w_ref[:, branch * width : (branch + 1) * width], NT, preferred_element_type=F32)


def branches_kernel(at_ref, *refs):
    pieces, (w_in_ref, dn_ref, row_s) = refs[:-3], refs[-3:]
    dn_ref[...] = branch_rows(at_ref, pieces, w_in_ref, (0, 1, 2), row_s)


def own_u_kernel(tokens_ref, w_in_ref, after_ref, u_ref, slope_ref):
    xn = norm_rows(tokens_ref[...].astype(F32)).astype(BF16)
    pre = jnp.dot(xn, w_in_ref[:, : tokens_ref.shape[1]], preferred_element_type=F32)
    u_ref[...], slope_ref[...] = silu_and_slope(pre)


def rows_kernel(at_ref, *refs):
    pieces, (dn_ref, dg_ref, u_ref, slope_ref, tokens_ref, grad_ref, w_out_ref, w_in_ref) = refs[:5], refs[5:-4]
    out_ref, dx_ref, row_s = refs[-3:]
    x = tokens_ref[...].astype(F32)
    assemble(at_ref, pieces, 0, row_s)
    attn_n = norm_rows(row_s[...].astype(F32))
    gated = (attn_n * u_ref[...].astype(F32)).astype(BF16)
    y = jnp.dot(gated, w_out_ref[...], preferred_element_type=F32)
    out_ref[...] = (x + y).astype(BF16)
    du = (dg_ref[...].astype(F32) * attn_n).astype(BF16).astype(F32)
    du = (du * slope_ref[...].astype(F32)).astype(BF16)
    dn = dn_ref[...] + through(du, w_in_ref, 0) + branch_rows(at_ref, pieces, w_in_ref, (3,), row_s)
    r = lax.rsqrt(jnp.mean(x * x, axis=-1, keepdims=True) + eps)
    n = x * r
    dx = r * (dn - n * jnp.mean(dn * n, axis=-1, keepdims=True))
    dx_ref[...] = (grad_ref[...].astype(F32) + dx).astype(BF16)


def sum_kernel(groups, *refs):
    total = refs[0][...].astype(F32)
    for ref in refs[1:groups]:
        total += ref[...].astype(F32)
    refs[-2][...] = total
    refs[-1][...] = jnp.zeros(refs[-1].shape, F32)


def call(kernel, scalars, arrays, outs, scratch=(), after=(), aliases=None, limit=16, sems=0):
    smem = pl.BlockSpec(memory_space=pltpu.SMEM)
    vmem = pl.BlockSpec(memory_space=pltpu.VMEM)
    anywhere = pl.BlockSpec(memory_space=pl.ANY)
    return pl.pallas_call(
        kernel,
        out_shape=[jax.ShapeDtypeStruct(*out) for out in outs],
        in_specs=[smem] * len(scalars) + [vmem] * len(arrays) + [anywhere] * len(after),
        out_specs=[smem if out[1] == jnp.int32 else vmem for out in outs],
        scratch_shapes=[pltpu.VMEM(*shape) for shape in scratch] + ([pltpu.SemaphoreType.DMA((sems,))] if sems else []),
        input_output_aliases=aliases or {},
        compiler_params=pltpu.CompilerParams(vmem_limit_bytes=limit * 2**20),
        cost_estimate=pl.CostEstimate(flops=0, bytes_accessed=0, transcendentals=0),
    )(*scalars, *arrays, *after)


def per_device(groups, tokens, w_in, w_out, block_counts, tails, grad_out):
    count, width = tokens.shape
    own, tall, wide, tall_t = (count, width), (SPAN, HD), (SPAN, 2 * HD), (HD, SPAN)
    piece, half, sums_shape = (count, HD), (BLK, width), (2 * TILES, TILE)

    def swap(x, mask):
        return lax.ppermute(x, "h", [(i, i ^ mask) for i in range(HEADS)])

    def onward(x):
        return lax.ppermute(x, "g", [(i, i + 1) for i in range(groups - 1)])

    def backward(x):
        return lax.ppermute(x, "g", [(i + 1, i) for i in range(groups - 1)])

    def trade(pieces, after=()):
        mine, other, *pairs = pieces
        other = swap(other, 1)
        pairs = call(
            merge_kernel,
            (),
            (other,),
            [(x.shape, BF16) for x in pairs],
            after=(*pairs, *after),
            aliases={1: 0, 2: 1, 3: 2},
            limit=4,
        )
        return [mine, other] + [swap(x, mask) for x, mask in zip(pairs, (2, 4, 6))]

    x_rows, y_rows = swap(tokens, 2), swap(tokens, 4)
    other = swap(tokens, 1)
    *info, w_head = call(
        start_kernel,
        (block_counts, tails),
        (),
        [((2 * MAXB,), jnp.int32)] * 2 + [((2,), jnp.int32), ((width, 4 * HD), BF16)],
        after=(w_in,),
        limit=51,
        sems=4,
    )
    *kept, kv = project(info, (0, 1), ((tokens,), (other,)), w_head, ())
    *dg_pieces, dg_own = call(
        d_gated_kernel, info[2:], (grad_out, w_out), trade_outs(HD) + [(own, BF16)], after=(kv,)
    )
    x_rows, y_rows, x_half, y_half = call(
        cut_kernel,
        (),
        (x_rows, y_rows),
        [(own, BF16), (own, BF16), (half, BF16), (half, BF16)],
        after=(kv, dg_own),
        aliases={0: 0, 1: 1},
        limit=4,
    )
    corner = swap(x_half, 4), swap(y_half, 2)
    chunks = ((x_rows,), (swap(x_rows, 1),), (y_rows,), (swap(y_rows, 1),))
    *kept, kv = project(info, (2, 3, 4, 5), chunks, w_head, kept, kv=kv)
    far_kv = [onward(kv)]
    corner = call(gate_kernel, (), (), [(half, BF16), (half, BF16)], after=(*corner, kv), aliases={0: 0, 1: 1}, limit=4)
    *kept, kv, q = project(info, (6, 7), (corner, [swap(x, 1) for x in corner]), w_head, kept, True)
    far_kv.append(onward(kv))
    q_next = backward(q)
    normed, act, slope = kept
    d_gated = trade(dg_pieces, (kv,))

    near, kt, qt, slope_qt = call(fwd_own_kernel, info[:2], (act, slope), [(tall, F32)] + [(tall_t, BF16)] * 3)
    attn, kv, far_kt, sums = call(
        fwd_far_kernel,
        info,
        (act, *far_kv, near, *d_gated),
        [(tall, BF16), (wide, BF16), (tall_t, BF16), (sums_shape, F32)],
        [(tall, F32), (tall, BF16)],
    )
    sums = call(add_kernel, (), (sums, swap(sums, 1)), [(sums_shape, F32)], limit=4)[0]
    sums = [sums] + [swap(sums, mask) for mask in (2, 4, 6)]

    g, u_cols = call(
        cotangent_kernel,
        info[1:],
        (act, slope, attn, *sums, *d_gated),
        [(tall, BF16), (tall_t, BF16)],
        [(tall, BF16)],
        (q_next,),
    )
    g_next = backward(g)
    q_cols, d_q, dkv = call(
        queries_kernel,
        info[:1],
        (act, slope_qt, qt, kt, g, kv, far_kt),
        [(tall_t, BF16), (tall, BF16), (wide, F32)],
        [(tall_t, BF16)],
    )
    rows, cols = 4 * HD // groups, 4 * HD
    outs = call(
        functools.partial(keys_kernel, groups),
        (info[0], info[2]),
        (dkv, act, slope, q_next, g_next, u_cols, q_cols, d_q, attn, normed),
        trade_outs(cols) + [((rows, width), BF16)] * groups,
        [((2 * HD, SPAN), BF16), ((4 * HD, width), BF16), (wide, F32)],
    )
    shares = [outs[5]] + [
        lax.ppermute(outs[5 + mask], "g", [(i, i ^ mask) for i in range(groups)]) for mask in range(1, groups)
    ]
    pieces = trade(outs[:5])
    u, slope_u = call(own_u_kernel, (), (tokens, w_in), [(own, BF16), (own, BF16)], after=(outs[0],))
    grad_w_in, end = call(
        functools.partial(sum_kernel, groups), (), tuple(shares), [((rows, width), F32), ((8, HD), F32)]
    )
    d_normed = call(branches_kernel, info[2:], (*pieces[:4], w_in), [(own, F32)], [(own, BF16)])[0]
    layer_out, grad_tokens = call(
        rows_kernel,
        info[2:],
        (*pieces, d_normed, dg_own, u, slope_u, tokens, grad_out, w_out, w_in),
        [(own, BF16), (own, BF16)],
        [(own, BF16)],
        (end,),
    )
    parts = groups // 4
    if parts > 1:
        perm = [
            (i * HEADS + j, ((i // parts) * HEADS + j) * parts + i % parts)
            for i in range(groups)
            for j in range(HEADS)
        ]
        grad_w_in = lax.ppermute(grad_w_in, ("g", "h"), perm)
    return (layer_out, grad_tokens, grad_w_in)


def solution(mesh):
    groups = mesh.shape["seq"] // HEADS
    split = Mesh(mesh.devices.reshape(groups, HEADS), ("g", "h"))
    rows = P(("g", "h"), None)
    return jax.shard_map(
        functools.partial(per_device, groups),
        mesh=split,
        in_specs=(rows, P(), P(), P(), P(), rows),
        out_specs=(rows, rows, rows),
        check_vma=False,
    )
```

```python
import functools

import jax
import jax.numpy as jnp
from jax import lax
from jax.experimental import pallas as pl
from jax.experimental.pallas import tpu as pltpu
from jax.sharding import Mesh, PartitionSpec as P

HEADS = 8
HD = 128
BLK = 128
MAXB = 16
SPAN = MAXB * BLK
TILE = 256
TILES = SPAN // TILE
CHUNK = 512
CHUNKS = SPAN // CHUNK
SCALE = HD ** (-0.5)
LOG2E = 1.4426950408889634

eps = 1e-05

NT = (((1,), (1,)), ((), ()))
F32, BF16 = jnp.float32, jnp.bfloat16

U, Q, V, K = (slice(i * HD, (i + 1) * HD) for i in range(4))
PLACE = (0, 2, 1, 3)
UQ, VK = slice(0, 2 * HD), slice(2 * HD, 4 * HD)


def start_kernel(counts_ref, tails_ref, w_ref, lo_ref, nv_ref, at_ref, wh_ref, sems):
    group = lax.axis_index("g").astype(jnp.int32)
    at_ref[0] = group
    head = lax.axis_index("h").astype(jnp.int32)
    at_ref[1] = head
    copies = []
    for i in range(4):
        source = w_ref.at[:, lanes_at(PLACE[i] * (w_ref.shape[0] // HD) + head)]
        copies.append(pltpu.make_async_copy(source, wh_ref.at[:, i * HD : (i + 1) * HD], sems.at[i]))
        copies[i].start()
    base = group * MAXB
    for j in range(2 * MAXB):
        lo_ref[j] = j * BLK
        nv_ref[j] = BLK

    def user(n, start):
        end = start + counts_ref[n]

        def block(j, carry):
            lo_ref[j] = (start - base) * BLK
            nv_ref[j] = jnp.where(j == end - 1 - base, tails_ref[n], BLK)
            return carry

        lax.fori_loop(jnp.maximum(start - base, 0), jnp.minimum(end - base, 2 * MAXB), block, 0)
        return end

    lax.fori_loop(0, counts_ref.shape[0], user, jnp.int32(0))
    for copy in copies:
        copy.wait()


def by_half(t, ref, shape, dim):
    side = lax.broadcasted_iota(jnp.int32, shape, dim)
    return jnp.where(side < BLK, ref[2 * t], ref[2 * t + 1])


def from_start(t, lo_ref, at, keys, dim):
    parts = [part >= lo_ref[2 * t + i] - at for i, part in enumerate(jnp.split(keys, 2, axis=1 - dim))]
    return jnp.concatenate(parts, axis=1 - dim)


def valid_rows(t, nv_ref):
    row = lax.broadcasted_iota(jnp.int32, (TILE, 1), 0)
    return (row & (BLK - 1)) < by_half(t, nv_ref, (TILE, 1), 0)


def rows_at(t):
    return pl.ds(pl.multiple_of(t * TILE, TILE), TILE)


def chunk_at(c):
    return pl.ds(pl.multiple_of(c * CHUNK, CHUNK), CHUNK)


def tiles_back(t, first, step, carry):
    count = t - first + 1

    def pair(i, carry):
        return step(pl.multiple_of((t - 2 * i - 1) * TILE, TILE), 2 * TILE, carry)

    carry = lax.fori_loop(0, count // 2, pair, carry)
    return lax.fori_loop(0, count % 2, lambda i, c: step(pl.multiple_of(first * TILE, TILE), TILE, c), carry)


def lanes_at(i):
    return pl.ds(pl.multiple_of(i * HD, HD), HD)


def norm_rows(x):
    return x * lax.rsqrt(jnp.mean(x * x, axis=-1, keepdims=True) + eps)


def silu_and_slope(pre):
    s = 0.5 + 0.5 * jnp.tanh(0.5 * pre)
    return (pre * s).astype(BF16), (s * (1.0 + pre * (1.0 - s))).astype(BF16)


def store_rows(x, place, wh_ref, normed_ref, act_ref, slope_ref, kv_ref, i):
    rows = rows_at(place)
    xn = norm_rows(x.astype(F32)).astype(BF16)
    normed_ref[rows, :] = xn
    act, slope = silu_and_slope(jnp.dot(xn, wh_ref[...], preferred_element_type=F32))
    act_ref[rows, :] = act
    slope_ref[rows, :] = slope
    kv_ref[i * TILE : (i + 1) * TILE, :] = act[:, VK]


def proj_kernel(masks, pieces, last, ahead, at_ref, *refs):
    x_refs, wh_ref = refs[: sum(pieces)], refs[sum(pieces)]
    outs = refs[-5:-1] if last else refs[-4:]
    if ahead:
        outs[3][: ahead * TILE, :] = refs[sum(pieces) + 1][...]
    for i, mask in enumerate(masks):
        parts = [ref[...] for ref in x_refs[sum(pieces[:i]) : sum(pieces[: i + 1])]]
        x = parts[0] if len(parts) == 1 else jnp.concatenate(parts, axis=0)
        store_rows(x, at_ref[1] ^ mask, wh_ref, *outs, ahead + i)
    if last:
        refs[-1][...] = outs[1][:, Q]


def proj_outs(width, n):
    return [((SPAN, width), BF16), ((SPAN, 4 * HD), BF16), ((SPAN, 4 * HD), BF16), ((n * TILE, 2 * HD), BF16)]


def project(info, masks, chunks, w, kept, last=False, kv=None):
    pieces = tuple(len(chunk) for chunk in chunks)
    flat = [piece for chunk in chunks for piece in chunk]
    lead = () if kv is None else (kv,)
    ahead = 0 if kv is None else kv.shape[0] // TILE
    start = 2 + len(flat) + len(lead)
    return call(
        functools.partial(proj_kernel, masks, pieces, last, ahead),
        (info[2],),
        (*flat, w, *lead),
        proj_outs(w.shape[0], ahead + len(masks)) + ([((SPAN, HD), BF16)] if last else []),
        after=kept,
        aliases={start + i: i for i in range(len(kept))},
    )


def cut_kernel(x_ref, y_ref, *refs):
    x_half, y_half = refs[-2:]
    x_half[...] = x_ref[:BLK, :]
    y_half[...] = y_ref[BLK:, :]


def gate_kernel(*refs):
    pass


def merge_kernel(other_ref, *refs):
    for i, ref in enumerate(refs[-3:]):
        ref[TILE:, :] = other_ref[(i + 1) * TILE : (i + 2) * TILE, :]


def places(refs):
    mine, other, *pairs = refs
    return [(mine, 0), (other, 0)] + [(ref, at) for ref in pairs for at in (0, TILE)]


def outgoing(refs):
    mine, other, *pairs = refs
    found = [(mine, 0)] * HEADS
    for i in range(4):
        found[2 * i + 1] = other, i * TILE
    for i in range(3):
        found[2 * i + 2] = pairs[i], 0
    return found


def trade_outs(cols):
    return [((TILE, cols), BF16), ((4 * TILE, cols), BF16)] + [((2 * TILE, cols), BF16)] * 3


def d_gated_kernel(at_ref, g_ref, w_ref, *refs):
    pieces, d_ref = refs[-6:-1], refs[-1]
    d_ref[...] = lax.dot_general(g_ref[...], w_ref[...], NT, preferred_element_type=F32).astype(BF16)
    for mask, (ref, at) in enumerate(outgoing(pieces)):
        ref[at : at + TILE, :] = d_ref[:, lanes_at(at_ref[1] ^ mask)]


def sigmoid(s):
    return pl.reciprocal(1.0 + jnp.exp2(s * (-SCALE * LOG2E)), approx=True)


def weigh(q, kt, v, mask):
    s = jnp.dot(q, kt, preferred_element_type=F32)
    w = jnp.where(mask, s * sigmoid(s), 0.0).astype(BF16)
    return jnp.dot(w, v, preferred_element_type=F32)


def fwd_own_kernel(lo_ref, nv_ref, act_ref, slope_ref, out_ref, kt_ref, qt_ref, slope_qt_ref):
    for t in range(TILES):
        rows = slice(t * TILE, (t + 1) * TILE)
        kt_ref[:, rows] = act_ref[rows, K].T
    row = lax.broadcasted_iota(jnp.int32, (TILE, CHUNK), 0)
    col = lax.broadcasted_iota(jnp.int32, (TILE, CHUNK), 1)

    def q_tile(t, carry):
        q = act_ref[rows_at(t), Q]

        def keys(at, size, acc):
            mask = from_start(t, lo_ref, at, col[:, :size], 1) & ((col - row)[:, :size] <= t * TILE - at)
            return acc + weigh(q, kt_ref[:, pl.ds(at, size)], act_ref[pl.ds(at, size), V], mask)

        first = jnp.maximum(lo_ref[2 * t], 0) // TILE
        acc = tiles_back(t, first, keys, jnp.zeros((TILE, HD), F32))
        out_ref[rows_at(t), :] = jnp.where(valid_rows(t, nv_ref), acc, 0.0)
        return carry

    lax.fori_loop(0, TILES, q_tile, 0)
    for t in range(TILES):
        rows = slice(t * TILE, (t + 1) * TILE)
        qt_ref[:, rows] = act_ref[rows, Q].T
        slope_qt_ref[:, rows] = slope_ref[rows, Q].T


def fwd_far_kernel(
    lo_ref, nv_ref, at_ref, act_ref, kva_ref, kvb_ref, near_ref, *refs,
):
    dg_refs, (out_ref, kv_ref, kt_ref, sum_ref, attn_s, dg_s) = refs[:5], refs[5:]
    head = at_ref[1]
    slot = 0
    for ref in (kva_ref, kvb_ref):
        for at in range(0, ref.shape[0], TILE):
            kv_ref[rows_at(slot ^ head), :] = ref[at : at + TILE, :]
            slot += 1
    for mask, (ref, at) in enumerate(places(dg_refs)):
        dg_s[rows_at(head ^ mask), :] = ref[at : at + TILE, :]
    first = jnp.minimum(lo_ref[0] + SPAN, SPAN) // CHUNK
    for t in range(TILES):
        rows = slice(t * TILE, (t + 1) * TILE)

        @pl.when(t // 2 >= first)
        def _():
            kt_ref[:, rows] = kv_ref[rows, HD:].T

    attn_s[...] = near_ref[...]
    col = lax.broadcasted_iota(jnp.int32, (TILE, CHUNK), 1)

    def q_tile(t, carry):
        q = act_ref[rows_at(t), Q]

        def k_chunk(c, acc):
            mask = from_start(t, lo_ref, c * CHUNK - SPAN, col, 1)
            return acc + weigh(q, kt_ref[:, chunk_at(c)], kv_ref[chunk_at(c), :HD], mask)

        start = (lo_ref[2 * t] + SPAN) // CHUNK
        acc = lax.fori_loop(start, CHUNKS, k_chunk, jnp.zeros((TILE, HD), F32))
        attn_s[rows_at(t), :] += jnp.where(valid_rows(t, nv_ref), acc, 0.0)
        return carry

    lax.fori_loop(0, far_tiles(lo_ref), q_tile, 0)
    ones = jnp.ones((8, HD), BF16)
    for t in range(TILES):
        rows = slice(t * TILE, (t + 1) * TILE)
        attn = attn_s[rows, :] * (SCALE / SPAN)
        out_ref[rows, :] = attn.astype(BF16)
        d_n = dg_s[rows, :].astype(F32) * act_ref[rows, U].astype(F32)
        square = lax.dot_general(ones, (attn * attn).astype(BF16), NT, preferred_element_type=F32)
        cross = lax.dot_general(ones, (attn * d_n).astype(BF16), NT, preferred_element_type=F32)
        sum_ref[t : t + 1, :] = square[:1]
        sum_ref[TILES + t : TILES + t + 1, :] = cross[:1]


def add_kernel(a_ref, b_ref, out_ref):
    out_ref[...] = a_ref[...] + b_ref[...]


def far_tiles(lo_ref):
    return sum((lo_ref[2 * t] < 0).astype(jnp.int32) for t in range(TILES))


def row_scales(sum_refs):
    width = HEADS * HD
    total = sum_refs[0][...]
    for ref in sum_refs[1:]:
        total += ref[...]
    r = lax.rsqrt(total[:TILES] * (1.0 / width) + eps)
    c = total[TILES:] * (1.0 / width) * r
    return jnp.concatenate([r, c], axis=0).T


def cotangent(t, scales, nv_ref, u, attn, d_gated):
    r, c = scales[:, t : t + 1], scales[:, TILES + t : TILES + t + 1]
    n = attn.astype(F32) * r
    g = r * (d_gated * u.astype(F32) - n * c)
    return n, jnp.where(valid_rows(t, nv_ref), g, 0.0).astype(BF16)


def back_scores(qt, k, v, gt, mask):
    s = jnp.dot(k, qt, preferred_element_type=F32)
    sig = jnp.where(mask, sigmoid(s), 0.0)
    dw = jnp.dot(v, gt, preferred_element_type=F32)
    ds = dw * sig * (1.0 + (s * SCALE) * (1.0 - sig))
    return (s * sig).astype(BF16), ds.astype(BF16)


def cotangent_kernel(nv_ref, at_ref, act_ref, slope_ref, attn_ref, *refs):
    sum_refs, dg_refs, (g_ref, cols_ref, dg_s) = refs[:4], refs[4:9], refs[-3:]
    for mask, (ref, at) in enumerate(places(dg_refs)):
        dg_s[rows_at(at_ref[1] ^ mask), :] = ref[at : at + TILE, :]
    scales = row_scales(sum_refs)
    for t in range(TILES):
        rows = slice(t * TILE, (t + 1) * TILE)
        d_gated = dg_s[rows, :].astype(F32)
        n, g = cotangent(t, scales, nv_ref, act_ref[rows, U], attn_ref[rows, :], d_gated)
        g_ref[rows, :] = g
        du = (d_gated * n).astype(BF16).astype(F32)
        cols_ref[:, rows] = (du * slope_ref[rows, U].astype(F32)).astype(BF16).T


def queries_kernel(lo_ref, act_ref, slope_qt_ref, qt_ref, kt_ref, g_ref, kv_ref, far_kt_ref, cols_ref, rows_ref, dkv_ref, gt_s):
    for t in range(TILES):
        rows = slice(t * TILE, (t + 1) * TILE)
        gt_s[:, rows] = g_ref[rows, :].T
    for c in range(CHUNKS):
        dkv_ref[c * CHUNK : (c + 1) * CHUNK, :] = jnp.zeros((CHUNK, 2 * HD), F32)
    key = lax.broadcasted_iota(jnp.int32, (CHUNK, TILE), 0)
    query = lax.broadcasted_iota(jnp.int32, (CHUNK, TILE), 1)

    def q_tile(t, carry):
        q, qt = act_ref[rows_at(t), Q], qt_ref[:, rows_at(t)]
        g, gt = g_ref[rows_at(t), :], gt_s[:, rows_at(t)]

        def far_chunk(c, dqt):
            at = chunk_at(c)
            mask = from_start(t, lo_ref, c * CHUNK - SPAN, key, 0)
            ds = back_scores(qt, kv_ref[at, HD:], kv_ref[at, :HD], gt, mask)[1]
            return dqt + jnp.dot(far_kt_ref[:, at], ds, preferred_element_type=F32)

        def keys(start, size, dqt):
            at = pl.ds(start, size)
            mask = from_start(t, lo_ref, start, key[:size], 0) & ((key - query)[:size] <= t * TILE - start)
            w, ds = back_scores(qt, act_ref[at, K], act_ref[at, V], gt, mask)
            dkv_ref[at, :HD] += jnp.dot(w, g, preferred_element_type=F32)
            dkv_ref[at, HD:] += jnp.dot(ds, q, preferred_element_type=F32)
            return dqt + jnp.dot(kt_ref[:, at], ds, preferred_element_type=F32)

        first = lo_ref[2 * t]
        start = jnp.minimum(first + SPAN, SPAN) // CHUNK
        dqt = lax.fori_loop(start, CHUNKS, far_chunk, jnp.zeros((HD, TILE), F32))
        dqt = tiles_back(t, jnp.maximum(first, 0) // TILE, keys, dqt)
        dq = (dqt * (SCALE / SPAN)).astype(BF16).astype(F32)
        dq = (dq * slope_qt_ref[:, rows_at(t)].astype(F32)).astype(BF16)
        cols_ref[:, rows_at(t)] = dq
        rows_ref[rows_at(t), :] = dq.T
        return carry

    lax.fori_loop(0, TILES, q_tile, 0)


def keys_kernel(
    groups, lo_ref, at_ref, own_ref, act_ref, slope_ref, q_ref, g_ref, u_cols_ref, q_cols_ref, dq_ref, attn_ref, normed_ref, *refs
):
    pieces, shares, (cols_s, all_s, acc_s) = refs[:5], refs[5:-3], refs[-3:]
    first = jnp.minimum(lo_ref[2 * TILES], SPAN) // CHUNK
    key = lax.broadcasted_iota(jnp.int32, (CHUNK, TILE), 0)

    def clear(c, carry):
        acc_s[chunk_at(c), :] = jnp.zeros((CHUNK, 2 * HD), F32)
        return carry

    lax.fori_loop(first, CHUNKS, clear, 0)

    def q_tile(t, carry):
        q, g = q_ref[rows_at(t), :], g_ref[rows_at(t), :]
        qt, gt = q.T, g.T

        def k_chunk(c, carry):
            at = chunk_at(c)
            mask = from_start(TILES + t, lo_ref, c * CHUNK, key, 0)
            w, ds = back_scores(qt, act_ref[at, K], act_ref[at, V], gt, mask)
            acc_s[at, :HD] += jnp.dot(w, g, preferred_element_type=F32)
            acc_s[at, HD:] += jnp.dot(ds, q, preferred_element_type=F32)
            return carry

        return lax.fori_loop(lo_ref[2 * (TILES + t)] // CHUNK, CHUNKS, k_chunk, carry)

    count = sum((lo_ref[2 * (TILES + t)] < SPAN).astype(jnp.int32) for t in range(TILES))
    lax.fori_loop(0, count, q_tile, 0)
    for mask, (ref, at) in enumerate(outgoing(pieces)):
        t = at_ref[1] ^ mask
        rows = rows_at(t)
        d = own_ref[rows, :] + jnp.where(t // 2 >= first, acc_s[rows, :], 0.0)
        d = (d * (SCALE / SPAN)).astype(BF16).astype(F32)
        d = (d * slope_ref[rows, VK].astype(F32)).astype(BF16)
        ref[at : at + TILE, :HD] = attn_ref[rows, :]
        ref[at : at + TILE, HD : 2 * HD] = dq_ref[rows, :]
        ref[at : at + TILE, 2 * HD :] = d
        cols_s[:, rows] = d.T
    share = jnp.dot(cols_s[...], normed_ref[...], preferred_element_type=F32).astype(BF16)
    all_s[HD : 2 * HD, :], all_s[3 * HD :, :] = share[:HD], share[HD:]
    all_s[:HD, :] = jnp.dot(u_cols_ref[...], normed_ref[...], preferred_element_type=F32).astype(BF16)
    all_s[2 * HD : 3 * HD, :] = jnp.dot(q_cols_ref[...], normed_ref[...], preferred_element_type=F32).astype(BF16)
    size = 4 * HD // groups
    for mask in range(groups):
        at = pl.multiple_of((at_ref[0] ^ mask) * size, size)
        shares[mask][...] = all_s[pl.ds(at, size), :]


def assemble(at_ref, refs, part, out_s):
    for mask, (ref, at) in enumerate(places(refs)):
        out_s[:, lanes_at(at_ref[1] ^ mask)] = ref[at : at + TILE, part * HD : (part + 1) * HD]


def branch_rows(at_ref, refs, w_ref, distances, row_s):
    width, total = w_ref.shape[0], 0.0
    for part, branch in ((1, 2), (2, 1), (3, 3)):
        assemble(at_ref, refs, part, row_s)
        for i in distances:
            at = ((at_ref[1] // 2) ^ i) * 2 * HD
            x = row_s[:, pl.ds(pl.multiple_of(at, 2 * HD), 2 * HD)]
            w = w_ref[:, pl.ds(pl.multiple_of(branch * width + at, 2 * HD), 2 * HD)]
            total += lax.dot_general(x, w, NT, preferred_element_type=F32)
    return total


def through(x, w_ref, branch):
    width = w_ref.shape[0]
    return lax.dot_general(x, w_ref[:, branch * width : (branch + 1) * width], NT, preferred_element_type=F32)


def branches_kernel(at_ref, *refs):
    pieces, (w_in_ref, dn_ref, row_s) = refs[:-3], refs[-3:]
    dn_ref[...] = branch_rows(at_ref, pieces, w_in_ref, (0, 1, 2), row_s)


def own_u_kernel(tokens_ref, w_in_ref, after_ref, u_ref, slope_ref):
    xn = norm_rows(tokens_ref[...].astype(F32)).astype(BF16)
    pre = jnp.dot(xn, w_in_ref[:, : tokens_ref.shape[1]], preferred_element_type=F32)
    u_ref[...], slope_ref[...] = silu_and_slope(pre)


def rows_kernel(at_ref, *refs):
    pieces, (dn_ref, dg_ref, u_ref, slope_ref, tokens_ref, grad_ref, w_out_ref, w_in_ref) = refs[:5], refs[5:-4]
    out_ref, dx_ref, row_s = refs[-3:]
    x = tokens_ref[...].astype(F32)
    assemble(at_ref, pieces, 0, row_s)
    attn_n = norm_rows(row_s[...].astype(F32))
    gated = (attn_n * u_ref[...].astype(F32)).astype(BF16)
    y = jnp.dot(gated, w_out_ref[...], preferred_element_type=F32)
    out_ref[...] = (x + y).astype(BF16)
    du = (dg_ref[...].astype(F32) * attn_n).astype(BF16).astype(F32)
    du = (du * slope_ref[...].astype(F32)).astype(BF16)
    dn = dn_ref[...] + through(du, w_in_ref, 0) + branch_rows(at_ref, pieces, w_in_ref, (3,), row_s)
    r = lax.rsqrt(jnp.mean(x * x, axis=-1, keepdims=True) + eps)
    n = x * r
    dx = r * (dn - n * jnp.mean(dn * n, axis=-1, keepdims=True))
    dx_ref[...] = (grad_ref[...].astype(F32) + dx).astype(BF16)


def sum_kernel(groups, *refs):
    total = refs[0][...].astype(F32)
    for ref in refs[1:groups]:
        total += ref[...].astype(F32)
    refs[-2][...] = total
    refs[-1][...] = jnp.zeros(refs[-1].shape, F32)


def call(kernel, scalars, arrays, outs, scratch=(), after=(), aliases=None, limit=16, sems=0):
    smem = pl.BlockSpec(memory_space=pltpu.SMEM)
    vmem = pl.BlockSpec(memory_space=pltpu.VMEM)
    anywhere = pl.BlockSpec(memory_space=pl.ANY)
    return pl.pallas_call(
        kernel,
        out_shape=[jax.ShapeDtypeStruct(*out) for out in outs],
        in_specs=[smem] * len(scalars) + [vmem] * len(arrays) + [anywhere] * len(after),
        out_specs=[smem if out[1] == jnp.int32 else vmem for out in outs],
        scratch_shapes=[pltpu.VMEM(*shape) for shape in scratch] + ([pltpu.SemaphoreType.DMA((sems,))] if sems else []),
        input_output_aliases=aliases or {},
        compiler_params=pltpu.CompilerParams(vmem_limit_bytes=limit * 2**20),
        cost_estimate=pl.CostEstimate(flops=0, bytes_accessed=0, transcendentals=0),
    )(*scalars, *arrays, *after)


def per_device(groups, tokens, w_in, w_out, block_counts, tails, grad_out):
    count, width = tokens.shape
    own, tall, wide, tall_t = (count, width), (SPAN, HD), (SPAN, 2 * HD), (HD, SPAN)
    piece, half, sums_shape = (count, HD), (BLK, width), (2 * TILES, TILE)

    def swap(x, mask):
        return lax.ppermute(x, "h", [(i, i ^ mask) for i in range(HEADS)])

    def onward(x):
        return lax.ppermute(x, "g", [(i, i + 1) for i in range(groups - 1)])

    def backward(x):
        return lax.ppermute(x, "g", [(i + 1, i) for i in range(groups - 1)])

    def trade(pieces, after=()):
        mine, other, *pairs = pieces
        other = swap(other, 1)
        pairs = call(
            merge_kernel,
            (),
            (other,),
            [(x.shape, BF16) for x in pairs],
            after=(*pairs, *after),
            aliases={1: 0, 2: 1, 3: 2},
            limit=4,
        )
        return [mine, other] + [swap(x, mask) for x, mask in zip(pairs, (2, 4, 6))]

    x_rows, y_rows = swap(tokens, 2), swap(tokens, 4)
    other = swap(tokens, 1)
    *info, w_head = call(
        start_kernel,
        (block_counts, tails),
        (),
        [((2 * MAXB,), jnp.int32)] * 2 + [((2,), jnp.int32), ((width, 4 * HD), BF16)],
        after=(w_in,),
        limit=51,
        sems=4,
    )
    *kept, kv = project(info, (0, 1), ((tokens,), (other,)), w_head, ())
    *dg_pieces, dg_own = call(
        d_gated_kernel, info[2:], (grad_out, w_out), trade_outs(HD) + [(own, BF16)], after=(kv,)
    )
    x_rows, y_rows, x_half, y_half = call(
        cut_kernel,
        (),
        (x_rows, y_rows),
        [(own, BF16), (own, BF16), (half, BF16), (half, BF16)],
        after=(kv, dg_own),
        aliases={0: 0, 1: 1},
        limit=4,
    )
    corner = swap(x_half, 4), swap(y_half, 2)
    chunks = ((x_rows,), (swap(x_rows, 1),), (y_rows,), (swap(y_rows, 1),))
    *kept, kv = project(info, (2, 3, 4, 5), chunks, w_head, kept, kv=kv)
    far_kv = [onward(kv)]
    corner = call(gate_kernel, (), (), [(half, BF16), (half, BF16)], after=(*corner, kv), aliases={0: 0, 1: 1}, limit=4)
    *kept, kv, q = project(info, (6, 7), (corner, [swap(x, 1) for x in corner]), w_head, kept, True)
    far_kv.append(onward(kv))
    q_next = backward(q)
    normed, act, slope = kept
    d_gated = trade(dg_pieces, (kv,))

    near, kt, qt, slope_qt = call(fwd_own_kernel, info[:2], (act, slope), [(tall, F32)] + [(tall_t, BF16)] * 3)
    attn, kv, far_kt, sums = call(
        fwd_far_kernel,
        info,
        (act, *far_kv, near, *d_gated),
        [(tall, BF16), (wide, BF16), (tall_t, BF16), (sums_shape, F32)],
        [(tall, F32), (tall, BF16)],
    )
    sums = call(add_kernel, (), (sums, swap(sums, 1)), [(sums_shape, F32)], limit=4)[0]
    sums = [sums] + [swap(sums, mask) for mask in (2, 4, 6)]

    g, u_cols = call(
        cotangent_kernel,
        info[1:],
        (act, slope, attn, *sums, *d_gated),
        [(tall, BF16), (tall_t, BF16)],
        [(tall, BF16)],
        (q_next,),
    )
    g_next = backward(g)
    q_cols, d_q, dkv = call(
        queries_kernel,
        info[:1],
        (act, slope_qt, qt, kt, g, kv, far_kt),
        [(tall_t, BF16), (tall, BF16), (wide, F32)],
        [(tall_t, BF16)],
    )
    rows, cols = 4 * HD // groups, 4 * HD
    outs = call(
        functools.partial(keys_kernel, groups),
        (info[0], info[2]),
        (dkv, act, slope, q_next, g_next, u_cols, q_cols, d_q, attn, normed),
        trade_outs(cols) + [((rows, width), BF16)] * groups,
        [((2 * HD, SPAN), BF16), ((4 * HD, width), BF16), (wide, F32)],
    )
    shares = [outs[5]] + [
        lax.ppermute(outs[5 + mask], "g", [(i, i ^ mask) for i in range(groups)]) for mask in range(1, groups)
    ]
    pieces = trade(outs[:5])
    u, slope_u = call(own_u_kernel, (), (tokens, w_in), [(own, BF16), (own, BF16)], after=(outs[0],))
    grad_w_in, end = call(
        functools.partial(sum_kernel, groups), (), tuple(shares[::-1]), [((rows, width), F32), ((8, HD), F32)]
    )
    d_normed = call(branches_kernel, info[2:], (*pieces[:4], w_in), [(own, F32)], [(own, BF16)])[0]
    layer_out, grad_tokens = call(
        rows_kernel,
        info[2:],
        (*pieces, d_normed, dg_own, u, slope_u, tokens, grad_out, w_out, w_in),
        [(own, BF16), (own, BF16)],
        [(own, BF16)],
        (end,),
    )
    parts = groups // 4
    if parts > 1:
        perm = [
            (i * HEADS + j, ((i // parts) * HEADS + j) * parts + i % parts)
            for i in range(groups)
            for j in range(HEADS)
        ]
        grad_w_in = lax.ppermute(grad_w_in, ("g", "h"), perm)
    return (layer_out, grad_tokens, grad_w_in)


def solution(mesh):
    groups = mesh.shape["seq"] // HEADS
    split = Mesh(mesh.devices.reshape(groups, HEADS), ("g", "h"))
    rows = P(("g", "h"), None)
    return jax.shard_map(
        functools.partial(per_device, groups),
        mesh=split,
        in_specs=(rows, P(), P(), P(), P(), rows),
        out_specs=(rows, rows, rows),
        check_vma=False,
    )
```

```python
import functools

import jax
import jax.numpy as jnp
from jax import lax
from jax.experimental import pallas as pl
from jax.experimental.pallas import tpu as pltpu
from jax.sharding import Mesh, PartitionSpec as P

HEADS = 8
HD = 128
BLK = 128
MAXB = 16
SPAN = MAXB * BLK
TILE = 256
TILES = SPAN // TILE
CHUNK = 512
CHUNKS = SPAN // CHUNK
SCALE = HD ** (-0.5)
LOG2E = 1.4426950408889634

eps = 1e-05

NT = (((1,), (1,)), ((), ()))
F32, BF16 = jnp.float32, jnp.bfloat16

U, Q, V, K = (slice(i * HD, (i + 1) * HD) for i in range(4))
PLACE = (0, 2, 1, 3)
UQ, VK = slice(0, 2 * HD), slice(2 * HD, 4 * HD)


def start_kernel(counts_ref, tails_ref, w_ref, lo_ref, nv_ref, at_ref, wh_ref, sems):
    group = lax.axis_index("g").astype(jnp.int32)
    at_ref[0] = group
    head = lax.axis_index("h").astype(jnp.int32)
    at_ref[1] = head
    copies = []
    for i in range(4):
        source = w_ref.at[:, lanes_at(PLACE[i] * (w_ref.shape[0] // HD) + head)]
        copies.append(pltpu.make_async_copy(source, wh_ref.at[:, i * HD : (i + 1) * HD], sems.at[i]))
        copies[i].start()
    base = group * MAXB
    for j in range(2 * MAXB):
        lo_ref[j] = j * BLK
        nv_ref[j] = BLK

    def user(n, start):
        end = start + counts_ref[n]

        def block(j, carry):
            lo_ref[j] = (start - base) * BLK
            nv_ref[j] = jnp.where(j == end - 1 - base, tails_ref[n], BLK)
            return carry

        lax.fori_loop(jnp.maximum(start - base, 0), jnp.minimum(end - base, 2 * MAXB), block, 0)
        return end

    lax.fori_loop(0, counts_ref.shape[0], user, jnp.int32(0))
    for copy in copies:
        copy.wait()


def by_half(t, ref, shape, dim):
    side = lax.broadcasted_iota(jnp.int32, shape, dim)
    return jnp.where(side < BLK, ref[2 * t], ref[2 * t + 1])


def from_start(t, lo_ref, at, keys, dim):
    parts = [part >= lo_ref[2 * t + i] - at for i, part in enumerate(jnp.split(keys, 2, axis=1 - dim))]
    return jnp.concatenate(parts, axis=1 - dim)


def valid_rows(t, nv_ref):
    row = lax.broadcasted_iota(jnp.int32, (TILE, 1), 0)
    return (row & (BLK - 1)) < by_half(t, nv_ref, (TILE, 1), 0)


def rows_at(t):
    return pl.ds(pl.multiple_of(t * TILE, TILE), TILE)


def chunk_at(c):
    return pl.ds(pl.multiple_of(c * CHUNK, CHUNK), CHUNK)


def tiles_back(t, first, step, carry):
    count = t - first + 1

    def pair(i, carry):
        return step(pl.multiple_of((t - 2 * i - 1) * TILE, TILE), 2 * TILE, carry)

    carry = lax.fori_loop(0, count // 2, pair, carry)
    return lax.fori_loop(0, count % 2, lambda i, c: step(pl.multiple_of(first * TILE, TILE), TILE, c), carry)


def lanes_at(i):
    return pl.ds(pl.multiple_of(i * HD, HD), HD)


def norm_rows(x):
    return x * lax.rsqrt(jnp.mean(x * x, axis=-1, keepdims=True) + eps)


def silu_and_slope(pre):
    s = 0.5 + 0.5 * jnp.tanh(0.5 * pre)
    return (pre * s).astype(BF16), (s * (1.0 + pre * (1.0 - s))).astype(BF16)


def store_rows(x, place, wh_ref, normed_ref, act_ref, slope_ref, kv_ref, i):
    rows = rows_at(place)
    xn = norm_rows(x.astype(F32)).astype(BF16)
    normed_ref[rows, :] = xn
    act, slope = silu_and_slope(jnp.dot(xn, wh_ref[...], preferred_element_type=F32))
    act_ref[rows, :] = act
    slope_ref[rows, :] = slope
    kv_ref[i * TILE : (i + 1) * TILE, :] = act[:, VK]


def proj_kernel(masks, pieces, last, ahead, at_ref, *refs):
    x_refs, wh_ref = refs[: sum(pieces)], refs[sum(pieces)]
    outs = refs[-5:-1] if last else refs[-4:]
    if ahead:
        outs[3][: ahead * TILE, :] = refs[sum(pieces) + 1][...]
    for i, mask in enumerate(masks):
        parts = [ref[...] for ref in x_refs[sum(pieces[:i]) : sum(pieces[: i + 1])]]
        x = parts[0] if len(parts) == 1 else jnp.concatenate(parts, axis=0)
        store_rows(x, at_ref[1] ^ mask, wh_ref, *outs, ahead + i)
    if last:
        refs[-1][...] = outs[1][:, Q]


def proj_outs(width, n):
    return [((SPAN, width), BF16), ((SPAN, 4 * HD), BF16), ((SPAN, 4 * HD), BF16), ((n * TILE, 2 * HD), BF16)]


def project(info, masks, chunks, w, kept, last=False, kv=None):
    pieces = tuple(len(chunk) for chunk in chunks)
    flat = [piece for chunk in chunks for piece in chunk]
    lead = () if kv is None else (kv,)
    ahead = 0 if kv is None else kv.shape[0] // TILE
    start = 2 + len(flat) + len(lead)
    return call(
        functools.partial(proj_kernel, masks, pieces, last, ahead),
        (info[2],),
        (*flat, w, *lead),
        proj_outs(w.shape[0], ahead + len(masks)) + ([((SPAN, HD), BF16)] if last else []),
        after=kept,
        aliases={start + i: i for i in range(len(kept))},
    )


def cut_kernel(x_ref, y_ref, *refs):
    x_half, y_half = refs[-2:]
    x_half[...] = x_ref[:BLK, :]
    y_half[...] = y_ref[BLK:, :]


def gate_kernel(*refs):
    pass


def merge_kernel(other_ref, *refs):
    for i, ref in enumerate(refs[-3:]):
        ref[TILE:, :] = other_ref[(i + 1) * TILE : (i + 2) * TILE, :]


def places(refs):
    mine, other, *pairs = refs
    return [(mine, 0), (other, 0)] + [(ref, at) for ref in pairs for at in (0, TILE)]


def outgoing(refs):
    mine, other, *pairs = refs
    found = [(mine, 0)] * HEADS
    for i in range(4):
        found[2 * i + 1] = other, i * TILE
    for i in range(3):
        found[2 * i + 2] = pairs[i], 0
    return found


def trade_outs(cols):
    return [((TILE, cols), BF16), ((4 * TILE, cols), BF16)] + [((2 * TILE, cols), BF16)] * 3


def d_gated_kernel(at_ref, g_ref, w_ref, *refs):
    pieces, d_ref = refs[-6:-1], refs[-1]
    d_ref[...] = lax.dot_general(g_ref[...], w_ref[...], NT, preferred_element_type=F32).astype(BF16)
    for mask, (ref, at) in enumerate(outgoing(pieces)):
        ref[at : at + TILE, :] = d_ref[:, lanes_at(at_ref[1] ^ mask)]


def sigmoid(s):
    return pl.reciprocal(1.0 + jnp.exp2(s * (-SCALE * LOG2E)), approx=True)


def weigh(q, kt, v, mask):
    s = jnp.dot(q, kt, preferred_element_type=F32)
    w = jnp.where(mask, s * sigmoid(s), 0.0).astype(BF16)
    return jnp.dot(w, v, preferred_element_type=F32)


def fwd_own_kernel(lo_ref, nv_ref, act_ref, slope_ref, out_ref, kt_ref, qt_ref, slope_qt_ref):
    for t in range(TILES):
        rows = slice(t * TILE, (t + 1) * TILE)
        kt_ref[:, rows] = act_ref[rows, K].T
    row = lax.broadcasted_iota(jnp.int32, (TILE, CHUNK), 0)
    col = lax.broadcasted_iota(jnp.int32, (TILE, CHUNK), 1)

    def q_tile(t, carry):
        q = act_ref[rows_at(t), Q]

        def keys(at, size, acc):
            mask = from_start(t, lo_ref, at, col[:, :size], 1) & ((col - row)[:, :size] <= t * TILE - at)
            return acc + weigh(q, kt_ref[:, pl.ds(at, size)], act_ref[pl.ds(at, size), V], mask)

        first = jnp.maximum(lo_ref[2 * t], 0) // TILE
        acc = tiles_back(t, first, keys, jnp.zeros((TILE, HD), F32))
        out_ref[rows_at(t), :] = jnp.where(valid_rows(t, nv_ref), acc, 0.0)
        return carry

    lax.fori_loop(0, TILES, q_tile, 0)
    for t in range(TILES):
        rows = slice(t * TILE, (t + 1) * TILE)
        qt_ref[:, rows] = act_ref[rows, Q].T
        slope_qt_ref[:, rows] = slope_ref[rows, Q].T


def fwd_far_kernel(
    lo_ref, nv_ref, at_ref, act_ref, kva_ref, kvb_ref, near_ref, *refs,
):
    dg_refs, (out_ref, kv_ref, kt_ref, sum_ref, attn_s, dg_s) = refs[:5], refs[5:]
    head = at_ref[1]
    slot = 0
    for ref in (kva_ref, kvb_ref):
        for at in range(0, ref.shape[0], TILE):
            kv_ref[rows_at(slot ^ head), :] = ref[at : at + TILE, :]
            slot += 1
    for mask, (ref, at) in enumerate(places(dg_refs)):
        dg_s[rows_at(head ^ mask), :] = ref[at : at + TILE, :]
    first = jnp.minimum(lo_ref[0] + SPAN, SPAN) // CHUNK
    for t in range(TILES):
        rows = slice(t * TILE, (t + 1) * TILE)

        @pl.when(t // 2 >= first)
        def _():
            kt_ref[:, rows] = kv_ref[rows, HD:].T

    attn_s[...] = near_ref[...]
    col = lax.broadcasted_iota(jnp.int32, (TILE, CHUNK), 1)

    def q_tile(t, carry):
        q = act_ref[rows_at(t), Q]

        def k_chunk(c, acc):
            mask = from_start(t, lo_ref, c * CHUNK - SPAN, col, 1)
            return acc + weigh(q, kt_ref[:, chunk_at(c)], kv_ref[chunk_at(c), :HD], mask)

        start = (lo_ref[2 * t] + SPAN) // CHUNK
        acc = lax.fori_loop(start, CHUNKS, k_chunk, jnp.zeros((TILE, HD), F32))
        attn_s[rows_at(t), :] += jnp.where(valid_rows(t, nv_ref), acc, 0.0)
        return carry

    lax.fori_loop(0, far_tiles(lo_ref), q_tile, 0)
    ones = jnp.ones((8, HD), BF16)
    for t in range(TILES):
        rows = slice(t * TILE, (t + 1) * TILE)
        attn = attn_s[rows, :] * (SCALE / SPAN)
        out_ref[rows, :] = attn.astype(BF16)
        d_n = dg_s[rows, :].astype(F32) * act_ref[rows, U].astype(F32)
        square = lax.dot_general(ones, (attn * attn).astype(BF16), NT, preferred_element_type=F32)
        cross = lax.dot_general(ones, (attn * d_n).astype(BF16), NT, preferred_element_type=F32)
        sum_ref[t : t + 1, :] = square[:1]
        sum_ref[TILES + t : TILES + t + 1, :] = cross[:1]


def add_kernel(a_ref, b_ref, out_ref):
    out_ref[...] = (a_ref[...].astype(F32) + b_ref[...].astype(F32)).astype(out_ref.dtype)


def far_tiles(lo_ref):
    return sum((lo_ref[2 * t] < 0).astype(jnp.int32) for t in range(TILES))


def row_scales(sum_refs):
    width = HEADS * HD
    total = sum_refs[0][...]
    for ref in sum_refs[1:]:
        total += ref[...]
    r = lax.rsqrt(total[:TILES] * (1.0 / width) + eps)
    c = total[TILES:] * (1.0 / width) * r
    return jnp.concatenate([r, c], axis=0).T


def cotangent(t, scales, nv_ref, u, attn, d_gated):
    r, c = scales[:, t : t + 1], scales[:, TILES + t : TILES + t + 1]
    n = attn.astype(F32) * r
    g = r * (d_gated * u.astype(F32) - n * c)
    return n, jnp.where(valid_rows(t, nv_ref), g, 0.0).astype(BF16)


def back_scores(qt, k, v, gt, mask):
    s = jnp.dot(k, qt, preferred_element_type=F32)
    sig = jnp.where(mask, sigmoid(s), 0.0)
    dw = jnp.dot(v, gt, preferred_element_type=F32)
    ds = dw * sig * (1.0 + (s * SCALE) * (1.0 - sig))
    return (s * sig).astype(BF16), ds.astype(BF16)


def cotangent_kernel(nv_ref, at_ref, act_ref, slope_ref, attn_ref, *refs):
    sum_refs, dg_refs, (g_ref, cols_ref, dg_s) = refs[:4], refs[4:9], refs[-3:]
    for mask, (ref, at) in enumerate(places(dg_refs)):
        dg_s[rows_at(at_ref[1] ^ mask), :] = ref[at : at + TILE, :]
    scales = row_scales(sum_refs)
    for t in range(TILES):
        rows = slice(t * TILE, (t + 1) * TILE)
        d_gated = dg_s[rows, :].astype(F32)
        n, g = cotangent(t, scales, nv_ref, act_ref[rows, U], attn_ref[rows, :], d_gated)
        g_ref[rows, :] = g
        du = (d_gated * n).astype(BF16).astype(F32)
        cols_ref[:, rows] = (du * slope_ref[rows, U].astype(F32)).astype(BF16).T


def queries_kernel(lo_ref, act_ref, slope_qt_ref, qt_ref, kt_ref, g_ref, kv_ref, far_kt_ref, cols_ref, rows_ref, dkv_ref, gt_s):
    for t in range(TILES):
        rows = slice(t * TILE, (t + 1) * TILE)
        gt_s[:, rows] = g_ref[rows, :].T
    for c in range(CHUNKS):
        dkv_ref[c * CHUNK : (c + 1) * CHUNK, :] = jnp.zeros((CHUNK, 2 * HD), F32)
    key = lax.broadcasted_iota(jnp.int32, (CHUNK, TILE), 0)
    query = lax.broadcasted_iota(jnp.int32, (CHUNK, TILE), 1)

    def q_tile(t, carry):
        q, qt = act_ref[rows_at(t), Q], qt_ref[:, rows_at(t)]
        g, gt = g_ref[rows_at(t), :], gt_s[:, rows_at(t)]

        def far_chunk(c, dqt):
            at = chunk_at(c)
            mask = from_start(t, lo_ref, c * CHUNK - SPAN, key, 0)
            ds = back_scores(qt, kv_ref[at, HD:], kv_ref[at, :HD], gt, mask)[1]
            return dqt + jnp.dot(far_kt_ref[:, at], ds, preferred_element_type=F32)

        def keys(start, size, dqt):
            at = pl.ds(start, size)
            mask = from_start(t, lo_ref, start, key[:size], 0) & ((key - query)[:size] <= t * TILE - start)
            w, ds = back_scores(qt, act_ref[at, K], act_ref[at, V], gt, mask)
            dkv_ref[at, :HD] += jnp.dot(w, g, preferred_element_type=F32)
            dkv_ref[at, HD:] += jnp.dot(ds, q, preferred_element_type=F32)
            return dqt + jnp.dot(kt_ref[:, at], ds, preferred_element_type=F32)

        first = lo_ref[2 * t]
        start = jnp.minimum(first + SPAN, SPAN) // CHUNK
        dqt = lax.fori_loop(start, CHUNKS, far_chunk, jnp.zeros((HD, TILE), F32))
        dqt = tiles_back(t, jnp.maximum(first, 0) // TILE, keys, dqt)
        dq = (dqt * (SCALE / SPAN)).astype(BF16).astype(F32)
        dq = (dq * slope_qt_ref[:, rows_at(t)].astype(F32)).astype(BF16)
        cols_ref[:, rows_at(t)] = dq
        rows_ref[rows_at(t), :] = dq.T
        return carry

    lax.fori_loop(0, TILES, q_tile, 0)


def keys_kernel(
    groups, lo_ref, at_ref, own_ref, act_ref, slope_ref, q_ref, g_ref, u_cols_ref, q_cols_ref, dq_ref, attn_ref, normed_ref, *refs
):
    pieces, shares, (cols_s, all_s, acc_s) = refs[:5], refs[5:-3], refs[-3:]
    first = jnp.minimum(lo_ref[2 * TILES], SPAN) // CHUNK
    key = lax.broadcasted_iota(jnp.int32, (CHUNK, TILE), 0)

    def clear(c, carry):
        acc_s[chunk_at(c), :] = jnp.zeros((CHUNK, 2 * HD), F32)
        return carry

    lax.fori_loop(first, CHUNKS, clear, 0)

    def q_tile(t, carry):
        q, g = q_ref[rows_at(t), :], g_ref[rows_at(t), :]
        qt, gt = q.T, g.T

        def k_chunk(c, carry):
            at = chunk_at(c)
            mask = from_start(TILES + t, lo_ref, c * CHUNK, key, 0)
            w, ds = back_scores(qt, act_ref[at, K], act_ref[at, V], gt, mask)
            acc_s[at, :HD] += jnp.dot(w, g, preferred_element_type=F32)
            acc_s[at, HD:] += jnp.dot(ds, q, preferred_element_type=F32)
            return carry

        return lax.fori_loop(lo_ref[2 * (TILES + t)] // CHUNK, CHUNKS, k_chunk, carry)

    count = sum((lo_ref[2 * (TILES + t)] < SPAN).astype(jnp.int32) for t in range(TILES))
    lax.fori_loop(0, count, q_tile, 0)
    for mask, (ref, at) in enumerate(outgoing(pieces)):
        t = at_ref[1] ^ mask
        rows = rows_at(t)
        d = own_ref[rows, :] + jnp.where(t // 2 >= first, acc_s[rows, :], 0.0)
        d = (d * (SCALE / SPAN)).astype(BF16).astype(F32)
        d = (d * slope_ref[rows, VK].astype(F32)).astype(BF16)
        ref[at : at + TILE, :HD] = attn_ref[rows, :]
        ref[at : at + TILE, HD : 2 * HD] = dq_ref[rows, :]
        ref[at : at + TILE, 2 * HD :] = d
        cols_s[:, rows] = d.T
    share = jnp.dot(cols_s[...], normed_ref[...], preferred_element_type=F32).astype(BF16)
    all_s[HD : 2 * HD, :], all_s[3 * HD :, :] = share[:HD], share[HD:]
    all_s[:HD, :] = jnp.dot(u_cols_ref[...], normed_ref[...], preferred_element_type=F32).astype(BF16)
    all_s[2 * HD : 3 * HD, :] = jnp.dot(q_cols_ref[...], normed_ref[...], preferred_element_type=F32).astype(BF16)
    size = 4 * HD // groups
    for mask in range(groups):
        at = pl.multiple_of((at_ref[0] ^ mask) * size, size)
        part = all_s[pl.ds(at, size), :]
        if groups == 4:
            ref, half = shares[mask % 2], mask // 2 * size
            ref[half : half + size, :] = part.astype(ref.dtype)
        else:
            shares[mask][...] = part


def assemble(at_ref, refs, part, out_s):
    for mask, (ref, at) in enumerate(places(refs)):
        out_s[:, lanes_at(at_ref[1] ^ mask)] = ref[at : at + TILE, part * HD : (part + 1) * HD]


def branch_rows(at_ref, refs, w_ref, distances, row_s):
    width, total = w_ref.shape[0], 0.0
    for part, branch in ((1, 2), (2, 1), (3, 3)):
        assemble(at_ref, refs, part, row_s)
        for i in distances:
            at = ((at_ref[1] // 2) ^ i) * 2 * HD
            x = row_s[:, pl.ds(pl.multiple_of(at, 2 * HD), 2 * HD)]
            w = w_ref[:, pl.ds(pl.multiple_of(branch * width + at, 2 * HD), 2 * HD)]
            total += lax.dot_general(x, w, NT, preferred_element_type=F32)
    return total


def through(x, w_ref, branch):
    width = w_ref.shape[0]
    return lax.dot_general(x, w_ref[:, branch * width : (branch + 1) * width], NT, preferred_element_type=F32)


def branches_kernel(at_ref, *refs):
    pieces, (w_in_ref, dn_ref, row_s) = refs[:4], refs[4:]
    dn_ref[...] = branch_rows(at_ref, pieces, w_in_ref, (0, 1, 2), row_s)


def own_u_kernel(tokens_ref, w_in_ref, after_ref, u_ref, slope_ref):
    xn = norm_rows(tokens_ref[...].astype(F32)).astype(BF16)
    pre = jnp.dot(xn, w_in_ref[:, : tokens_ref.shape[1]], preferred_element_type=F32)
    u_ref[...], slope_ref[...] = silu_and_slope(pre)


def rows_kernel(at_ref, *refs):
    pieces, (dn_ref, dg_ref, u_ref, slope_ref, tokens_ref, grad_ref, w_out_ref, w_in_ref) = refs[:5], refs[5:-4]
    out_ref, dx_ref, end_ref, row_s = refs[-4:]
    end_ref[...] = jnp.zeros(end_ref.shape, F32)
    x = tokens_ref[...].astype(F32)
    assemble(at_ref, pieces, 0, row_s)
    attn_n = norm_rows(row_s[...].astype(F32))
    gated = (attn_n * u_ref[...].astype(F32)).astype(BF16)
    y = jnp.dot(gated, w_out_ref[...], preferred_element_type=F32)
    out_ref[...] = (x + y).astype(BF16)
    du = (dg_ref[...].astype(F32) * attn_n).astype(BF16).astype(F32)
    du = (du * slope_ref[...].astype(F32)).astype(BF16)
    dn = dn_ref[...] + through(du, w_in_ref, 0) + branch_rows(at_ref, pieces, w_in_ref, (3,), row_s)
    r = lax.rsqrt(jnp.mean(x * x, axis=-1, keepdims=True) + eps)
    n = x * r
    dx = r * (dn - n * jnp.mean(dn * n, axis=-1, keepdims=True))
    dx_ref[...] = (grad_ref[...].astype(F32) + dx).astype(BF16)


def half_kernel(keep_ref, got_ref, mine_ref, send_ref):
    size = mine_ref.shape[0]
    mine_ref[...] = keep_ref[:size, :] + got_ref[:size, :].astype(F32)
    send_ref[...] = (keep_ref[size:, :] + got_ref[size:, :].astype(F32)).astype(BF16)


def sum_kernel(*refs):
    total = refs[0][...].astype(F32)
    for ref in refs[1:-2]:
        total += ref[...].astype(F32)
    refs[-1][...] = total


def call(kernel, scalars, arrays, outs, scratch=(), after=(), aliases=None, limit=16, sems=0):
    smem = pl.BlockSpec(memory_space=pltpu.SMEM)
    vmem = pl.BlockSpec(memory_space=pltpu.VMEM)
    anywhere = pl.BlockSpec(memory_space=pl.ANY)
    return pl.pallas_call(
        kernel,
        out_shape=[jax.ShapeDtypeStruct(*out) for out in outs],
        in_specs=[smem] * len(scalars) + [vmem] * len(arrays) + [anywhere] * len(after),
        out_specs=[smem if out[1] == jnp.int32 else vmem for out in outs],
        scratch_shapes=[pltpu.VMEM(*shape) for shape in scratch] + ([pltpu.SemaphoreType.DMA((sems,))] if sems else []),
        input_output_aliases=aliases or {},
        compiler_params=pltpu.CompilerParams(vmem_limit_bytes=limit * 2**20),
        cost_estimate=pl.CostEstimate(flops=0, bytes_accessed=0, transcendentals=0),
    )(*scalars, *arrays, *after)


def per_device(groups, tokens, w_in, w_out, block_counts, tails, grad_out):
    count, width = tokens.shape
    own, tall, wide, tall_t = (count, width), (SPAN, HD), (SPAN, 2 * HD), (HD, SPAN)
    piece, half, sums_shape = (count, HD), (BLK, width), (2 * TILES, TILE)

    def swap(x, mask):
        return lax.ppermute(x, "h", [(i, i ^ mask) for i in range(HEADS)])

    def onward(x):
        return lax.ppermute(x, "g", [(i, i + 1) for i in range(groups - 1)])

    def backward(x):
        return lax.ppermute(x, "g", [(i + 1, i) for i in range(groups - 1)])

    def trade(pieces, after=()):
        mine, other, *pairs = pieces
        other = swap(other, 1)
        pairs = call(
            merge_kernel,
            (),
            (other,),
            [(x.shape, BF16) for x in pairs],
            after=(*pairs, *after),
            aliases={1: 0, 2: 1, 3: 2},
            limit=4,
        )
        return [mine, other] + [swap(x, mask) for x, mask in zip(pairs, (2, 4, 6))]

    x_rows, y_rows = swap(tokens, 2), swap(tokens, 4)
    other = swap(tokens, 1)
    *info, w_head = call(
        start_kernel,
        (block_counts, tails),
        (),
        [((2 * MAXB,), jnp.int32)] * 2 + [((2,), jnp.int32), ((width, 4 * HD), BF16)],
        after=(w_in,),
        limit=51,
        sems=4,
    )
    *kept, kv = project(info, (0, 1), ((tokens,), (other,)), w_head, ())
    *dg_pieces, dg_own = call(
        d_gated_kernel, info[2:], (grad_out, w_out), trade_outs(HD) + [(own, BF16)], after=(kv,)
    )
    x_rows, y_rows, x_half, y_half = call(
        cut_kernel,
        (),
        (x_rows, y_rows),
        [(own, BF16), (own, BF16), (half, BF16), (half, BF16)],
        after=(kv, dg_own),
        aliases={0: 0, 1: 1},
        limit=4,
    )
    corner = swap(x_half, 4), swap(y_half, 2)
    chunks = ((x_rows,), (swap(x_rows, 1),), (y_rows,), (swap(y_rows, 1),))
    *kept, kv = project(info, (2, 3, 4, 5), chunks, w_head, kept, kv=kv)
    far_kv = [onward(kv)]
    corner = call(gate_kernel, (), (), [(half, BF16), (half, BF16)], after=(*corner, kv), aliases={0: 0, 1: 1}, limit=4)
    *kept, kv, q = project(info, (6, 7), (corner, [swap(x, 1) for x in corner]), w_head, kept, True)
    far_kv.append(onward(kv))
    q_next = backward(q)
    normed, act, slope = kept
    d_gated = trade(dg_pieces, (kv,))

    near, kt, qt, slope_qt = call(fwd_own_kernel, info[:2], (act, slope), [(tall, F32)] + [(tall_t, BF16)] * 3)
    attn, kv, far_kt, sums = call(
        fwd_far_kernel,
        info,
        (act, *far_kv, near, *d_gated),
        [(tall, BF16), (wide, BF16), (tall_t, BF16), (sums_shape, F32)],
        [(tall, F32), (tall, BF16)],
    )
    sums = call(add_kernel, (), (sums, swap(sums, 1)), [(sums_shape, F32)], limit=4)[0]
    sums = [sums] + [swap(sums, mask) for mask in (2, 4, 6)]

    g, u_cols = call(
        cotangent_kernel,
        info[1:],
        (act, slope, attn, *sums, *d_gated),
        [(tall, BF16), (tall_t, BF16)],
        [(tall, BF16)],
        (q_next,),
    )
    g_next = backward(g)
    q_cols, d_q, dkv = call(
        queries_kernel,
        info[:1],
        (act, slope_qt, qt, kt, g, kv, far_kt),
        [(tall_t, BF16), (tall, BF16), (wide, F32)],
        [(tall_t, BF16)],
    )
    rows, cols = 4 * HD // groups, 4 * HD
    outs = call(
        functools.partial(keys_kernel, groups),
        (info[0], info[2]),
        (dkv, act, slope, q_next, g_next, u_cols, q_cols, d_q, attn, normed),
        trade_outs(cols)
        + ([((2 * rows, width), F32), ((2 * rows, width), BF16)] if groups == 4 else [((rows, width), BF16)] * groups),
        [((2 * HD, SPAN), BF16), ((4 * HD, width), BF16), (wide, F32)],
    )
    def between(x, mask):
        return lax.ppermute(x, "g", [(i, i ^ mask) for i in range(groups)])

    if groups == 4:
        keep, send = outs[5:]
        half = [((rows, width), F32), ((rows, width), BF16)]
        keep, send = call(half_kernel, (), (keep, between(send, 1)), half, limit=8)
        shares = keep, between(send, 2)
    else:
        shares = [outs[5]] + [between(x, mask + 1) for mask, x in enumerate(outs[6:])]
    pieces = trade(outs[:5])
    u, slope_u = call(own_u_kernel, (), (tokens, w_in), [(own, BF16), (own, BF16)], after=(outs[0],))
    d_normed = call(
        branches_kernel,
        info[2:],
        (*pieces[:4], w_in),
        [(own, F32)],
        [(own, BF16)],
    )[0]
    layer_out, grad_tokens, end = call(
        rows_kernel,
        info[2:],
        (*pieces, d_normed, dg_own, u, slope_u, tokens, grad_out, w_out, w_in),
        [(own, BF16), (own, BF16), ((8, HD), F32)],
        [(own, BF16)],
    )
    grad_w_in = call(
        sum_kernel, (), tuple(shares), [((rows, width), F32)], after=(end,)
    )[0]
    parts = groups // 4
    if parts > 1:
        perm = [
            (i * HEADS + j, ((i // parts) * HEADS + j) * parts + i % parts)
            for i in range(groups)
            for j in range(HEADS)
        ]
        grad_w_in = lax.ppermute(grad_w_in, ("g", "h"), perm)
    return (layer_out, grad_tokens, grad_w_in)


def solution(mesh):
    groups = mesh.shape["seq"] // HEADS
    split = Mesh(mesh.devices.reshape(groups, HEADS), ("g", "h"))
    rows = P(("g", "h"), None)
    return jax.shard_map(
        functools.partial(per_device, groups),
        mesh=split,
        in_specs=(rows, P(), P(), P(), P(), rows),
        out_specs=(rows, rows, rows),
        check_vma=False,
    )
```

```python
import functools

import jax
import jax.numpy as jnp
from jax import lax
from jax.experimental import pallas as pl
from jax.experimental.pallas import tpu as pltpu
from jax.sharding import Mesh, PartitionSpec as P

HEADS = 8
HD = 128
BLK = 128
MAXB = 16
SPAN = MAXB * BLK
TILE = 256
TILES = SPAN // TILE
CHUNK = 512
CHUNKS = SPAN // CHUNK
SCALE = HD ** (-0.5)
LOG2E = 1.4426950408889634

eps = 1e-05

NT = (((1,), (1,)), ((), ()))
F32, BF16 = jnp.float32, jnp.bfloat16

U, Q, V, K = (slice(i * HD, (i + 1) * HD) for i in range(4))
PLACE = (0, 2, 1, 3)
UQ, VK = slice(0, 2 * HD), slice(2 * HD, 4 * HD)


def start_kernel(counts_ref, tails_ref, w_ref, lo_ref, nv_ref, at_ref, wh_ref, sems):
    group = lax.axis_index("g").astype(jnp.int32)
    at_ref[0] = group
    head = lax.axis_index("h").astype(jnp.int32)
    at_ref[1] = head
    copies = []
    for i in range(4):
        source = w_ref.at[:, lanes_at(PLACE[i] * (w_ref.shape[0] // HD) + head)]
        copies.append(pltpu.make_async_copy(source, wh_ref.at[:, i * HD : (i + 1) * HD], sems.at[i]))
        copies[i].start()
    base = group * MAXB
    for j in range(2 * MAXB):
        lo_ref[j] = j * BLK
        nv_ref[j] = BLK

    def user(n, start):
        end = start + counts_ref[n]

        def block(j, carry):
            lo_ref[j] = (start - base) * BLK
            nv_ref[j] = jnp.where(j == end - 1 - base, tails_ref[n], BLK)
            return carry

        lax.fori_loop(jnp.maximum(start - base, 0), jnp.minimum(end - base, 2 * MAXB), block, 0)
        return end

    lax.fori_loop(0, counts_ref.shape[0], user, jnp.int32(0))
    for copy in copies:
        copy.wait()


def by_half(t, ref, shape, dim):
    side = lax.broadcasted_iota(jnp.int32, shape, dim)
    return jnp.where(side < BLK, ref[2 * t], ref[2 * t + 1])


def from_start(t, lo_ref, at, keys, dim):
    parts = [part >= lo_ref[2 * t + i] - at for i, part in enumerate(jnp.split(keys, 2, axis=1 - dim))]
    return jnp.concatenate(parts, axis=1 - dim)


def valid_rows(t, nv_ref):
    row = lax.broadcasted_iota(jnp.int32, (TILE, 1), 0)
    return (row & (BLK - 1)) < by_half(t, nv_ref, (TILE, 1), 0)


def rows_at(t):
    return pl.ds(pl.multiple_of(t * TILE, TILE), TILE)


def chunk_at(c):
    return pl.ds(pl.multiple_of(c * CHUNK, CHUNK), CHUNK)


def tiles_back(t, first, step, carry):
    count = t - first + 1

    def pair(i, carry):
        return step(pl.multiple_of((t - 2 * i - 1) * TILE, TILE), 2 * TILE, carry)

    carry = lax.fori_loop(0, count // 2, pair, carry)
    return lax.fori_loop(0, count % 2, lambda i, c: step(pl.multiple_of(first * TILE, TILE), TILE, c), carry)


def lanes_at(i):
    return pl.ds(pl.multiple_of(i * HD, HD), HD)


def norm_rows(x):
    return x * lax.rsqrt(jnp.mean(x * x, axis=-1, keepdims=True) + eps)


def silu_and_slope(pre):
    s = 0.5 + 0.5 * jnp.tanh(0.5 * pre)
    return (pre * s).astype(BF16), (s * (1.0 + pre * (1.0 - s))).astype(BF16)


def store_rows(x, place, wh_ref, normed_ref, act_ref, slope_ref, kv_ref, i):
    rows = rows_at(place)
    xn = norm_rows(x.astype(F32)).astype(BF16)
    normed_ref[rows, :] = xn
    act, slope = silu_and_slope(jnp.dot(xn, wh_ref[...], preferred_element_type=F32))
    act_ref[rows, :] = act
    slope_ref[rows, :] = slope
    kv_ref[i * TILE : (i + 1) * TILE, :] = act[:, VK]


def proj_kernel(masks, pieces, last, ahead, at_ref, *refs):
    x_refs, wh_ref = refs[: sum(pieces)], refs[sum(pieces)]
    outs = refs[-5:-1] if last else refs[-4:]
    if ahead:
        outs[3][: ahead * TILE, :] = refs[sum(pieces) + 1][...]
    for i, mask in enumerate(masks):
        parts = [ref[...] for ref in x_refs[sum(pieces[:i]) : sum(pieces[: i + 1])]]
        x = parts[0] if len(parts) == 1 else jnp.concatenate(parts, axis=0)
        store_rows(x, at_ref[1] ^ mask, wh_ref, *outs, ahead + i)
    if last:
        refs[-1][...] = outs[1][:, Q]


def proj_outs(width, n):
    return [((SPAN, width), BF16), ((SPAN, 4 * HD), BF16), ((SPAN, 4 * HD), BF16), ((n * TILE, 2 * HD), BF16)]


def project(info, masks, chunks, w, kept, last=False, kv=None):
    pieces = tuple(len(chunk) for chunk in chunks)
    flat = [piece for chunk in chunks for piece in chunk]
    lead = () if kv is None else (kv,)
    ahead = 0 if kv is None else kv.shape[0] // TILE
    start = 2 + len(flat) + len(lead)
    return call(
        functools.partial(proj_kernel, masks, pieces, last, ahead),
        (info[2],),
        (*flat, w, *lead),
        proj_outs(w.shape[0], ahead + len(masks)) + ([((SPAN, HD), BF16)] if last else []),
        after=kept,
        aliases={start + i: i for i in range(len(kept))},
    )


def cut_kernel(x_ref, y_ref, *refs):
    x_half, y_half = refs[-2:]
    x_half[...] = x_ref[:BLK, :]
    y_half[...] = y_ref[BLK:, :]


def gate_kernel(*refs):
    pass


def merge_kernel(other_ref, *refs):
    for i, ref in enumerate(refs[-3:]):
        ref[TILE:, :] = other_ref[(i + 1) * TILE : (i + 2) * TILE, :]


def places(refs):
    mine, other, *pairs = refs
    return [(mine, 0), (other, 0)] + [(ref, at) for ref in pairs for at in (0, TILE)]


def outgoing(refs):
    mine, other, *pairs = refs
    found = [(mine, 0)] * HEADS
    for i in range(4):
        found[2 * i + 1] = other, i * TILE
    for i in range(3):
        found[2 * i + 2] = pairs[i], 0
    return found


def trade_outs(cols):
    return [((TILE, cols), BF16), ((4 * TILE, cols), BF16)] + [((2 * TILE, cols), BF16)] * 3


def d_gated_kernel(at_ref, g_ref, w_ref, *refs):
    pieces, d_ref = refs[-6:-1], refs[-1]
    d_ref[...] = lax.dot_general(g_ref[...], w_ref[...], NT, preferred_element_type=F32).astype(BF16)
    for mask, (ref, at) in enumerate(outgoing(pieces)):
        ref[at : at + TILE, :] = d_ref[:, lanes_at(at_ref[1] ^ mask)]


def sigmoid(s):
    return pl.reciprocal(1.0 + jnp.exp2(s * (-SCALE * LOG2E)), approx=True)


def weigh(q, kt, v, mask):
    s = jnp.dot(q, kt, preferred_element_type=F32)
    w = jnp.where(mask, s * sigmoid(s), 0.0).astype(BF16)
    return jnp.dot(w, v, preferred_element_type=F32)


def fwd_own_kernel(lo_ref, nv_ref, act_ref, slope_ref, out_ref, kt_ref, qt_ref, slope_qt_ref):
    for t in range(TILES):
        rows = slice(t * TILE, (t + 1) * TILE)
        kt_ref[:, rows] = act_ref[rows, K].T
    row = lax.broadcasted_iota(jnp.int32, (TILE, CHUNK), 0)
    col = lax.broadcasted_iota(jnp.int32, (TILE, CHUNK), 1)

    def q_tile(t, carry):
        q = act_ref[rows_at(t), Q]

        def keys(at, size, acc):
            mask = from_start(t, lo_ref, at, col[:, :size], 1) & ((col - row)[:, :size] <= t * TILE - at)
            return acc + weigh(q, kt_ref[:, pl.ds(at, size)], act_ref[pl.ds(at, size), V], mask)

        first = jnp.maximum(lo_ref[2 * t], 0) // TILE
        acc = tiles_back(t, first, keys, jnp.zeros((TILE, HD), F32))
        out_ref[rows_at(t), :] = jnp.where(valid_rows(t, nv_ref), acc, 0.0)
        return carry

    lax.fori_loop(0, TILES, q_tile, 0)
    for t in range(TILES):
        rows = slice(t * TILE, (t + 1) * TILE)
        qt_ref[:, rows] = act_ref[rows, Q].T
        slope_qt_ref[:, rows] = slope_ref[rows, Q].T


def fwd_far_kernel(
    lo_ref, nv_ref, at_ref, act_ref, kva_ref, kvb_ref, near_ref, *refs,
):
    dg_refs, (out_ref, kv_ref, kt_ref, sum_ref, attn_s, dg_s) = refs[:5], refs[5:]
    head = at_ref[1]
    slot = 0
    for ref in (kva_ref, kvb_ref):
        for at in range(0, ref.shape[0], TILE):
            kv_ref[rows_at(slot ^ head), :] = ref[at : at + TILE, :]
            slot += 1
    for mask, (ref, at) in enumerate(places(dg_refs)):
        dg_s[rows_at(head ^ mask), :] = ref[at : at + TILE, :]
    first = jnp.minimum(lo_ref[0] + SPAN, SPAN) // CHUNK
    for t in range(TILES):
        rows = slice(t * TILE, (t + 1) * TILE)

        @pl.when(t // 2 >= first)
        def _():
            kt_ref[:, rows] = kv_ref[rows, HD:].T

    attn_s[...] = near_ref[...]
    col = lax.broadcasted_iota(jnp.int32, (TILE, CHUNK), 1)

    def q_tile(t, carry):
        q = act_ref[rows_at(t), Q]

        def k_chunk(c, acc):
            mask = from_start(t, lo_ref, c * CHUNK - SPAN, col, 1)
            return acc + weigh(q, kt_ref[:, chunk_at(c)], kv_ref[chunk_at(c), :HD], mask)

        start = (lo_ref[2 * t] + SPAN) // CHUNK
        acc = lax.fori_loop(start, CHUNKS, k_chunk, jnp.zeros((TILE, HD), F32))
        attn_s[rows_at(t), :] += jnp.where(valid_rows(t, nv_ref), acc, 0.0)
        return carry

    lax.fori_loop(0, far_tiles(lo_ref), q_tile, 0)
    ones = jnp.ones((8, HD), BF16)
    for t in range(TILES):
        rows = slice(t * TILE, (t + 1) * TILE)
        attn = attn_s[rows, :] * (SCALE / SPAN)
        out_ref[rows, :] = attn.astype(BF16)
        d_n = dg_s[rows, :].astype(F32) * act_ref[rows, U].astype(F32)
        square = lax.dot_general(ones, (attn * attn).astype(BF16), NT, preferred_element_type=F32)
        cross = lax.dot_general(ones, (attn * d_n).astype(BF16), NT, preferred_element_type=F32)
        sum_ref[t : t + 1, :] = square[:1]
        sum_ref[TILES + t : TILES + t + 1, :] = cross[:1]


def add_kernel(a_ref, b_ref, out_ref):
    out_ref[...] = (a_ref[...].astype(F32) + b_ref[...].astype(F32)).astype(out_ref.dtype)


def far_tiles(lo_ref):
    return sum((lo_ref[2 * t] < 0).astype(jnp.int32) for t in range(TILES))


def row_scales(sum_refs):
    width = HEADS * HD
    total = sum_refs[0][...]
    for ref in sum_refs[1:]:
        total += ref[...]
    r = lax.rsqrt(total[:TILES] * (1.0 / width) + eps)
    c = total[TILES:] * (1.0 / width) * r
    return jnp.concatenate([r, c], axis=0).T


def cotangent(t, scales, nv_ref, u, attn, d_gated):
    r, c = scales[:, t : t + 1], scales[:, TILES + t : TILES + t + 1]
    n = attn.astype(F32) * r
    g = r * (d_gated * u.astype(F32) - n * c)
    return n, jnp.where(valid_rows(t, nv_ref), g, 0.0).astype(BF16)


def back_scores(qt, k, v, gt, mask):
    s = jnp.dot(k, qt, preferred_element_type=F32)
    sig = jnp.where(mask, sigmoid(s), 0.0)
    dw = jnp.dot(v, gt, preferred_element_type=F32)
    ds = dw * sig * (1.0 + (s * SCALE) * (1.0 - sig))
    return (s * sig).astype(BF16), ds.astype(BF16)


def cotangent_kernel(nv_ref, at_ref, act_ref, slope_ref, attn_ref, *refs):
    sum_refs, dg_refs, (g_ref, cols_ref, dg_s) = refs[:4], refs[4:9], refs[-3:]
    for mask, (ref, at) in enumerate(places(dg_refs)):
        dg_s[rows_at(at_ref[1] ^ mask), :] = ref[at : at + TILE, :]
    scales = row_scales(sum_refs)
    for t in range(TILES):
        rows = slice(t * TILE, (t + 1) * TILE)
        d_gated = dg_s[rows, :].astype(F32)
        n, g = cotangent(t, scales, nv_ref, act_ref[rows, U], attn_ref[rows, :], d_gated)
        g_ref[rows, :] = g
        du = (d_gated * n).astype(BF16).astype(F32)
        cols_ref[:, rows] = (du * slope_ref[rows, U].astype(F32)).astype(BF16).T


def queries_kernel(lo_ref, act_ref, slope_qt_ref, qt_ref, kt_ref, g_ref, kv_ref, far_kt_ref, cols_ref, rows_ref, dkv_ref, gt_s):
    for t in range(TILES):
        rows = slice(t * TILE, (t + 1) * TILE)
        gt_s[:, rows] = g_ref[rows, :].T
    for c in range(CHUNKS):
        dkv_ref[c * CHUNK : (c + 1) * CHUNK, :] = jnp.zeros((CHUNK, 2 * HD), F32)
    key = lax.broadcasted_iota(jnp.int32, (CHUNK, TILE), 0)
    query = lax.broadcasted_iota(jnp.int32, (CHUNK, TILE), 1)

    def q_tile(t, carry):
        q, qt = act_ref[rows_at(t), Q], qt_ref[:, rows_at(t)]
        g, gt = g_ref[rows_at(t), :], gt_s[:, rows_at(t)]

        def far_chunk(c, dqt):
            at = chunk_at(c)
            mask = from_start(t, lo_ref, c * CHUNK - SPAN, key, 0)
            ds = back_scores(qt, kv_ref[at, HD:], kv_ref[at, :HD], gt, mask)[1]
            return dqt + jnp.dot(far_kt_ref[:, at], ds, preferred_element_type=F32)

        def keys(start, size, dqt):
            at = pl.ds(start, size)
            mask = from_start(t, lo_ref, start, key[:size], 0) & ((key - query)[:size] <= t * TILE - start)
            w, ds = back_scores(qt, act_ref[at, K], act_ref[at, V], gt, mask)
            dkv_ref[at, :HD] += jnp.dot(w, g, preferred_element_type=F32)
            dkv_ref[at, HD:] += jnp.dot(ds, q, preferred_element_type=F32)
            return dqt + jnp.dot(kt_ref[:, at], ds, preferred_element_type=F32)

        first = lo_ref[2 * t]
        start = jnp.minimum(first + SPAN, SPAN) // CHUNK
        dqt = lax.fori_loop(start, CHUNKS, far_chunk, jnp.zeros((HD, TILE), F32))
        dqt = tiles_back(t, jnp.maximum(first, 0) // TILE, keys, dqt)
        dq = (dqt * (SCALE / SPAN)).astype(BF16).astype(F32)
        dq = (dq * slope_qt_ref[:, rows_at(t)].astype(F32)).astype(BF16)
        cols_ref[:, rows_at(t)] = dq
        rows_ref[rows_at(t), :] = dq.T
        return carry

    lax.fori_loop(0, TILES, q_tile, 0)


def keys_kernel(lo_ref, at_ref, own_ref, act_ref, slope_ref, q_ref, g_ref, dq_ref, attn_ref, *refs):
    pieces, (cols_ref, acc_s) = refs[:5], refs[5:]
    first = jnp.minimum(lo_ref[2 * TILES], SPAN) // CHUNK
    key = lax.broadcasted_iota(jnp.int32, (CHUNK, TILE), 0)

    def clear(c, carry):
        acc_s[chunk_at(c), :] = jnp.zeros((CHUNK, 2 * HD), F32)
        return carry

    lax.fori_loop(first, CHUNKS, clear, 0)

    def q_tile(t, carry):
        q, g = q_ref[rows_at(t), :], g_ref[rows_at(t), :]
        qt, gt = q.T, g.T

        def k_chunk(c, carry):
            at = chunk_at(c)
            mask = from_start(TILES + t, lo_ref, c * CHUNK, key, 0)
            w, ds = back_scores(qt, act_ref[at, K], act_ref[at, V], gt, mask)
            acc_s[at, :HD] += jnp.dot(w, g, preferred_element_type=F32)
            acc_s[at, HD:] += jnp.dot(ds, q, preferred_element_type=F32)
            return carry

        return lax.fori_loop(lo_ref[2 * (TILES + t)] // CHUNK, CHUNKS, k_chunk, carry)

    count = sum((lo_ref[2 * (TILES + t)] < SPAN).astype(jnp.int32) for t in range(TILES))
    lax.fori_loop(0, count, q_tile, 0)
    for mask, (ref, at) in enumerate(outgoing(pieces)):
        t = at_ref[1] ^ mask
        rows = rows_at(t)
        d = own_ref[rows, :] + jnp.where(t // 2 >= first, acc_s[rows, :], 0.0)
        d = (d * (SCALE / SPAN)).astype(BF16).astype(F32)
        d = (d * slope_ref[rows, VK].astype(F32)).astype(BF16)
        ref[at : at + TILE, :HD] = attn_ref[rows, :]
        ref[at : at + TILE, HD : 2 * HD] = dq_ref[rows, :]
        ref[at : at + TILE, 2 * HD :] = d
        cols_ref[:, rows] = d.T


def share_kernel(groups, at_ref, u_cols_ref, q_cols_ref, cols_ref, normed_ref, *refs):
    shares, all_s = refs[:-1], refs[-1]
    share = jnp.dot(cols_ref[...], normed_ref[...], preferred_element_type=F32).astype(BF16)
    all_s[HD : 2 * HD, :], all_s[3 * HD :, :] = share[:HD], share[HD:]
    all_s[:HD, :] = jnp.dot(u_cols_ref[...], normed_ref[...], preferred_element_type=F32).astype(BF16)
    all_s[2 * HD : 3 * HD, :] = jnp.dot(q_cols_ref[...], normed_ref[...], preferred_element_type=F32).astype(BF16)
    size = 4 * HD // groups
    for mask in range(groups):
        at = pl.multiple_of((at_ref[0] ^ mask) * size, size)
        part = all_s[pl.ds(at, size), :]
        if groups == 4:
            ref, half = shares[mask % 2], mask // 2 * size
            ref[half : half + size, :] = part.astype(ref.dtype)
        else:
            shares[mask][...] = part


def assemble(at_ref, refs, part, out_s):
    for mask, (ref, at) in enumerate(places(refs)):
        out_s[:, lanes_at(at_ref[1] ^ mask)] = ref[at : at + TILE, part * HD : (part + 1) * HD]


def branch_rows(at_ref, refs, w_ref, distances, row_s):
    width, total = w_ref.shape[0], 0.0
    for part, branch in ((1, 2), (2, 1), (3, 3)):
        assemble(at_ref, refs, part, row_s)
        for i in distances:
            at = ((at_ref[1] // 2) ^ i) * 2 * HD
            x = row_s[:, pl.ds(pl.multiple_of(at, 2 * HD), 2 * HD)]
            w = w_ref[:, pl.ds(pl.multiple_of(branch * width + at, 2 * HD), 2 * HD)]
            total += lax.dot_general(x, w, NT, preferred_element_type=F32)
    return total


def through(x, w_ref, branch):
    width = w_ref.shape[0]
    return lax.dot_general(x, w_ref[:, branch * width : (branch + 1) * width], NT, preferred_element_type=F32)


def branches_kernel(at_ref, *refs):
    pieces, (w_in_ref, dn_ref, row_s) = refs[:4], refs[4:]
    dn_ref[...] = branch_rows(at_ref, pieces, w_in_ref, (0, 1, 2), row_s)


def own_u_kernel(tokens_ref, w_in_ref, after_ref, u_ref, slope_ref):
    xn = norm_rows(tokens_ref[...].astype(F32)).astype(BF16)
    pre = jnp.dot(xn, w_in_ref[:, : tokens_ref.shape[1]], preferred_element_type=F32)
    u_ref[...], slope_ref[...] = silu_and_slope(pre)


def rows_kernel(at_ref, *refs):
    pieces, (dn_ref, dg_ref, u_ref, slope_ref, tokens_ref, grad_ref, w_out_ref, w_in_ref) = refs[:5], refs[5:-4]
    out_ref, dx_ref, end_ref, row_s = refs[-4:]
    end_ref[...] = jnp.zeros(end_ref.shape, F32)
    x = tokens_ref[...].astype(F32)
    assemble(at_ref, pieces, 0, row_s)
    attn_n = norm_rows(row_s[...].astype(F32))
    gated = (attn_n * u_ref[...].astype(F32)).astype(BF16)
    y = jnp.dot(gated, w_out_ref[...], preferred_element_type=F32)
    out_ref[...] = (x + y).astype(BF16)
    du = (dg_ref[...].astype(F32) * attn_n).astype(BF16).astype(F32)
    du = (du * slope_ref[...].astype(F32)).astype(BF16)
    dn = dn_ref[...] + through(du, w_in_ref, 0) + branch_rows(at_ref, pieces, w_in_ref, (3,), row_s)
    r = lax.rsqrt(jnp.mean(x * x, axis=-1, keepdims=True) + eps)
    n = x * r
    dx = r * (dn - n * jnp.mean(dn * n, axis=-1, keepdims=True))
    dx_ref[...] = (grad_ref[...].astype(F32) + dx).astype(BF16)


def half_kernel(keep_ref, got_ref, mine_ref, send_ref):
    size = mine_ref.shape[0]
    mine_ref[...] = keep_ref[:size, :] + got_ref[:size, :].astype(F32)
    send_ref[...] = (keep_ref[size:, :] + got_ref[size:, :].astype(F32)).astype(BF16)


def sum_kernel(*refs):
    total = refs[0][...].astype(F32)
    for ref in refs[1:-2]:
        total += ref[...].astype(F32)
    refs[-1][...] = total


def call(kernel, scalars, arrays, outs, scratch=(), after=(), aliases=None, limit=16, sems=0):
    smem = pl.BlockSpec(memory_space=pltpu.SMEM)
    vmem = pl.BlockSpec(memory_space=pltpu.VMEM)
    anywhere = pl.BlockSpec(memory_space=pl.ANY)
    return pl.pallas_call(
        kernel,
        out_shape=[jax.ShapeDtypeStruct(*out) for out in outs],
        in_specs=[smem] * len(scalars) + [vmem] * len(arrays) + [anywhere] * len(after),
        out_specs=[smem if out[1] == jnp.int32 else vmem for out in outs],
        scratch_shapes=[pltpu.VMEM(*shape) for shape in scratch] + ([pltpu.SemaphoreType.DMA((sems,))] if sems else []),
        input_output_aliases=aliases or {},
        compiler_params=pltpu.CompilerParams(vmem_limit_bytes=limit * 2**20),
        cost_estimate=pl.CostEstimate(flops=0, bytes_accessed=0, transcendentals=0),
    )(*scalars, *arrays, *after)


def per_device(groups, tokens, w_in, w_out, block_counts, tails, grad_out):
    count, width = tokens.shape
    own, tall, wide, tall_t = (count, width), (SPAN, HD), (SPAN, 2 * HD), (HD, SPAN)
    piece, half, sums_shape = (count, HD), (BLK, width), (2 * TILES, TILE)

    def swap(x, mask):
        return lax.ppermute(x, "h", [(i, i ^ mask) for i in range(HEADS)])

    def onward(x):
        return lax.ppermute(x, "g", [(i, i + 1) for i in range(groups - 1)])

    def backward(x):
        return lax.ppermute(x, "g", [(i + 1, i) for i in range(groups - 1)])

    def trade(pieces, after=()):
        mine, other, *pairs = pieces
        other = swap(other, 1)
        pairs = call(
            merge_kernel,
            (),
            (other,),
            [(x.shape, BF16) for x in pairs],
            after=(*pairs, *after),
            aliases={1: 0, 2: 1, 3: 2},
            limit=4,
        )
        return [mine, other] + [swap(x, mask) for x, mask in zip(pairs, (2, 4, 6))]

    x_rows, y_rows = swap(tokens, 2), swap(tokens, 4)
    other = swap(tokens, 1)
    *info, w_head = call(
        start_kernel,
        (block_counts, tails),
        (),
        [((2 * MAXB,), jnp.int32)] * 2 + [((2,), jnp.int32), ((width, 4 * HD), BF16)],
        after=(w_in,),
        limit=51,
        sems=4,
    )
    *kept, kv = project(info, (0, 1), ((tokens,), (other,)), w_head, ())
    *dg_pieces, dg_own = call(
        d_gated_kernel, info[2:], (grad_out, w_out), trade_outs(HD) + [(own, BF16)], after=(kv,)
    )
    x_rows, y_rows, x_half, y_half = call(
        cut_kernel,
        (),
        (x_rows, y_rows),
        [(own, BF16), (own, BF16), (half, BF16), (half, BF16)],
        after=(kv, dg_own),
        aliases={0: 0, 1: 1},
        limit=4,
    )
    corner = swap(x_half, 4), swap(y_half, 2)
    chunks = ((x_rows,), (swap(x_rows, 1),), (y_rows,), (swap(y_rows, 1),))
    *kept, kv = project(info, (2, 3, 4, 5), chunks, w_head, kept, kv=kv)
    far_kv = [onward(kv)]
    corner = call(gate_kernel, (), (), [(half, BF16), (half, BF16)], after=(*corner, kv), aliases={0: 0, 1: 1}, limit=4)
    *kept, kv, q = project(info, (6, 7), (corner, [swap(x, 1) for x in corner]), w_head, kept, True)
    far_kv.append(onward(kv))
    q_next = backward(q)
    normed, act, slope = kept
    d_gated = trade(dg_pieces, (kv,))

    near, kt, qt, slope_qt = call(fwd_own_kernel, info[:2], (act, slope), [(tall, F32)] + [(tall_t, BF16)] * 3)
    attn, kv, far_kt, sums = call(
        fwd_far_kernel,
        info,
        (act, *far_kv, near, *d_gated),
        [(tall, BF16), (wide, BF16), (tall_t, BF16), (sums_shape, F32)],
        [(tall, F32), (tall, BF16)],
    )
    sums = call(add_kernel, (), (sums, swap(sums, 1)), [(sums_shape, F32)], limit=4)[0]
    sums = [sums] + [swap(sums, mask) for mask in (2, 4, 6)]

    g, u_cols = call(
        cotangent_kernel,
        info[1:],
        (act, slope, attn, *sums, *d_gated),
        [(tall, BF16), (tall_t, BF16)],
        [(tall, BF16)],
        (q_next,),
    )
    g_next = backward(g)
    q_cols, d_q, dkv = call(
        queries_kernel,
        info[:1],
        (act, slope_qt, qt, kt, g, kv, far_kt),
        [(tall_t, BF16), (tall, BF16), (wide, F32)],
        [(tall_t, BF16)],
    )
    rows = 4 * HD // groups
    *pieces, cols = call(
        keys_kernel,
        (info[0], info[2]),
        (dkv, act, slope, q_next, g_next, d_q, attn),
        trade_outs(4 * HD) + [((2 * HD, SPAN), BF16)],
        [(wide, F32)],
    )
    outs = call(
        functools.partial(share_kernel, groups),
        info[2:],
        (u_cols, q_cols, cols, normed),
        [((2 * rows, width), F32), ((2 * rows, width), BF16)] if groups == 4 else [((rows, width), BF16)] * groups,
        [((4 * HD, width), BF16)],
    )

    def between(x, mask):
        return lax.ppermute(x, "g", [(i, i ^ mask) for i in range(groups)])

    if groups == 4:
        keep, send = outs
        half = [((rows, width), F32), ((rows, width), BF16)]
        keep, send = call(half_kernel, (), (keep, between(send, 1)), half, limit=8)
        shares = keep, between(send, 2)
    else:
        shares = [outs[0]] + [between(x, mask + 1) for mask, x in enumerate(outs[1:])]
    pieces = trade(pieces)
    u, slope_u = call(own_u_kernel, (), (tokens, w_in), [(own, BF16), (own, BF16)], after=(cols,))
    d_normed = call(
        branches_kernel,
        info[2:],
        (*pieces[:4], w_in),
        [(own, F32)],
        [(own, BF16)],
    )[0]
    layer_out, grad_tokens, end = call(
        rows_kernel,
        info[2:],
        (*pieces, d_normed, dg_own, u, slope_u, tokens, grad_out, w_out, w_in),
        [(own, BF16), (own, BF16), ((8, HD), F32)],
        [(own, BF16)],
    )
    grad_w_in = call(
        sum_kernel, (), tuple(shares), [((rows, width), F32)], after=(end,)
    )[0]
    parts = groups // 4
    if parts > 1:
        perm = [
            (i * HEADS + j, ((i // parts) * HEADS + j) * parts + i % parts)
            for i in range(groups)
            for j in range(HEADS)
        ]
        grad_w_in = lax.ppermute(grad_w_in, ("g", "h"), perm)
    return (layer_out, grad_tokens, grad_w_in)


def solution(mesh):
    groups = mesh.shape["seq"] // HEADS
    split = Mesh(mesh.devices.reshape(groups, HEADS), ("g", "h"))
    rows = P(("g", "h"), None)
    return jax.shard_map(
        functools.partial(per_device, groups),
        mesh=split,
        in_specs=(rows, P(), P(), P(), P(), rows),
        out_specs=(rows, rows, rows),
        check_vma=False,
    )
```

```python
import functools

import jax
import jax.numpy as jnp
from jax import lax
from jax.experimental import pallas as pl
from jax.experimental.pallas import tpu as pltpu
from jax.sharding import Mesh, PartitionSpec as P

HEADS = 8
HD = 128
BLK = 128
MAXB = 16
SPAN = MAXB * BLK
TILE = 256
TILES = SPAN // TILE
CHUNK = 512
CHUNKS = SPAN // CHUNK
SCALE = HD ** (-0.5)
LOG2E = 1.4426950408889634

eps = 1e-05

NT = (((1,), (1,)), ((), ()))
F32, BF16 = jnp.float32, jnp.bfloat16

U, Q, V, K = (slice(i * HD, (i + 1) * HD) for i in range(4))
PLACE = (0, 2, 1, 3)
UQ, VK = slice(0, 2 * HD), slice(2 * HD, 4 * HD)


def start_kernel(counts_ref, tails_ref, w_ref, lo_ref, nv_ref, at_ref, wh_ref, sems):
    group = lax.axis_index("g").astype(jnp.int32)
    at_ref[0] = group
    head = lax.axis_index("h").astype(jnp.int32)
    at_ref[1] = head
    copies = []
    for i in range(4):
        source = w_ref.at[:, lanes_at(PLACE[i] * (w_ref.shape[0] // HD) + head)]
        copies.append(pltpu.make_async_copy(source, wh_ref.at[:, i * HD : (i + 1) * HD], sems.at[i]))
        copies[i].start()
    base = group * MAXB
    for j in range(2 * MAXB):
        lo_ref[j] = j * BLK
        nv_ref[j] = BLK

    def user(n, start):
        end = start + counts_ref[n]

        def block(j, carry):
            lo_ref[j] = (start - base) * BLK
            nv_ref[j] = jnp.where(j == end - 1 - base, tails_ref[n], BLK)
            return carry

        lax.fori_loop(jnp.maximum(start - base, 0), jnp.minimum(end - base, 2 * MAXB), block, 0)
        return end

    lax.fori_loop(0, counts_ref.shape[0], user, jnp.int32(0))
    for copy in copies:
        copy.wait()


def by_half(t, ref, shape, dim):
    side = lax.broadcasted_iota(jnp.int32, shape, dim)
    return jnp.where(side < BLK, ref[2 * t], ref[2 * t + 1])


def from_start(t, lo_ref, at, keys, dim):
    parts = [part >= lo_ref[2 * t + i] - at for i, part in enumerate(jnp.split(keys, 2, axis=1 - dim))]
    return jnp.concatenate(parts, axis=1 - dim)


def with_mask(visible, mask, body, carry):
    return lax.cond(visible, lambda c: body(None, c), lambda c: body(mask(), c), carry)


def latest_start(t, lo_ref):
    return jnp.maximum(lo_ref[2 * t], lo_ref[2 * t + 1])


def valid_rows(t, nv_ref):
    row = lax.broadcasted_iota(jnp.int32, (TILE, 1), 0)
    return (row & (BLK - 1)) < by_half(t, nv_ref, (TILE, 1), 0)


def rows_at(t):
    return pl.ds(pl.multiple_of(t * TILE, TILE), TILE)


def chunk_at(c):
    return pl.ds(pl.multiple_of(c * CHUNK, CHUNK), CHUNK)


def tiles_back(t, first, step, carry):
    count = t - first + 1

    def pair(i, carry):
        return step(pl.multiple_of((t - 2 * i - 1) * TILE, TILE), 2 * TILE, carry)

    carry = lax.fori_loop(0, count // 2, pair, carry)
    return lax.fori_loop(0, count % 2, lambda i, c: step(pl.multiple_of(first * TILE, TILE), TILE, c), carry)


def lanes_at(i):
    return pl.ds(pl.multiple_of(i * HD, HD), HD)


def norm_rows(x):
    return x * lax.rsqrt(jnp.mean(x * x, axis=-1, keepdims=True) + eps)


def silu_and_slope(pre):
    s = 0.5 + 0.5 * jnp.tanh(0.5 * pre)
    return (pre * s).astype(BF16), (s * (1.0 + pre * (1.0 - s))).astype(BF16)


def store_rows(x, place, wh_ref, normed_ref, act_ref, slope_ref, kv_ref, i):
    rows = rows_at(place)
    xn = norm_rows(x.astype(F32)).astype(BF16)
    normed_ref[rows, :] = xn
    act, slope = silu_and_slope(jnp.dot(xn, wh_ref[...], preferred_element_type=F32))
    act_ref[rows, :] = act
    slope_ref[rows, :] = slope
    kv_ref[i * TILE : (i + 1) * TILE, :] = act[:, VK]


def proj_kernel(masks, pieces, last, ahead, at_ref, *refs):
    x_refs, wh_ref = refs[: sum(pieces)], refs[sum(pieces)]
    outs = refs[-5:-1] if last else refs[-4:]
    if ahead:
        outs[3][: ahead * TILE, :] = refs[sum(pieces) + 1][...]
    for i, mask in enumerate(masks):
        parts = [ref[...] for ref in x_refs[sum(pieces[:i]) : sum(pieces[: i + 1])]]
        x = parts[0] if len(parts) == 1 else jnp.concatenate(parts, axis=0)
        store_rows(x, at_ref[1] ^ mask, wh_ref, *outs, ahead + i)
    if last:
        refs[-1][...] = outs[1][:, Q]


def proj_outs(width, n):
    return [((SPAN, width), BF16), ((SPAN, 4 * HD), BF16), ((SPAN, 4 * HD), BF16), ((n * TILE, 2 * HD), BF16)]


def project(info, masks, chunks, w, kept, last=False, kv=None):
    pieces = tuple(len(chunk) for chunk in chunks)
    flat = [piece for chunk in chunks for piece in chunk]
    lead = () if kv is None else (kv,)
    ahead = 0 if kv is None else kv.shape[0] // TILE
    start = 2 + len(flat) + len(lead)
    return call(
        functools.partial(proj_kernel, masks, pieces, last, ahead),
        (info[2],),
        (*flat, w, *lead),
        proj_outs(w.shape[0], ahead + len(masks)) + ([((SPAN, HD), BF16)] if last else []),
        after=kept,
        aliases={start + i: i for i in range(len(kept))},
    )


def cut_kernel(x_ref, y_ref, *refs):
    x_half, y_half = refs[-2:]
    x_half[...] = x_ref[:BLK, :]
    y_half[...] = y_ref[BLK:, :]


def gate_kernel(*refs):
    pass


def merge_kernel(other_ref, *refs):
    for i, ref in enumerate(refs[-3:]):
        ref[TILE:, :] = other_ref[(i + 1) * TILE : (i + 2) * TILE, :]


def places(refs):
    mine, other, *pairs = refs
    return [(mine, 0), (other, 0)] + [(ref, at) for ref in pairs for at in (0, TILE)]


def outgoing(refs):
    mine, other, *pairs = refs
    found = [(mine, 0)] * HEADS
    for i in range(4):
        found[2 * i + 1] = other, i * TILE
    for i in range(3):
        found[2 * i + 2] = pairs[i], 0
    return found


def trade_outs(cols):
    return [((TILE, cols), BF16), ((4 * TILE, cols), BF16)] + [((2 * TILE, cols), BF16)] * 3


def d_gated_kernel(at_ref, g_ref, w_ref, *refs):
    pieces, d_ref = refs[-6:-1], refs[-1]
    d_ref[...] = lax.dot_general(g_ref[...], w_ref[...], NT, preferred_element_type=F32).astype(BF16)
    for mask, (ref, at) in enumerate(outgoing(pieces)):
        ref[at : at + TILE, :] = d_ref[:, lanes_at(at_ref[1] ^ mask)]


def sigmoid(s):
    return pl.reciprocal(1.0 + jnp.exp2(s * (-SCALE * LOG2E)), approx=True)


def weigh(q, kt, v, mask):
    s = jnp.dot(q, kt, preferred_element_type=F32)
    w = s * sigmoid(s)
    w = (w if mask is None else jnp.where(mask, w, 0.0)).astype(BF16)
    return jnp.dot(w, v, preferred_element_type=F32)


def fwd_own_kernel(lo_ref, nv_ref, act_ref, slope_ref, out_ref, kt_ref, qt_ref, slope_qt_ref):
    for t in range(TILES):
        rows = slice(t * TILE, (t + 1) * TILE)
        kt_ref[:, rows] = act_ref[rows, K].T
    row = lax.broadcasted_iota(jnp.int32, (TILE, CHUNK), 0)
    col = lax.broadcasted_iota(jnp.int32, (TILE, CHUNK), 1)

    def q_tile(t, carry):
        q = act_ref[rows_at(t), Q]

        def keys(at, size, acc):
            def mask():
                return from_start(t, lo_ref, at, col[:, :size], 1) & ((col - row)[:, :size] <= t * TILE - at)

            def body(mask, acc):
                return acc + weigh(q, kt_ref[:, pl.ds(at, size)], act_ref[pl.ds(at, size), V], mask)

            visible = (at >= latest_start(t, lo_ref)) & (at + size <= t * TILE)
            return with_mask(visible, mask, body, acc)

        first = jnp.maximum(lo_ref[2 * t], 0) // TILE
        acc = tiles_back(t, first, keys, jnp.zeros((TILE, HD), F32))
        out_ref[rows_at(t), :] = jnp.where(valid_rows(t, nv_ref), acc, 0.0)
        return carry

    lax.fori_loop(0, TILES, q_tile, 0)
    for t in range(TILES):
        rows = slice(t * TILE, (t + 1) * TILE)
        qt_ref[:, rows] = act_ref[rows, Q].T
        slope_qt_ref[:, rows] = slope_ref[rows, Q].T


def fwd_far_kernel(
    lo_ref, nv_ref, at_ref, act_ref, kva_ref, kvb_ref, near_ref, *refs,
):
    dg_refs, (out_ref, kv_ref, kt_ref, sum_ref, attn_s, dg_s) = refs[:5], refs[5:]
    head = at_ref[1]
    slot = 0
    for ref in (kva_ref, kvb_ref):
        for at in range(0, ref.shape[0], TILE):
            kv_ref[rows_at(slot ^ head), :] = ref[at : at + TILE, :]
            slot += 1
    for mask, (ref, at) in enumerate(places(dg_refs)):
        dg_s[rows_at(head ^ mask), :] = ref[at : at + TILE, :]
    first = jnp.minimum(lo_ref[0] + SPAN, SPAN) // CHUNK
    for t in range(TILES):
        rows = slice(t * TILE, (t + 1) * TILE)

        @pl.when(t // 2 >= first)
        def _():
            kt_ref[:, rows] = kv_ref[rows, HD:].T

    attn_s[...] = near_ref[...]
    col = lax.broadcasted_iota(jnp.int32, (TILE, CHUNK), 1)

    def q_tile(t, carry):
        q = act_ref[rows_at(t), Q]

        def k_chunk(c, acc):
            def mask():
                return from_start(t, lo_ref, c * CHUNK - SPAN, col, 1)

            def body(mask, acc):
                return acc + weigh(q, kt_ref[:, chunk_at(c)], kv_ref[chunk_at(c), :HD], mask)

            return with_mask(c * CHUNK - SPAN >= latest_start(t, lo_ref), mask, body, acc)

        start = (lo_ref[2 * t] + SPAN) // CHUNK
        acc = lax.fori_loop(start, CHUNKS, k_chunk, jnp.zeros((TILE, HD), F32))
        attn_s[rows_at(t), :] += jnp.where(valid_rows(t, nv_ref), acc, 0.0)
        return carry

    lax.fori_loop(0, far_tiles(lo_ref), q_tile, 0)
    ones = jnp.ones((8, HD), BF16)
    for t in range(TILES):
        rows = slice(t * TILE, (t + 1) * TILE)
        attn = attn_s[rows, :] * (SCALE / SPAN)
        out_ref[rows, :] = attn.astype(BF16)
        d_n = dg_s[rows, :].astype(F32) * act_ref[rows, U].astype(F32)
        square = lax.dot_general(ones, (attn * attn).astype(BF16), NT, preferred_element_type=F32)
        cross = lax.dot_general(ones, (attn * d_n).astype(BF16), NT, preferred_element_type=F32)
        sum_ref[t : t + 1, :] = square[:1]
        sum_ref[TILES + t : TILES + t + 1, :] = cross[:1]


def add_kernel(a_ref, b_ref, out_ref):
    out_ref[...] = (a_ref[...].astype(F32) + b_ref[...].astype(F32)).astype(out_ref.dtype)


def far_tiles(lo_ref):
    return sum((lo_ref[2 * t] < 0).astype(jnp.int32) for t in range(TILES))


def row_scales(sum_refs):
    width = HEADS * HD
    total = sum_refs[0][...]
    for ref in sum_refs[1:]:
        total += ref[...]
    r = lax.rsqrt(total[:TILES] * (1.0 / width) + eps)
    c = total[TILES:] * (1.0 / width) * r
    return jnp.concatenate([r, c], axis=0).T


def cotangent(t, scales, nv_ref, u, attn, d_gated):
    r, c = scales[:, t : t + 1], scales[:, TILES + t : TILES + t + 1]
    n = attn.astype(F32) * r
    g = r * (d_gated * u.astype(F32) - n * c)
    return n, jnp.where(valid_rows(t, nv_ref), g, 0.0).astype(BF16)


def back_scores(qt, k, v, gt, mask):
    s = jnp.dot(k, qt, preferred_element_type=F32)
    sig = sigmoid(s)
    if mask is not None:
        sig = jnp.where(mask, sig, 0.0)
    w = s * sig
    dw = jnp.dot(v, gt, preferred_element_type=F32)
    ds = dw * (sig + SCALE * (w - w * sig))
    return w.astype(BF16), ds.astype(BF16)


def cotangent_kernel(nv_ref, at_ref, act_ref, slope_ref, attn_ref, *refs):
    sum_refs, dg_refs, (g_ref, cols_ref, dg_s) = refs[:4], refs[4:9], refs[-3:]
    for mask, (ref, at) in enumerate(places(dg_refs)):
        dg_s[rows_at(at_ref[1] ^ mask), :] = ref[at : at + TILE, :]
    scales = row_scales(sum_refs)
    for t in range(TILES):
        rows = slice(t * TILE, (t + 1) * TILE)
        d_gated = dg_s[rows, :].astype(F32)
        n, g = cotangent(t, scales, nv_ref, act_ref[rows, U], attn_ref[rows, :], d_gated)
        g_ref[rows, :] = g
        du = (d_gated * n).astype(BF16).astype(F32)
        cols_ref[:, rows] = (du * slope_ref[rows, U].astype(F32)).astype(BF16).T


def queries_kernel(lo_ref, act_ref, slope_qt_ref, qt_ref, kt_ref, g_ref, kv_ref, far_kt_ref, cols_ref, rows_ref, dkv_ref, gt_s):
    for t in range(TILES):
        rows = slice(t * TILE, (t + 1) * TILE)
        gt_s[:, rows] = g_ref[rows, :].T
    for c in range(CHUNKS):
        dkv_ref[c * CHUNK : (c + 1) * CHUNK, :] = jnp.zeros((CHUNK, 2 * HD), F32)
    key = lax.broadcasted_iota(jnp.int32, (CHUNK, TILE), 0)
    query = lax.broadcasted_iota(jnp.int32, (CHUNK, TILE), 1)

    def q_tile(t, carry):
        q, qt = act_ref[rows_at(t), Q], qt_ref[:, rows_at(t)]
        g, gt = g_ref[rows_at(t), :], gt_s[:, rows_at(t)]

        def far_chunk(c, dqt):
            at = chunk_at(c)

            def mask():
                return from_start(t, lo_ref, c * CHUNK - SPAN, key, 0)

            def body(mask, dqt):
                ds = back_scores(qt, kv_ref[at, HD:], kv_ref[at, :HD], gt, mask)[1]
                return dqt + jnp.dot(far_kt_ref[:, at], ds, preferred_element_type=F32)

            return with_mask(c * CHUNK - SPAN >= latest_start(t, lo_ref), mask, body, dqt)

        def keys(start, size, dqt):
            at = pl.ds(start, size)

            def mask():
                return from_start(t, lo_ref, start, key[:size], 0) & ((key - query)[:size] <= t * TILE - start)

            def body(mask, dqt):
                w, ds = back_scores(qt, act_ref[at, K], act_ref[at, V], gt, mask)
                dkv_ref[at, :HD] += jnp.dot(w, g, preferred_element_type=F32)
                dkv_ref[at, HD:] += jnp.dot(ds, q, preferred_element_type=F32)
                return dqt + jnp.dot(kt_ref[:, at], ds, preferred_element_type=F32)

            visible = (start >= latest_start(t, lo_ref)) & (start + size <= t * TILE)
            return with_mask(visible, mask, body, dqt)

        first = lo_ref[2 * t]
        start = jnp.minimum(first + SPAN, SPAN) // CHUNK
        dqt = lax.fori_loop(start, CHUNKS, far_chunk, jnp.zeros((HD, TILE), F32))
        dqt = tiles_back(t, jnp.maximum(first, 0) // TILE, keys, dqt)
        dq = (dqt * (SCALE / SPAN)).astype(BF16).astype(F32)
        dq = (dq * slope_qt_ref[:, rows_at(t)].astype(F32)).astype(BF16)
        cols_ref[:, rows_at(t)] = dq
        rows_ref[rows_at(t), :] = dq.T
        return carry

    lax.fori_loop(0, TILES, q_tile, 0)


def keys_kernel(lo_ref, at_ref, own_ref, act_ref, slope_ref, q_ref, g_ref, dq_ref, attn_ref, *refs):
    pieces, (cols_ref, acc_s) = refs[:5], refs[5:]
    first = jnp.minimum(lo_ref[2 * TILES], SPAN) // CHUNK
    key = lax.broadcasted_iota(jnp.int32, (CHUNK, TILE), 0)

    def clear(c, carry):
        acc_s[chunk_at(c), :] = jnp.zeros((CHUNK, 2 * HD), F32)
        return carry

    lax.fori_loop(first, CHUNKS, clear, 0)

    def q_tile(t, carry):
        q, g = q_ref[rows_at(t), :], g_ref[rows_at(t), :]
        qt, gt = q.T, g.T

        def k_chunk(c, carry):
            at = chunk_at(c)

            def mask():
                return from_start(TILES + t, lo_ref, c * CHUNK, key, 0)

            def body(mask, carry):
                w, ds = back_scores(qt, act_ref[at, K], act_ref[at, V], gt, mask)
                acc_s[at, :HD] += jnp.dot(w, g, preferred_element_type=F32)
                acc_s[at, HD:] += jnp.dot(ds, q, preferred_element_type=F32)
                return carry

            return with_mask(c * CHUNK >= latest_start(TILES + t, lo_ref), mask, body, carry)

        return lax.fori_loop(lo_ref[2 * (TILES + t)] // CHUNK, CHUNKS, k_chunk, carry)

    count = sum((lo_ref[2 * (TILES + t)] < SPAN).astype(jnp.int32) for t in range(TILES))
    lax.fori_loop(0, count, q_tile, 0)
    for mask, (ref, at) in enumerate(outgoing(pieces)):
        t = at_ref[1] ^ mask
        rows = rows_at(t)
        d = own_ref[rows, :] + jnp.where(t // 2 >= first, acc_s[rows, :], 0.0)
        d = (d * (SCALE / SPAN)).astype(BF16).astype(F32)
        d = (d * slope_ref[rows, VK].astype(F32)).astype(BF16)
        ref[at : at + TILE, :HD] = attn_ref[rows, :]
        ref[at : at + TILE, HD : 2 * HD] = dq_ref[rows, :]
        ref[at : at + TILE, 2 * HD :] = d
        cols_ref[:, rows] = d.T


def share_kernel(groups, at_ref, u_cols_ref, q_cols_ref, cols_ref, normed_ref, *refs):
    shares, all_s = refs[:-1], refs[-1]
    share = jnp.dot(cols_ref[...], normed_ref[...], preferred_element_type=F32).astype(BF16)
    all_s[HD : 2 * HD, :], all_s[3 * HD :, :] = share[:HD], share[HD:]
    all_s[:HD, :] = jnp.dot(u_cols_ref[...], normed_ref[...], preferred_element_type=F32).astype(BF16)
    all_s[2 * HD : 3 * HD, :] = jnp.dot(q_cols_ref[...], normed_ref[...], preferred_element_type=F32).astype(BF16)
    size = 4 * HD // groups
    for mask in range(groups):
        at = pl.multiple_of((at_ref[0] ^ mask) * size, size)
        part = all_s[pl.ds(at, size), :]
        if groups == 4:
            ref, half = shares[mask % 2], mask // 2 * size
            ref[half : half + size, :] = part.astype(ref.dtype)
        else:
            shares[mask][...] = part


def assemble(at_ref, refs, part, out_s):
    for mask, (ref, at) in enumerate(places(refs)):
        out_s[:, lanes_at(at_ref[1] ^ mask)] = ref[at : at + TILE, part * HD : (part + 1) * HD]


def branch_rows(at_ref, refs, w_ref, distances, row_s):
    width, total = w_ref.shape[0], 0.0
    for part, branch in ((1, 2), (2, 1), (3, 3)):
        assemble(at_ref, refs, part, row_s)
        for i in distances:
            at = ((at_ref[1] // 2) ^ i) * 2 * HD
            x = row_s[:, pl.ds(pl.multiple_of(at, 2 * HD), 2 * HD)]
            w = w_ref[:, pl.ds(pl.multiple_of(branch * width + at, 2 * HD), 2 * HD)]
            total += lax.dot_general(x, w, NT, preferred_element_type=F32)
    return total


def through(x, w_ref, branch):
    width = w_ref.shape[0]
    return lax.dot_general(x, w_ref[:, branch * width : (branch + 1) * width], NT, preferred_element_type=F32)


def branches_kernel(at_ref, *refs):
    pieces, (w_in_ref, dn_ref, row_s) = refs[:4], refs[4:]
    dn_ref[...] = branch_rows(at_ref, pieces, w_in_ref, (0, 1, 2), row_s)


def own_u_kernel(tokens_ref, w_in_ref, after_ref, u_ref, slope_ref):
    xn = norm_rows(tokens_ref[...].astype(F32)).astype(BF16)
    pre = jnp.dot(xn, w_in_ref[:, : tokens_ref.shape[1]], preferred_element_type=F32)
    u_ref[...], slope_ref[...] = silu_and_slope(pre)


def rows_kernel(at_ref, *refs):
    pieces, (dn_ref, dg_ref, u_ref, slope_ref, tokens_ref, grad_ref, w_out_ref, w_in_ref) = refs[:5], refs[5:-4]
    out_ref, dx_ref, end_ref, row_s = refs[-4:]
    end_ref[...] = jnp.zeros(end_ref.shape, F32)
    x = tokens_ref[...].astype(F32)
    assemble(at_ref, pieces, 0, row_s)
    attn_n = norm_rows(row_s[...].astype(F32))
    gated = (attn_n * u_ref[...].astype(F32)).astype(BF16)
    y = jnp.dot(gated, w_out_ref[...], preferred_element_type=F32)
    out_ref[...] = (x + y).astype(BF16)
    du = (dg_ref[...].astype(F32) * attn_n).astype(BF16).astype(F32)
    du = (du * slope_ref[...].astype(F32)).astype(BF16)
    dn = dn_ref[...] + through(du, w_in_ref, 0) + branch_rows(at_ref, pieces, w_in_ref, (3,), row_s)
    r = lax.rsqrt(jnp.mean(x * x, axis=-1, keepdims=True) + eps)
    n = x * r
    dx = r * (dn - n * jnp.mean(dn * n, axis=-1, keepdims=True))
    dx_ref[...] = (grad_ref[...].astype(F32) + dx).astype(BF16)


def half_kernel(keep_ref, got_ref, mine_ref, send_ref):
    size = mine_ref.shape[0]
    mine_ref[...] = keep_ref[:size, :] + got_ref[:size, :].astype(F32)
    send_ref[...] = (keep_ref[size:, :] + got_ref[size:, :].astype(F32)).astype(BF16)


def sum_kernel(*refs):
    total = refs[0][...].astype(F32)
    for ref in refs[1:-2]:
        total += ref[...].astype(F32)
    refs[-1][...] = total


def call(kernel, scalars, arrays, outs, scratch=(), after=(), aliases=None, limit=16, sems=0):
    smem = pl.BlockSpec(memory_space=pltpu.SMEM)
    vmem = pl.BlockSpec(memory_space=pltpu.VMEM)
    anywhere = pl.BlockSpec(memory_space=pl.ANY)
    return pl.pallas_call(
        kernel,
        out_shape=[jax.ShapeDtypeStruct(*out) for out in outs],
        in_specs=[smem] * len(scalars) + [vmem] * len(arrays) + [anywhere] * len(after),
        out_specs=[smem if out[1] == jnp.int32 else vmem for out in outs],
        scratch_shapes=[pltpu.VMEM(*shape) for shape in scratch] + ([pltpu.SemaphoreType.DMA((sems,))] if sems else []),
        input_output_aliases=aliases or {},
        compiler_params=pltpu.CompilerParams(vmem_limit_bytes=limit * 2**20),
        cost_estimate=pl.CostEstimate(flops=0, bytes_accessed=0, transcendentals=0),
    )(*scalars, *arrays, *after)


def per_device(groups, tokens, w_in, w_out, block_counts, tails, grad_out):
    count, width = tokens.shape
    own, tall, wide, tall_t = (count, width), (SPAN, HD), (SPAN, 2 * HD), (HD, SPAN)
    piece, half, sums_shape = (count, HD), (BLK, width), (2 * TILES, TILE)

    def swap(x, mask):
        return lax.ppermute(x, "h", [(i, i ^ mask) for i in range(HEADS)])

    def onward(x):
        return lax.ppermute(x, "g", [(i, i + 1) for i in range(groups - 1)])

    def backward(x):
        return lax.ppermute(x, "g", [(i + 1, i) for i in range(groups - 1)])

    def trade(pieces, after=()):
        mine, other, *pairs = pieces
        other = swap(other, 1)
        pairs = call(
            merge_kernel,
            (),
            (other,),
            [(x.shape, BF16) for x in pairs],
            after=(*pairs, *after),
            aliases={1: 0, 2: 1, 3: 2},
            limit=4,
        )
        return [mine, other] + [swap(x, mask) for x, mask in zip(pairs, (2, 4, 6))]

    x_rows, y_rows = swap(tokens, 2), swap(tokens, 4)
    other = swap(tokens, 1)
    *info, w_head = call(
        start_kernel,
        (block_counts, tails),
        (),
        [((2 * MAXB,), jnp.int32)] * 2 + [((2,), jnp.int32), ((width, 4 * HD), BF16)],
        after=(w_in,),
        limit=51,
        sems=4,
    )
    *kept, kv = project(info, (0, 1), ((tokens,), (other,)), w_head, ())
    *dg_pieces, dg_own = call(
        d_gated_kernel, info[2:], (grad_out, w_out), trade_outs(HD) + [(own, BF16)], after=(kv,)
    )
    x_rows, y_rows, x_half, y_half = call(
        cut_kernel,
        (),
        (x_rows, y_rows),
        [(own, BF16), (own, BF16), (half, BF16), (half, BF16)],
        after=(kv, dg_own),
        aliases={0: 0, 1: 1},
        limit=4,
    )
    corner = swap(x_half, 4), swap(y_half, 2)
    chunks = ((x_rows,), (swap(x_rows, 1),), (y_rows,), (swap(y_rows, 1),))
    *kept, kv = project(info, (2, 3, 4, 5), chunks, w_head, kept, kv=kv)
    far_kv = [onward(kv)]
    corner = call(gate_kernel, (), (), [(half, BF16), (half, BF16)], after=(*corner, kv), aliases={0: 0, 1: 1}, limit=4)
    *kept, kv, q = project(info, (6, 7), (corner, [swap(x, 1) for x in corner]), w_head, kept, True)
    far_kv.append(onward(kv))
    q_next = backward(q)
    normed, act, slope = kept
    d_gated = trade(dg_pieces, (kv,))

    near, kt, qt, slope_qt = call(fwd_own_kernel, info[:2], (act, slope), [(tall, F32)] + [(tall_t, BF16)] * 3)
    attn, kv, far_kt, sums = call(
        fwd_far_kernel,
        info,
        (act, *far_kv, near, *d_gated),
        [(tall, BF16), (wide, BF16), (tall_t, BF16), (sums_shape, F32)],
        [(tall, F32), (tall, BF16)],
    )
    sums = call(add_kernel, (), (sums, swap(sums, 1)), [(sums_shape, F32)], limit=4)[0]
    sums = [sums] + [swap(sums, mask) for mask in (2, 4, 6)]

    g, u_cols = call(
        cotangent_kernel,
        info[1:],
        (act, slope, attn, *sums, *d_gated),
        [(tall, BF16), (tall_t, BF16)],
        [(tall, BF16)],
        (q_next,),
    )
    g_next = backward(g)
    q_cols, d_q, dkv = call(
        queries_kernel,
        info[:1],
        (act, slope_qt, qt, kt, g, kv, far_kt),
        [(tall_t, BF16), (tall, BF16), (wide, F32)],
        [(tall_t, BF16)],
    )
    rows = 4 * HD // groups
    *pieces, cols = call(
        keys_kernel,
        (info[0], info[2]),
        (dkv, act, slope, q_next, g_next, d_q, attn),
        trade_outs(4 * HD) + [((2 * HD, SPAN), BF16)],
        [(wide, F32)],
    )
    outs = call(
        functools.partial(share_kernel, groups),
        info[2:],
        (u_cols, q_cols, cols, normed),
        [((2 * rows, width), F32), ((2 * rows, width), BF16)] if groups == 4 else [((rows, width), BF16)] * groups,
        [((4 * HD, width), BF16)],
    )

    def between(x, mask):
        return lax.ppermute(x, "g", [(i, i ^ mask) for i in range(groups)])

    if groups == 4:
        keep, send = outs
        half = [((rows, width), F32), ((rows, width), BF16)]
        keep, send = call(half_kernel, (), (keep, between(send, 1)), half, limit=8)
        shares = keep, between(send, 2)
    else:
        shares = [outs[0]] + [between(x, mask + 1) for mask, x in enumerate(outs[1:])]
    pieces = trade(pieces)
    u, slope_u = call(own_u_kernel, (), (tokens, w_in), [(own, BF16), (own, BF16)], after=(cols,))
    d_normed = call(
        branches_kernel,
        info[2:],
        (*pieces[:4], w_in),
        [(own, F32)],
        [(own, BF16)],
    )[0]
    layer_out, grad_tokens, end = call(
        rows_kernel,
        info[2:],
        (*pieces, d_normed, dg_own, u, slope_u, tokens, grad_out, w_out, w_in),
        [(own, BF16), (own, BF16), ((8, HD), F32)],
        [(own, BF16)],
    )
    grad_w_in = call(
        sum_kernel, (), tuple(shares), [((rows, width), F32)], after=(end,)
    )[0]
    parts = groups // 4
    if parts > 1:
        perm = [
            (i * HEADS + j, ((i // parts) * HEADS + j) * parts + i % parts)
            for i in range(groups)
            for j in range(HEADS)
        ]
        grad_w_in = lax.ppermute(grad_w_in, ("g", "h"), perm)
    return (layer_out, grad_tokens, grad_w_in)


def solution(mesh):
    groups = mesh.shape["seq"] // HEADS
    split = Mesh(mesh.devices.reshape(groups, HEADS), ("g", "h"))
    rows = P(("g", "h"), None)
    return jax.shard_map(
        functools.partial(per_device, groups),
        mesh=split,
        in_specs=(rows, P(), P(), P(), P(), rows),
        out_specs=(rows, rows, rows),
        check_vma=False,
    )
```
